32 devices in a mesh: dp: 8 (over y, x, core), mp: 4 (over z).
Axes of the slice: x: 2, y: 2, z: 4, core: 2. Of those that a mesh axis runs over, the one named last changes fastest.
Arguments:
- queries: bfloat16 [1024, 64, 128], P('dp', 'mp'), may hold values from -6 to 6
- key_cache: bfloat16 [1024, 8, 128, 128], P('dp', 'mp'), may hold values from -6 to 6
- value_cache: bfloat16 [1024, 8, 128, 128], P('dp', 'mp'), may hold values from -6 to 6
- key_new: bfloat16 [1024, 8, 128], P('dp', 'mp'), may hold values from -6 to 6
- value_new: bfloat16 [1024, 8, 128], P('dp', 'mp'), may hold values from -6 to 6
- lengths: int32 [1024], P('dp'), may hold values from 1 to 128, as said below
- occupied: int32 [1024], P('dp'), may hold values 0 or 1
- slot_request: int32 [1024], P('dp'), may hold values from 0 to 1023, as said below
- request_adapter: int32 [1024], replicated, may hold values from 0 to 15, as said below
- out_weight: bfloat16 [8192, 4096], P('mp'), may hold values from -0.375 to 0.375
- shrink_weight: bfloat16 [16, 8192, 64], P('dp', 'mp'), may hold values from -0.375 to 0.375
- expand_weight: bfloat16 [16, 64, 4096], P('dp', None, 'mp'), may hold values from -0.75 to 0.75
Outputs:
- mixed: bfloat16 [1024, 4096], P('dp', 'mp')
The draws below stay inside these ranges and needn't reach their ends.
Inputs may be any that keep to these rules, and one draw needn't show every extreme that they name: `slot_request`: A permutation: each request stands in exactly one slot. `request_adapter`: adapter n is owned by dp index n // 2. Among the slots of one dp index, at most 32 hold requests whose adapters one dp index owns; in every draw some dp index owns the adapters of exactly 32 slots of every dp index. `lengths`: each dp index has a slot of length 128.
All inputs are finite; a program needn't handle non-finite values. No bound on the sum of `occupied` on one device may be relied on, other than what follows from the above.
Results may differ from the reference program's by a relative error of at most 0.011.
Values may be sent and summed in bfloat16 or wider, within the bound.
No kernel may reach another device: no remote copies, remote signals or barrier semaphores. Data moves between devices by JAX's collectives and lax.ppermute only.
A program may use at most 128 MiB of HBM per device.

```python
import math
import jax
import jax.numpy as jnp
from jax import lax

D = 8192
HQ = 64
KVH = 8
HD = 128
DOUT = 4096
R = 64
RQ_DEV = 128
CACHE = 128
ADP_DEV = 2
SLOTS = 1024
NADP = 16
CAP = 32


def routing(key):
    owners_count = SLOTS // RQ_DEV
    tickets = owners_count * CAP
    hot_owner = jax.random.randint(jax.random.fold_in(key, 101), (), 0, owners_count)
    ticket_owner = jnp.arange(tickets, dtype=jnp.int32) // CAP

    def block(number):
        block_key = jax.random.fold_in(jax.random.fold_in(key, 102), number)
        shuffled = jax.random.permutation(block_key, tickets).astype(jnp.int32)
        scores = jnp.where(ticket_owner == hot_owner, -1, shuffled)
        ranking = jnp.argsort(scores, stable=True)
        chosen = ticket_owner[ranking[:RQ_DEV]]
        mixing = jax.random.permutation(jax.random.fold_in(block_key, 1), RQ_DEV)
        local_ids = jax.random.randint(jax.random.fold_in(block_key, 2), (RQ_DEV,), 0, ADP_DEV)
        return chosen[mixing] * ADP_DEV + local_ids
    slot_adapter = jax.vmap(block)(jnp.arange(owners_count)).reshape(SLOTS).astype(jnp.int32)
    placement = jax.random.permutation(jax.random.fold_in(key, 103), SLOTS).astype(jnp.int32)
    by_request = jnp.zeros((SLOTS,), jnp.int32).at[placement].set(slot_adapter)
    return (placement, by_request)


def draw_slot_request(key, part):
    return routing(key)[0]


def draw_request_adapter(key, part):
    return routing(key)[1]


def draw_lengths(key, part):
    owners_count = SLOTS // RQ_DEV
    drawn = jax.random.randint(jax.random.fold_in(key, 201), (owners_count, RQ_DEV), 1, CACHE + 1)
    full_at = jax.random.randint(jax.random.fold_in(key, 202), (owners_count,), 0, RQ_DEV)
    drawn = drawn.at[jnp.arange(owners_count), full_at].set(CACHE)
    return drawn.reshape(SLOTS).astype(jnp.int32)


def attention_draws(key):
    queries = jnp.clip(jax.random.normal(jax.random.fold_in(key, 301), (SLOTS, HQ, HD), jnp.float32), -6.0, 6.0)
    cached = jnp.clip(jax.random.normal(jax.random.fold_in(key, 302), (SLOTS, KVH, CACHE, HD), jnp.float32), -6.0, 6.0)
    fresh = jnp.clip(jax.random.normal(jax.random.fold_in(key, 303), (SLOTS, KVH, HD), jnp.float32), -6.0, 6.0)
    return (queries, cached, fresh)


def draw_queries(key, part):
    return attention_draws(key)[0].astype(jnp.bfloat16)


def draw_key_cache(key, part):
    return attention_draws(key)[1].astype(jnp.bfloat16)


def draw_key_new(key, part):
    return attention_draws(key)[2].astype(jnp.bfloat16)


def set_ends(entries, own_key, least, high):
    longest = entries.shape.index(max(entries.shape))
    spots = []
    for shift in (0, 1):
        where = [jax.random.randint(jax.random.fold_in(own_key, axis), (), 0, length) for axis, length in enumerate(entries.shape)]
        where[longest] = (where[longest] + shift) % entries.shape[longest]
        spots.append(tuple(where))
    return entries.at[spots[0]].set(least).at[spots[1]].set(high)


def shard_levels(own_key, extent, cuts, least, top_value):
    gain, own = 1.0, jax.random.fold_in(own_key, 6)
    for dim, parts in cuts:
        draws = jnp.exp(jax.random.uniform(jax.random.fold_in(own, dim), (parts,), jnp.float32, least / len(cuts), top_value / len(cuts)))
        gain = gain * jnp.repeat(draws, extent[dim] // parts).reshape([-1 if axis == dim else 1 for axis in range(len(extent))])
    return gain


def centred(own_key, extent, scale, limit, cuts=(), kind=jnp.bfloat16):
    level = shard_levels(own_key, extent, cuts, -0.22, 0.18) if cuts else 1.0
    values = jax.random.normal(own_key, extent, jnp.float32) * scale * level
    return jnp.minimum(jnp.maximum(values, -limit), limit).astype(kind)


def setup_inputs(seed: int = 0) -> dict:
    streams_of = jax.random.split(jax.random.key(seed), 13)
    queries = draw_queries(jax.random.fold_in(streams_of[12], 71), 0)
    key_cache = draw_key_cache(jax.random.fold_in(streams_of[12], 71), 0)
    value_cache = centred(streams_of[2], (SLOTS, KVH, CACHE, HD), 1.0, 6.0, ((0, 8), (1, 4)))
    key_new = draw_key_new(jax.random.fold_in(streams_of[12], 71), 0)
    value_new = centred(streams_of[4], (SLOTS, KVH, HD), 1.0, 6.0, ((0, 8), (1, 4)))
    lengths = draw_lengths(jax.random.fold_in(streams_of[12], 71), 0)
    occupied = set_ends((jax.random.randint(streams_of[6], (SLOTS,), 0, 4) < 3).astype(jnp.int32), jax.random.fold_in(streams_of[6], 1), 0, 1)
    slot_request = draw_slot_request(jax.random.fold_in(streams_of[12], 71), 0)
    request_adapter = draw_request_adapter(jax.random.fold_in(streams_of[12], 71), 0)
    out_weight = centred(streams_of[9], (D, DOUT), (D // 32) ** -0.5, 0.375, ((0, 4),))
    shrink_weight = centred(streams_of[10], (NADP, D, R), (D // 32) ** -0.5, 0.375, ((0, 8), (1, 4)))
    expand_weight = centred(streams_of[11], (NADP, R, DOUT), R ** -0.5, 0.75, ((0, 8), (2, 4)))
    return dict(queries=queries, key_cache=key_cache, value_cache=value_cache, key_new=key_new, value_new=value_new, lengths=lengths, occupied=occupied, slot_request=slot_request, request_adapter=request_adapter, out_weight=out_weight, shrink_weight=shrink_weight, expand_weight=expand_weight)


def attend(queries, key_cache, value_cache, key_new, value_new, lengths):
    rows, heads, width = queries.shape
    kv_heads = key_cache.shape[1]
    group = heads // kv_heads
    inverse = 1.0 / math.sqrt(width)
    grouped = queries.astype(jnp.float32).reshape(rows, kv_heads, group, width)
    cached = jnp.einsum('bgjd,bgtd->bgjt', grouped, key_cache.astype(jnp.float32)) * inverse
    fresh = jnp.einsum('bgjd,bgd->bgj', grouped, key_new.astype(jnp.float32)) * inverse
    valid = jnp.arange(key_cache.shape[2])[None, :] < lengths[:, None]
    cached = jnp.where(valid[:, None, None, :], cached, -jnp.inf)
    top = jnp.maximum(lax.optimization_barrier(jnp.max(cached, axis=-1)), fresh)
    cached_exp = jnp.exp(cached - top[..., None])
    fresh_exp = jnp.exp(fresh - top)
    total = lax.optimization_barrier(jnp.sum(cached_exp, axis=-1)) + fresh_exp
    cached_w = (cached_exp / total[..., None]).astype(jnp.bfloat16)
    fresh_w = (fresh_exp / total).astype(jnp.bfloat16)
    summed = jnp.einsum('bgjt,bgtd->bgjd', cached_w.astype(jnp.float32), value_cache.astype(jnp.float32))
    summed = summed + fresh_w.astype(jnp.float32)[..., None] * value_new.astype(jnp.float32)[:, :, None, :]
    return summed.reshape(rows, heads * width).astype(jnp.bfloat16)

def reference(queries, key_cache, value_cache, key_new, value_new, lengths, occupied, slot_request, request_adapter, out_weight, shrink_weight, expand_weight):
    blocks = SLOTS // RQ_DEV

    def blocked(array):
        return array.reshape((blocks, RQ_DEV) + array.shape[1:])
    slot_adapter = request_adapter[slot_request]

    def one_block(pieces):
        q_rows, k_rows, v_rows, kn_rows, vn_rows, len_rows, adapter_rows = pieces
        attended = attend(q_rows, k_rows, v_rows, kn_rows, vn_rows, len_rows)
        base = jnp.dot(attended, out_weight, preferred_element_type=jnp.float32)
        shrink = shrink_weight[adapter_rows].astype(jnp.float32)
        low = jnp.einsum('bd,bdr->br', attended.astype(jnp.float32), shrink).astype(jnp.bfloat16)
        expand = expand_weight[adapter_rows].astype(jnp.float32)
        delta = (0.5 * jnp.einsum('br,bre->be', low.astype(jnp.float32), expand)).astype(jnp.bfloat16)
        return base + delta.astype(jnp.float32)
    mixed = lax.map(one_block, (blocked(queries), blocked(key_cache), blocked(value_cache), blocked(key_new), blocked(value_new), blocked(lengths), blocked(slot_adapter)))
    mixed = mixed.reshape(SLOTS, DOUT)
    return (occupied.astype(jnp.float32)[:, None] * mixed).astype(jnp.bfloat16)
```

```python
import functools
import math

import jax
import jax.numpy as jnp
from jax import lax
from jax.experimental import pallas as pl
from jax.experimental.pallas import tpu as pltpu
from jax.sharding import PartitionSpec as P

VMEM_LIMIT = 40 * 1024 * 1024


def attend_kernel(
    lengths_ref, q_ref, k_ref, v_ref, kn_ref, vn_ref, out_ref, score_ref, acc_ref
):
    slots, heads, width = q_ref.shape
    kv_local, cache = k_ref.shape[1], k_ref.shape[2]
    group = heads // kv_local
    inverse = 1.0 / math.sqrt(width)
    step = pl.program_id(0)
    lane = lax.broadcasted_iota(jnp.int32, (group, cache), 1)
    for s in range(slots):
        scores = lax.dot_general(
            q_ref[s],
            k_ref[s].reshape(kv_local * cache, width),
            (((1,), (1,)), ((), ())),
            preferred_element_type=jnp.float32,
        )
        valid = lane < lengths_ref[step * slots + s]
        for g in range(kv_local):
            part = scores[g * group : (g + 1) * group, g * cache : (g + 1) * cache]
            score_ref[pl.ds(s * heads + g * group, group), :] = jnp.where(
                valid, part * inverse, -jnp.inf
            )
    q_all = q_ref[...].astype(jnp.float32).reshape(slots * kv_local, group, width)
    kn = kn_ref[...].astype(jnp.float32).reshape(slots * kv_local, 1, width)
    vn = vn_ref[...].astype(jnp.float32).reshape(slots * kv_local, 1, width)
    fresh = (jnp.sum(q_all * kn, axis=-1, keepdims=True) * inverse).reshape(slots * heads, 1)
    cached = score_ref[...]
    top = jnp.maximum(jnp.max(cached, axis=-1, keepdims=True), fresh)
    cached_exp = jnp.exp(cached - top)
    fresh_exp = jnp.exp(fresh - top)
    total = jnp.sum(cached_exp, axis=-1, keepdims=True) + fresh_exp
    scale = 1.0 / total
    weights = (cached_exp * scale).astype(jnp.bfloat16)
    fresh_w = (fresh_exp * scale).astype(jnp.bfloat16).astype(jnp.float32)
    new_part = (fresh_w.reshape(slots * kv_local, group, 1) * vn).reshape(slots * heads, width)
    row_group = lax.broadcasted_iota(jnp.int32, (heads, cache), 0) // group
    for s in range(slots):
        mine = weights[s * heads : (s + 1) * heads]
        spread = jnp.concatenate(
            [jnp.where(row_group == g, mine, jnp.zeros_like(mine)) for g in range(kv_local)],
            axis=1,
        )
        summed = jnp.dot(
            spread,
            v_ref[s].reshape(kv_local * cache, width),
            preferred_element_type=jnp.float32,
        )
        acc_ref[pl.ds(s * heads, heads), :] = summed + new_part[s * heads : (s + 1) * heads]
    for h in range(heads):
        out_ref[:, h * width : (h + 1) * width] = acc_ref[
            pl.ds(h, slots, stride=heads), :
        ].astype(out_ref.dtype)


def attend(queries, key_cache, value_cache, key_new, value_new, lengths):
    rows, heads, width = queries.shape
    kv_local, cache = key_cache.shape[1], key_cache.shape[2]
    block = min(16, rows)
    return pl.pallas_call(
        attend_kernel,
        grid_spec=pltpu.PrefetchScalarGridSpec(
            num_scalar_prefetch=1,
            grid=(rows // block,),
            in_specs=[
                pl.BlockSpec((block, heads, width), lambda i, n: (i, 0, 0)),
                pl.BlockSpec((block, kv_local, cache, width), lambda i, n: (i, 0, 0, 0)),
                pl.BlockSpec((block, kv_local, cache, width), lambda i, n: (i, 0, 0, 0)),
                pl.BlockSpec((block, kv_local, width), lambda i, n: (i, 0, 0)),
                pl.BlockSpec((block, kv_local, width), lambda i, n: (i, 0, 0)),
            ],
            out_specs=pl.BlockSpec((block, heads * width), lambda i, n: (i, 0)),
            scratch_shapes=[
                pltpu.VMEM((block * heads, cache), jnp.float32),
                pltpu.VMEM((block * heads, width), jnp.float32),
            ],
        ),
        out_shape=jax.ShapeDtypeStruct((rows, heads * width), jnp.bfloat16),
        compiler_params=pltpu.CompilerParams(vmem_limit_bytes=VMEM_LIMIT),
        cost_estimate=pl.CostEstimate(
            flops=4 * rows * heads * width * cache,
            bytes_accessed=4 * key_cache.size,
            transcendentals=rows * heads * cache,
        ),
        name="attend",
    )(lengths, queries, key_cache, value_cache, key_new, value_new)


def project_kernel(chunk_ref, a_ref, w_ref, out_ref):
    out_ref[...] = jnp.dot(
        a_ref[...], w_ref[...], preferred_element_type=jnp.float32
    ).astype(out_ref.dtype)


def project(attended, out_weight, chunk, out_local, dtype):
    rows, depth = attended.shape
    tile = min(256, out_local)
    tiles = out_local // tile
    return pl.pallas_call(
        project_kernel,
        grid_spec=pltpu.PrefetchScalarGridSpec(
            num_scalar_prefetch=1,
            grid=(tiles,),
            in_specs=[
                pl.BlockSpec((rows, depth), lambda j, c: (0, 0)),
                pl.BlockSpec((depth, tile), lambda j, c: (0, c[0] * tiles + j)),
            ],
            out_specs=pl.BlockSpec((rows, tile), lambda j, c: (0, j)),
        ),
        out_shape=jax.ShapeDtypeStruct((rows, out_local), dtype),
        compiler_params=pltpu.CompilerParams(vmem_limit_bytes=VMEM_LIMIT),
        cost_estimate=pl.CostEstimate(
            flops=2 * rows * depth * out_local,
            bytes_accessed=2 * depth * out_local,
            transcendentals=0,
        ),
        name="project",
    )(chunk.reshape(1), attended, out_weight)


def exchange(value, step):
    count = lax.axis_size("mp")
    return lax.ppermute(value, "mp", [(i, i ^ step) for i in range(count)])


def body(
    queries,
    key_cache,
    value_cache,
    key_new,
    value_new,
    lengths,
    occupied,
    slot_request,
    request_adapter,
    out_weight,
    shrink_weight,
    expand_weight,
):
    rows = queries.shape[0]
    adapters_here, depth, rank = shrink_weight.shape
    out_local = expand_weight.shape[2]
    owners_count = lax.axis_size("dp")
    shares = lax.axis_size("mp")
    me = lax.axis_index("mp")

    pair = adapters_here * rank
    shrink_packed = jnp.moveaxis(shrink_weight, 0, 1).reshape(depth, pair)
    all_shrink = lax.all_gather(shrink_packed, "dp", axis=0)
    all_expand = lax.all_gather(expand_weight.reshape(pair, out_local), "dp", axis=0, tiled=True)

    attended = attend(queries, key_cache, value_cache, key_new, value_new, lengths)

    received = []
    for step in range(shares - 1, 0, -1):
        piece = project(attended, out_weight, me ^ step, out_local, jnp.bfloat16)
        received.append(exchange(piece, step))
    own = project(attended, out_weight, me, out_local, jnp.float32)

    matches = (
        slot_request[:, None] == jnp.arange(request_adapter.shape[0], dtype=jnp.int32)[None, :]
    )
    slot_adapter = jnp.sum(jnp.where(matches, request_adapter[None, :], 0), axis=1)
    adapter_of = jnp.arange(owners_count * pair, dtype=jnp.int32) // rank
    chosen = slot_adapter[:, None] == adapter_of[None, :]

    low = jnp.einsum("md,odr->mor", attended, all_shrink, preferred_element_type=jnp.float32)
    low = jnp.where(chosen.reshape(rows, owners_count, pair), low, 0.0).sum(axis=1)
    total = low
    for step in range(1, shares):
        total = total + exchange(low, step)
    total = total.astype(jnp.bfloat16)
    spread = jnp.where(chosen, jnp.tile(total, (1, owners_count)), jnp.zeros((), jnp.bfloat16))
    delta = (0.5 * jnp.dot(spread, all_expand, preferred_element_type=jnp.float32)).astype(
        jnp.bfloat16
    )
    base = own
    for piece in received:
        base = base + piece.astype(jnp.float32)
    mixed = occupied.astype(jnp.float32)[:, None] * (base + delta.astype(jnp.float32))
    return mixed.astype(jnp.bfloat16)


def solution(mesh):
    placed = (
        P("dp", "mp", None),
        P("dp", "mp", None, None),
        P("dp", "mp", None, None),
        P("dp", "mp", None),
        P("dp", "mp", None),
        P("dp"),
        P("dp"),
        P("dp"),
        P(),
        P("mp", None),
        P("dp", "mp", None),
        P("dp", None, "mp"),
    )
    return jax.shard_map(body, mesh=mesh, in_specs=placed, out_specs=P("dp", "mp"), check_vma=False)
```

```python
import functools
import math

import jax
import jax.numpy as jnp
from jax import lax
from jax.experimental import pallas as pl
from jax.experimental.pallas import tpu as pltpu
from jax.sharding import PartitionSpec as P

MIB = 1024 * 1024
TILE = 256


def attend_group(lengths, q, k_ref, v_ref, kn, vn, first, acc_ref):
    lanes, width = q.shape
    kv_local, cache = k_ref.shape[1], k_ref.shape[2]
    slots = len(lengths)
    heads = lanes // slots
    group = heads // kv_local
    inverse = 1.0 / math.sqrt(width)
    q_t = q.astype(jnp.float32).T
    lane = lax.broadcasted_iota(jnp.int32, (1, lanes), 1)
    slot_of = lane // heads
    limit = jnp.zeros((1, lanes), jnp.int32)
    for s in range(slots):
        limit = jnp.where(slot_of == s, lengths[s], limit)

    products = jnp.zeros((kv_local * cache, lanes), jnp.float32)
    for s in range(0, slots, 2):
        keys = jnp.concatenate(
            [k_ref[first + s + i].reshape(kv_local * cache, width) for i in range(2)], axis=1
        )
        mine = jnp.concatenate(
            [jnp.where(slot_of == s + i, q_t, 0.0).astype(jnp.bfloat16) for i in range(2)], axis=0
        )
        products += jnp.dot(keys, mine, preferred_element_type=jnp.float32)
    head_group = (lane % heads) // group
    scores = products[:cache]
    for g in range(1, kv_local):
        scores = jnp.where(head_group == g, products[g * cache : (g + 1) * cache], scores)
    position = lax.broadcasted_iota(jnp.int32, (cache, lanes), 0)
    scores = jnp.where(position < limit, scores * inverse, -jnp.inf)

    own_row = lax.broadcasted_iota(jnp.int32, (slots * kv_local, lanes), 0) == lane // group
    fresh = jnp.dot(kn, q_t.astype(jnp.bfloat16), preferred_element_type=jnp.float32)
    fresh = jnp.sum(jnp.where(own_row, fresh, 0.0), axis=0, keepdims=True) * inverse
    top = jnp.maximum(jnp.max(scores, axis=0, keepdims=True), fresh)
    cached_exp = jnp.exp(scores - top)
    fresh_exp = jnp.exp(fresh - top)
    scale = 1.0 / (jnp.sum(cached_exp, axis=0, keepdims=True) + fresh_exp)
    weights = (cached_exp * scale).T.astype(jnp.bfloat16)
    fresh_w = jnp.where(own_row, fresh_exp * scale, 0.0)
    fresh_w = fresh_w.T.astype(jnp.bfloat16)
    new_part = jnp.dot(fresh_w, vn, preferred_element_type=jnp.float32)

    row_group = lax.broadcasted_iota(jnp.int32, (heads, cache), 0) // group
    for s in range(slots):
        mine = weights[s * heads : (s + 1) * heads]
        spread = jnp.concatenate(
            [jnp.where(row_group == g, mine, jnp.zeros_like(mine)) for g in range(kv_local)],
            axis=1,
        )
        summed = jnp.dot(
            spread,
            v_ref[first + s].reshape(kv_local * cache, width),
            preferred_element_type=jnp.float32,
        )
        acc_ref[pl.ds((first + s) * heads, heads), :] = (
            summed + new_part[s * heads : (s + 1) * heads]
        )


def fetch(w_ref, buffer_ref, sem_ref, slot, column):
    return pltpu.make_async_copy(
        w_ref.at[:, pl.ds(pl.multiple_of(column, TILE), TILE)],
        buffer_ref.at[slot],
        sem_ref.at[slot],
    )


def project_tiles(a_ref, w_ref, buffer_ref, sem_ref, out_ref, first_slot, column):
    tiles = out_ref.shape[1] // TILE

    def tile(j, carry):
        slot = first_slot + j
        fetch(w_ref, buffer_ref, sem_ref, slot, column + j * TILE).wait()
        out_ref[:, pl.ds(pl.multiple_of(j * TILE, TILE), TILE)] = jnp.dot(
            a_ref[...], buffer_ref[slot], preferred_element_type=jnp.float32
        ).astype(out_ref.dtype)
        return carry

    lax.fori_loop(0, tiles, tile, 0)


def attend_kernel(
    lengths_ref,
    chunk_ref,
    q_ref,
    k_ref,
    v_ref,
    kn_ref,
    vn_ref,
    w_ref,
    out_ref,
    piece_ref,
    acc_ref,
    buffer_ref,
    sem_ref,
):
    slots, heads, width = q_ref.shape
    kv_local = k_ref.shape[1]
    step = pl.program_id(0)
    tiles = piece_ref.shape[1] // TILE
    column = chunk_ref[0] * piece_ref.shape[1]

    @pl.when(step == 0)
    def _():
        for j in range(tiles):
            fetch(w_ref, buffer_ref, sem_ref, j, column + j * TILE).start()

    count = 128 // heads
    for first in range(0, slots, count):
        attend_group(
            [lengths_ref[step * slots + first + s] for s in range(count)],
            q_ref[first : first + count].reshape(count * heads, width),
            k_ref,
            v_ref,
            kn_ref[first : first + count].reshape(count * kv_local, width),
            vn_ref[first : first + count].reshape(count * kv_local, width),
            first,
            acc_ref,
        )
    rows = pl.ds(pl.multiple_of(step * slots, slots), slots)
    for h in range(heads):
        out_ref[rows, h * width : (h + 1) * width] = acc_ref[
            pl.ds(h, slots, stride=heads), :
        ].astype(out_ref.dtype)

    @pl.when(step == pl.num_programs(0) - 1)
    def _():
        project_tiles(out_ref, w_ref, buffer_ref, sem_ref, piece_ref, 0, column)


def attend(queries, key_cache, value_cache, key_new, value_new, lengths, out_weight, chunk, out_local):
    rows, heads, width = queries.shape
    kv_local, cache = key_cache.shape[1], key_cache.shape[2]
    block = min(16, rows)
    depth = heads * width
    return pl.pallas_call(
        attend_kernel,
        grid_spec=pltpu.PrefetchScalarGridSpec(
            num_scalar_prefetch=2,
            grid=(rows // block,),
            in_specs=[
                pl.BlockSpec((block, heads, width), lambda i, n, c: (i, 0, 0)),
                pl.BlockSpec((block, kv_local, cache, width), lambda i, n, c: (i, 0, 0, 0)),
                pl.BlockSpec((block, kv_local, cache, width), lambda i, n, c: (i, 0, 0, 0)),
                pl.BlockSpec((block, kv_local, width), lambda i, n, c: (i, 0, 0)),
                pl.BlockSpec((block, kv_local, width), lambda i, n, c: (i, 0, 0)),
                pl.BlockSpec(memory_space=pl.ANY),
            ],
            out_specs=[
                pl.BlockSpec((rows, depth), lambda i, n, c: (0, 0)),
                pl.BlockSpec((rows, out_local), lambda i, n, c: (0, 0)),
            ],
            scratch_shapes=[
                pltpu.VMEM((block * heads, width), jnp.float32),
                pltpu.VMEM((out_local // TILE, depth, TILE), jnp.bfloat16),
                pltpu.SemaphoreType.DMA((out_local // TILE,)),
            ],
        ),
        out_shape=[
            jax.ShapeDtypeStruct((rows, depth), jnp.bfloat16),
            jax.ShapeDtypeStruct((rows, out_local), jnp.bfloat16),
        ],
        compiler_params=pltpu.CompilerParams(vmem_limit_bytes=60 * MIB),
        cost_estimate=pl.CostEstimate(
            flops=2 * rows * depth * out_local,
            bytes_accessed=4 * key_cache.size + 2 * depth * out_local,
            transcendentals=rows * heads * cache,
        ),
        name="attend",
    )(lengths, chunk.reshape(1), queries, key_cache, value_cache, key_new, value_new, out_weight)


def project_kernel(chunks_ref, a_ref, w_ref, *refs):
    *out_refs, buffer_ref, sem_ref = refs
    out_local = out_refs[0].shape[1]
    tiles = out_local // TILE
    for i in range(len(out_refs)):
        for j in range(tiles):
            column = chunks_ref[i] * out_local + j * TILE
            fetch(w_ref, buffer_ref, sem_ref, i * tiles + j, column).start()
    for i, out_ref in enumerate(out_refs):
        project_tiles(
            a_ref, w_ref, buffer_ref, sem_ref, out_ref, i * tiles, chunks_ref[i] * out_local
        )


def project(attended, out_weight, chunks, out_local, dtypes):
    rows, depth = attended.shape
    slots = len(dtypes) * (out_local // TILE)
    return pl.pallas_call(
        project_kernel,
        grid_spec=pltpu.PrefetchScalarGridSpec(
            num_scalar_prefetch=1,
            grid=(1,),
            in_specs=[
                pl.BlockSpec((rows, depth), lambda i, c: (0, 0)),
                pl.BlockSpec(memory_space=pl.ANY),
            ],
            out_specs=[pl.BlockSpec((rows, out_local), lambda i, c: (0, 0)) for _ in dtypes],
            scratch_shapes=[
                pltpu.VMEM((slots, depth, TILE), jnp.bfloat16),
                pltpu.SemaphoreType.DMA((slots,)),
            ],
        ),
        out_shape=[jax.ShapeDtypeStruct((rows, out_local), dtype) for dtype in dtypes],
        compiler_params=pltpu.CompilerParams(vmem_limit_bytes=40 * MIB),
        cost_estimate=pl.CostEstimate(
            flops=2 * rows * depth * out_local * len(dtypes),
            bytes_accessed=2 * depth * out_local * len(dtypes),
            transcendentals=0,
        ),
        name="project",
    )(jnp.stack(chunks), attended, out_weight)


def low_kernel(ranks, owners_ref, adapters_ref, a_ref, *refs):
    *piece_refs, out_ref = refs
    pair, depth = piece_refs[0].shape
    rows = a_ref.shape[0]
    a_t = a_ref[...].astype(jnp.float32).T.astype(jnp.bfloat16)
    row = lax.broadcasted_iota(jnp.int32, (pair, rows), 0)
    total = jnp.zeros((pair, rows), jnp.float32)
    for i, piece_ref in enumerate(piece_refs):
        part = jnp.dot(piece_ref[...], a_t, preferred_element_type=jnp.float32)
        first = owners_ref[i] * (pair // ranks)
        total += jnp.where(row // ranks + first == adapters_ref[...], part, 0.0)
    out_ref[...] = total


def low_rank(attended, pieces, owners, slot_adapter, rank):
    rows, depth = attended.shape
    pair = pieces[0].shape[0]
    vmem = pl.BlockSpec(memory_space=pltpu.VMEM)
    return pl.pallas_call(
        functools.partial(low_kernel, rank),
        in_specs=[pl.BlockSpec(memory_space=pltpu.SMEM), vmem, vmem] + [vmem] * len(pieces),
        out_specs=vmem,
        out_shape=jax.ShapeDtypeStruct((pair, rows), jnp.float32),
        compiler_params=pltpu.CompilerParams(vmem_limit_bytes=40 * MIB),
        cost_estimate=pl.CostEstimate(
            flops=2 * rows * depth * pair * len(pieces),
            bytes_accessed=2 * depth * pair * len(pieces),
            transcendentals=0,
        ),
        name="low_rank",
    )(
        jnp.stack(owners),
        slot_adapter.reshape(1, rows),
        attended,
        *pieces,
    )


def finish_kernel(ranks, count, shares, owners_ref, adapters_ref, occupied_ref, own_ref, *refs):
    out_ref = refs[-1]
    base_refs = refs[: shares - 1]
    low_refs = refs[shares - 1 : 2 * shares - 1]
    expand_refs = refs[2 * shares - 1 : -1]
    pair, rows = low_refs[0].shape
    low = low_refs[0][...]
    for ref in low_refs[1:]:
        low += ref[...]
    low = low.astype(jnp.bfloat16).astype(jnp.float32)
    row = lax.broadcasted_iota(jnp.int32, (pair, rows), 0)
    delta = jnp.zeros(out_ref.shape, jnp.float32)
    for i in range(0, count, 2):
        sides, weights = [], []
        for j in range(i, min(i + 2, count)):
            first = owners_ref[j] * (pair // ranks)
            mine = jnp.where(row // ranks + first == adapters_ref[...], low, 0.0)
            sides.append(mine.T.astype(jnp.bfloat16))
            weights.append(expand_refs[j][...])
        delta += jnp.dot(
            jnp.concatenate(sides, axis=1),
            jnp.concatenate(weights, axis=0),
            preferred_element_type=jnp.float32,
        )
    delta = (0.5 * delta).astype(jnp.bfloat16).astype(jnp.float32)
    live = jnp.broadcast_to(occupied_ref[...].astype(jnp.float32), (128, rows)).T
    for j in range(0, out_ref.shape[1], 128):
        columns = slice(j, j + 128)
        base = own_ref[:, columns]
        for ref in base_refs:
            base += ref[:, columns].astype(jnp.float32)
        out_ref[:, columns] = (live * (base + delta[:, columns])).astype(out_ref.dtype)


def finish(own, received, lows, pieces, owners, slot_adapter, occupied, rank):
    rows, out_local = own.shape
    vmem = pl.BlockSpec(memory_space=pltpu.VMEM)
    arrays = [own, *received, *lows, *pieces]
    return pl.pallas_call(
        functools.partial(finish_kernel, rank, len(pieces), len(lows)),
        in_specs=[pl.BlockSpec(memory_space=pltpu.SMEM), vmem, vmem] + [vmem] * len(arrays),
        out_specs=vmem,
        out_shape=jax.ShapeDtypeStruct((rows, out_local), jnp.bfloat16),
        compiler_params=pltpu.CompilerParams(vmem_limit_bytes=40 * MIB),
        cost_estimate=pl.CostEstimate(
            flops=2 * rows * out_local * pieces[0].shape[0] * len(pieces),
            bytes_accessed=sum(a.size * a.dtype.itemsize for a in arrays),
            transcendentals=0,
        ),
        name="finish",
    )(
        jnp.stack(owners),
        slot_adapter.reshape(1, rows),
        occupied.reshape(1, rows),
        *arrays,
    )


def exchange(value, axis, step):
    count = lax.axis_size(axis)
    return lax.ppermute(value, axis, [(i, i ^ step) for i in range(count)])


def gather_blocks(own):
    count = lax.axis_size("dp")
    bits = [1 << i for i in range(1, count.bit_length() - 1)]
    blocks = {0: own}
    if len(bits) >= 2:
        a, b = bits[:2]
        half = own.shape[0] // 2
        blocks[a] = exchange(own, "dp", a)
        blocks[b] = exchange(own, "dp", b)
        blocks[a | b] = jnp.concatenate(
            [exchange(blocks[a][:half], "dp", b), exchange(blocks[b][half:], "dp", a)]
        )
        bits = bits[2:]
    for bit in bits + [1]:
        for key in list(blocks):
            blocks[key | bit] = exchange(blocks[key], "dp", bit)
    return blocks


def body(
    queries,
    key_cache,
    value_cache,
    key_new,
    value_new,
    lengths,
    occupied,
    slot_request,
    request_adapter,
    out_weight,
    shrink_weight,
    expand_weight,
):
    adapters_here, depth, rank = shrink_weight.shape
    out_local = expand_weight.shape[2]
    shares = lax.axis_size("mp")
    me = lax.axis_index("mp")
    here = lax.axis_index("dp")

    pair = adapters_here * rank
    shrink = gather_blocks(jnp.swapaxes(shrink_weight, 1, 2).reshape(pair, depth))
    expand = gather_blocks(expand_weight.reshape(pair, out_local))
    owners = [here ^ key for key in shrink]

    matches = (
        slot_request[:, None] == jnp.arange(request_adapter.shape[0], dtype=jnp.int32)[None, :]
    )
    slot_adapter = jnp.sum(jnp.where(matches, request_adapter[None, :], 0), axis=1)

    steps = list(range(shares - 1, 0, -1))
    attended, piece = attend(
        queries,
        key_cache,
        value_cache,
        key_new,
        value_new,
        lengths,
        out_weight,
        me ^ steps[0],
        out_local,
    )
    received = [exchange(piece, "mp", steps[0])]
    *pieces, own = project(
        attended,
        out_weight,
        [me ^ step for step in steps[1:]] + [me],
        out_local,
        [jnp.bfloat16] * (shares - 2) + [jnp.float32],
    )
    received += [exchange(piece, "mp", step) for piece, step in zip(pieces, steps[1:])]

    low = low_rank(attended, list(shrink.values()), owners, slot_adapter, rank)
    lows = [low] + [exchange(low, "mp", step) for step in range(1, shares)]
    return finish(
        own, received, lows, list(expand.values()), owners, slot_adapter, occupied, rank
    )


def solution(mesh):
    placed = (
        P("dp", "mp", None),
        P("dp", "mp", None, None),
        P("dp", "mp", None, None),
        P("dp", "mp", None),
        P("dp", "mp", None),
        P("dp"),
        P("dp"),
        P("dp"),
        P(),
        P("mp", None),
        P("dp", "mp", None),
        P("dp", None, "mp"),
    )
    return jax.shard_map(body, mesh=mesh, in_specs=placed, out_specs=P("dp", "mp"), check_vma=False)
```

```python
import functools
import math

import jax
import jax.numpy as jnp
from jax import lax
from jax.experimental import pallas as pl
from jax.experimental.pallas import tpu as pltpu
from jax.sharding import PartitionSpec as P

MIB = 1024 * 1024
TILE = 256
SMALL = pl.CostEstimate(flops=1, bytes_accessed=1, transcendentals=0)


def attend_block(lengths, q_ref, k_ref, v_ref, kn_ref, vn_ref, first, acc_ref):
    slots = len(lengths)
    heads, width = q_ref.shape[1:]
    kv_local, cache = k_ref.shape[1], k_ref.shape[2]
    group = heads // kv_local
    inverse = 1.0 / math.sqrt(width)
    lane = lax.broadcasted_iota(jnp.int32, (group, cache), 1)
    parts = []
    for s in range(slots):
        scores = lax.dot_general(
            q_ref[first + s],
            k_ref[first + s].reshape(kv_local * cache, width),
            (((1,), (1,)), ((), ())),
            preferred_element_type=jnp.float32,
        )
        valid = lane < lengths[s]
        for g in range(kv_local):
            part = scores[g * group : (g + 1) * group, g * cache : (g + 1) * cache]
            parts.append(jnp.where(valid, part * inverse, -jnp.inf))
    cached = jnp.concatenate(parts, axis=0)
    block = pl.ds(first, slots)
    q_all = q_ref[block].astype(jnp.float32).reshape(slots * kv_local, group, width)
    kn = kn_ref[block].astype(jnp.float32).reshape(slots * kv_local, 1, width)
    vn = vn_ref[block].astype(jnp.float32).reshape(slots * kv_local, 1, width)
    fresh = (jnp.sum(q_all * kn, axis=-1, keepdims=True) * inverse).reshape(slots * heads, 1)
    top = jnp.maximum(jnp.max(cached, axis=-1, keepdims=True), fresh)
    cached_exp = jnp.exp(cached - top)
    fresh_exp = jnp.exp(fresh - top)
    scale = 1.0 / (jnp.sum(cached_exp, axis=-1, keepdims=True) + fresh_exp)
    weights = (cached_exp * scale).astype(jnp.bfloat16)
    fresh_w = (fresh_exp * scale).astype(jnp.bfloat16).astype(jnp.float32)
    new_part = (fresh_w.reshape(slots * kv_local, group, 1) * vn).reshape(slots * heads, width)
    for s in range(slots):
        values = jnp.concatenate([v_ref[first + s, g] for g in range(kv_local)], axis=1)
        summed = jnp.dot(
            weights[s * heads : (s + 1) * heads], values, preferred_element_type=jnp.float32
        )
        for g in range(kv_local):
            row = s * heads + g * group
            acc_ref[row : row + group, :] = (
                summed[g * group : (g + 1) * group, g * width : (g + 1) * width]
                + new_part[row : row + group]
            )


def fetch(w_ref, buffer_ref, sem_ref, slot, column):
    return pltpu.make_async_copy(
        w_ref.at[:, pl.ds(pl.multiple_of(column, TILE), TILE)],
        buffer_ref.at[slot],
        sem_ref.at[slot],
    )


def project_tiles(a_ref, w_ref, buffer_ref, sem_ref, out_ref, first_slot, column):
    tiles = out_ref.shape[1] // TILE

    def tile(j, carry):
        slot = first_slot + j
        fetch(w_ref, buffer_ref, sem_ref, slot, column + j * TILE).wait()
        out_ref[:, pl.ds(pl.multiple_of(j * TILE, TILE), TILE)] = jnp.dot(
            a_ref[...], buffer_ref[slot], preferred_element_type=jnp.float32
        ).astype(out_ref.dtype)
        return carry

    lax.fori_loop(0, tiles, tile, 0)


def attend_kernel(
    block,
    lengths_ref,
    chunk_ref,
    q_hbm,
    k_hbm,
    v_hbm,
    kn_hbm,
    vn_hbm,
    w_ref,
    out_ref,
    piece_ref,
    q_ref,
    k_ref,
    v_ref,
    kn_ref,
    vn_ref,
    acc_ref,
    buffer_ref,
    new_sem,
    block_sem,
    sem_ref,
):
    rows, heads, width = q_ref.shape
    blocks = rows // block
    tiles = piece_ref.shape[1] // TILE
    column = chunk_ref[0] * piece_ref.shape[1]

    def block_copies(i):
        part = pl.ds(pl.multiple_of(i * block, block), block)
        return [
            pltpu.make_async_copy(source.at[part], target.at[part], block_sem.at[j, i])
            for j, (source, target) in enumerate(
                ((q_hbm, q_ref), (k_hbm, k_ref), (v_hbm, v_ref))
            )
        ]

    new_copies = [
        pltpu.make_async_copy(kn_hbm, kn_ref, new_sem.at[0]),
        pltpu.make_async_copy(vn_hbm, vn_ref, new_sem.at[1]),
    ]
    for copy in new_copies:
        copy.start()

    def begin(i, carry):
        for copy in block_copies(i):
            copy.start()
        return carry

    lax.fori_loop(0, blocks, begin, 0)
    for j in range(tiles):
        fetch(w_ref, buffer_ref, sem_ref, j, column + j * TILE).start()
    for copy in new_copies:
        copy.wait()

    def one_block(i, carry):
        for copy in block_copies(i):
            copy.wait()
        first = pl.multiple_of(i * block, block)
        attend_block(
            [lengths_ref[first + s] for s in range(block)],
            q_ref,
            k_ref,
            v_ref,
            kn_ref,
            vn_ref,
            first,
            acc_ref,
        )
        for h in range(heads):
            out_ref[pl.ds(first, block), h * width : (h + 1) * width] = acc_ref[
                pl.ds(h, block, stride=heads), :
            ].astype(out_ref.dtype)
        return carry

    lax.fori_loop(0, blocks, one_block, 0)
    project_tiles(out_ref, w_ref, buffer_ref, sem_ref, piece_ref, 0, column)


def attend(queries, key_cache, value_cache, key_new, value_new, lengths, out_weight, chunk, out_local):
    rows, heads, width = queries.shape
    cache = key_cache.shape[2]
    block = min(16, rows)
    depth = heads * width
    tiles = out_local // TILE
    smem = pl.BlockSpec(memory_space=pltpu.SMEM)
    hbm = pl.BlockSpec(memory_space=pltpu.HBM)
    vmem = pl.BlockSpec(memory_space=pltpu.VMEM)
    arrays = (queries, key_cache, value_cache, key_new, value_new)
    return pl.pallas_call(
        functools.partial(attend_kernel, block),
        in_specs=[smem, smem] + [hbm] * 6,
        out_specs=[vmem, vmem],
        scratch_shapes=[pltpu.VMEM(a.shape, a.dtype) for a in arrays]
        + [
            pltpu.VMEM((block * heads, width), jnp.float32),
            pltpu.VMEM((tiles, depth, TILE), jnp.bfloat16),
            pltpu.SemaphoreType.DMA((2,)),
            pltpu.SemaphoreType.DMA((3, rows // block)),
            pltpu.SemaphoreType.DMA((tiles,)),
        ],
        out_shape=[
            jax.ShapeDtypeStruct((rows, depth), jnp.bfloat16),
            jax.ShapeDtypeStruct((rows, out_local), jnp.bfloat16),
        ],
        compiler_params=pltpu.CompilerParams(vmem_limit_bytes=60 * MIB),
        cost_estimate=SMALL,
        name="attend",
    )(lengths, chunk.reshape(1), *arrays, out_weight)


def project_kernel(chunks_ref, a_hbm, w_ref, *refs):
    *out_refs, a_ref, buffer_ref, a_sem, sem_ref = refs
    out_local = out_refs[0].shape[1]
    tiles = out_local // TILE
    copy = pltpu.make_async_copy(a_hbm, a_ref, a_sem.at[0])
    copy.start()
    for i in range(len(out_refs)):
        for j in range(tiles):
            column = chunks_ref[i] * out_local + j * TILE
            fetch(w_ref, buffer_ref, sem_ref, i * tiles + j, column).start()
    copy.wait()
    for i, out_ref in enumerate(out_refs):
        project_tiles(
            a_ref, w_ref, buffer_ref, sem_ref, out_ref, i * tiles, chunks_ref[i] * out_local
        )


def project(attended, out_weight, chunks, out_local, dtypes):
    rows, depth = attended.shape
    slots = len(dtypes) * (out_local // TILE)
    vmem = pl.BlockSpec(memory_space=pltpu.VMEM)
    hbm = pl.BlockSpec(memory_space=pl.ANY)
    return pl.pallas_call(
        project_kernel,
        in_specs=[pl.BlockSpec(memory_space=pltpu.SMEM), hbm, hbm],
        out_specs=[vmem for _ in dtypes],
        scratch_shapes=[
            pltpu.VMEM(attended.shape, attended.dtype),
            pltpu.VMEM((slots, depth, TILE), jnp.bfloat16),
            pltpu.SemaphoreType.DMA((1,)),
            pltpu.SemaphoreType.DMA((slots,)),
        ],
        out_shape=[jax.ShapeDtypeStruct((rows, out_local), dtype) for dtype in dtypes],
        compiler_params=pltpu.CompilerParams(vmem_limit_bytes=52 * MIB),
        cost_estimate=SMALL,
        name="project",
    )(jnp.stack(chunks), attended, out_weight)


def fetch_all(sources, targets, sems):
    copies = [
        pltpu.make_async_copy(source, target, sems.at[i])
        for i, (source, target) in enumerate(zip(sources, targets))
    ]
    for copy in copies:
        copy.start()
    return copies


def masked(low, owner, adapters, ranks, adapters_here):
    terms = jnp.concatenate([low] * adapters_here, axis=0)
    row = lax.broadcasted_iota(jnp.int32, terms.shape, 0)
    return jnp.where(row // ranks + owner * adapters_here == adapters, terms, 0.0)


def low_kernel(ranks, sides, owners_ref, adapters_ref, *refs):
    count = (len(refs) - 2 - 2 * sides) // 2
    a_hbm, piece_hbm = refs[:sides], refs[sides : sides + count]
    out_ref = refs[sides + count]
    a_refs = refs[sides + count + 1 : 2 * sides + count + 1]
    piece_refs = refs[2 * sides + count + 1 : -1]
    copies = fetch_all(a_hbm + piece_hbm, a_refs + piece_refs, refs[-1])
    pair = piece_refs[0].shape[0]
    sides_t = []
    for a_ref, copy in zip(a_refs, copies):
        copy.wait()
        sides_t.append(a_ref[...].astype(jnp.float32).T.astype(jnp.bfloat16))
    a_t = jnp.concatenate(sides_t, axis=1)
    row = lax.broadcasted_iota(jnp.int32, (pair, a_t.shape[1]), 0)
    total = jnp.zeros(row.shape, jnp.float32)
    for i, piece_ref in enumerate(piece_refs):
        copies[sides + i].wait()
        part = jnp.dot(piece_ref[...], a_t, preferred_element_type=jnp.float32)
        first = owners_ref[i] * (pair // ranks)
        total += jnp.where(row // ranks + first == adapters_ref[...], part, 0.0)
    low = total[:ranks]
    for a in range(1, pair // ranks):
        low += total[a * ranks : (a + 1) * ranks]
    out_ref[...] = low.astype(out_ref.dtype)


def low_rank(attended, pieces, owners, adapters, rank):
    slots = adapters.shape[0]
    arrays = [*attended, *pieces]
    vmem = pl.BlockSpec(memory_space=pltpu.VMEM)
    return pl.pallas_call(
        functools.partial(low_kernel, rank, len(attended)),
        in_specs=[pl.BlockSpec(memory_space=pltpu.SMEM), vmem]
        + [pl.BlockSpec(memory_space=pl.ANY)] * len(arrays),
        out_specs=vmem,
        out_shape=jax.ShapeDtypeStruct((rank, slots), jnp.bfloat16),
        scratch_shapes=[pltpu.VMEM(a.shape, a.dtype) for a in arrays]
        + [pltpu.SemaphoreType.DMA((len(arrays),))],
        compiler_params=pltpu.CompilerParams(vmem_limit_bytes=32 * MIB),
        cost_estimate=SMALL,
        name="low_rank",
    )(jnp.stack(owners), adapters.reshape(1, slots), *arrays)


def delta_kernel(ranks, owners_ref, adapters_ref, low_ref, *refs):
    count = (len(refs) - 3) // 2
    out_refs, piece_refs = refs[count : count + 2], refs[count + 2 : -1]
    copies = fetch_all(refs[:count], piece_refs, refs[-1])
    pair = piece_refs[0].shape[0]
    low = low_ref[...].astype(jnp.float32)
    sides, weights = [], []
    for i, piece_ref in enumerate(piece_refs):
        mine = masked(low, owners_ref[i], adapters_ref[...], ranks, pair // ranks)
        sides.append(mine.T.astype(jnp.bfloat16))
    for copy, piece_ref in zip(copies, piece_refs):
        copy.wait()
        weights.append(piece_ref[...])
    delta = jnp.dot(
        jnp.concatenate(sides, axis=1),
        jnp.concatenate(weights, axis=0),
        preferred_element_type=jnp.float32,
    )
    delta = (0.5 * delta).astype(jnp.bfloat16)
    rows = out_refs[0].shape[0]
    out_refs[0][...] = delta[:rows]
    out_refs[1][...] = delta[rows:]


def correct(low, pieces, owners, adapters, rank):
    slots = adapters.shape[0]
    out_local = pieces[0].shape[1]
    vmem = pl.BlockSpec(memory_space=pltpu.VMEM)
    out = jax.ShapeDtypeStruct((slots // 2, out_local), jnp.bfloat16)
    return pl.pallas_call(
        functools.partial(delta_kernel, rank),
        in_specs=[pl.BlockSpec(memory_space=pltpu.SMEM), vmem, vmem]
        + [pl.BlockSpec(memory_space=pl.ANY)] * len(pieces),
        out_specs=[vmem, vmem],
        out_shape=[out, out],
        scratch_shapes=[pltpu.VMEM(a.shape, a.dtype) for a in pieces]
        + [pltpu.SemaphoreType.DMA((len(pieces),))],
        compiler_params=pltpu.CompilerParams(vmem_limit_bytes=32 * MIB),
        cost_estimate=SMALL,
        name="correct",
    )(jnp.stack(owners), adapters.reshape(1, slots), low, *pieces)


def finish_kernel(occupied_ref, own_ref, *refs):
    *part_refs, out_ref = refs
    rows = out_ref.shape[0]
    live = jnp.broadcast_to(occupied_ref[...].astype(jnp.float32), (128, rows)).T
    for j in range(0, out_ref.shape[1], 128):
        columns = slice(j, j + 128)
        total = own_ref[:, columns]
        for ref in part_refs:
            total += ref[:, columns].astype(jnp.float32)
        out_ref[:, columns] = (live * total).astype(out_ref.dtype)


def finish(own, parts, occupied):
    rows, out_local = own.shape
    vmem = pl.BlockSpec(memory_space=pltpu.VMEM)
    return pl.pallas_call(
        finish_kernel,
        in_specs=[vmem] * (2 + len(parts)),
        out_specs=vmem,
        out_shape=jax.ShapeDtypeStruct((rows, out_local), jnp.bfloat16),
        compiler_params=pltpu.CompilerParams(vmem_limit_bytes=32 * MIB),
        cost_estimate=SMALL,
        name="finish",
    )(occupied.reshape(1, rows), own, *parts)


def exchange(value, axis, step):
    count = lax.axis_size(axis)
    return lax.ppermute(value, axis, [(i, i ^ step) for i in range(count)])


def neighbours():
    return [1 << i for i in range(1, lax.axis_size("dp").bit_length() - 1)]


def near_blocks(own):
    return {0: own, **{bit: exchange(own, "dp", bit) for bit in neighbours()[:2]}}


def far_blocks(blocks):
    blocks = dict(blocks)
    a, b, *others = neighbours()
    half = blocks[0].shape[0] // 2
    blocks[a | b] = jnp.concatenate(
        [exchange(blocks[a][:half], "dp", b), exchange(blocks[b][half:], "dp", a)]
    )
    for bit in others:
        for key in list(blocks):
            blocks[key | bit] = exchange(blocks[key], "dp", bit)
    return blocks


def body(
    queries,
    key_cache,
    value_cache,
    key_new,
    value_new,
    lengths,
    occupied,
    slot_request,
    request_adapter,
    out_weight,
    shrink_weight,
    expand_weight,
):
    adapters_here, depth, rank = shrink_weight.shape
    out_local = expand_weight.shape[2]
    shares = lax.axis_size("mp")
    me = lax.axis_index("mp")
    here = lax.axis_index("dp")
    pair = adapters_here * rank
    steps = list(range(shares - 1, 0, -1))

    shrink = near_blocks(jnp.swapaxes(shrink_weight, 1, 2).reshape(pair, depth))
    requests = jnp.concatenate([slot_request, exchange(slot_request, "dp", 1)])

    attended, piece = attend(
        queries,
        key_cache,
        value_cache,
        key_new,
        value_new,
        lengths,
        out_weight,
        me ^ steps[0],
        out_local,
    )
    received = [exchange(piece, "mp", steps[0])]
    beside = exchange(attended, "dp", 1)
    (piece,) = project(attended, out_weight, [me ^ steps[1]], out_local, [jnp.bfloat16])
    received.append(exchange(piece, "mp", steps[1]))
    expand = expand_weight.reshape(pair, out_local)
    shrink, expand, requests, attended, _ = lax.optimization_barrier(
        (shrink, expand, requests, attended, piece)
    )
    shrink = far_blocks(shrink)
    expand = near_blocks(expand)
    *pieces, own = project(
        attended,
        out_weight,
        [me ^ step for step in steps[2:]] + [me],
        out_local,
        [jnp.bfloat16] * (shares - 3) + [jnp.float32],
    )
    received += [exchange(piece, "mp", step) for piece, step in zip(pieces, steps[2:])]
    requests, attended, _ = lax.optimization_barrier((requests, attended, own))

    matches = requests[:, None] == jnp.arange(request_adapter.shape[0], dtype=jnp.int32)[None, :]
    adapters = jnp.sum(jnp.where(matches, request_adapter[None, :], 0), axis=1)
    owners = [here ^ key for key in shrink]
    low = low_rank([attended, beside], list(shrink.values()), owners, adapters, rank)
    expand, low = lax.optimization_barrier((expand, low))
    expand = far_blocks(expand)
    low = low.astype(jnp.float32)
    step = 1
    while step < shares:
        low = low + exchange(low.astype(jnp.bfloat16), "mp", step).astype(jnp.float32)
        step *= 2
    low = low.astype(jnp.bfloat16)
    correction, other = correct(low, list(expand.values()), owners, adapters, rank)
    return finish(own, [*received, correction, exchange(other, "dp", 1)], occupied)


def solution(mesh):
    placed = (
        P("dp", "mp", None),
        P("dp", "mp", None, None),
        P("dp", "mp", None, None),
        P("dp", "mp", None),
        P("dp", "mp", None),
        P("dp"),
        P("dp"),
        P("dp"),
        P(),
        P("mp", None),
        P("dp", "mp", None),
        P("dp", None, "mp"),
    )
    return jax.shard_map(body, mesh=mesh, in_specs=placed, out_specs=P("dp", "mp"), check_vma=False)
```

```python
import functools
import math

import jax
import jax.numpy as jnp
from jax import lax
from jax.experimental import pallas as pl
from jax.experimental.pallas import tpu as pltpu
from jax.sharding import PartitionSpec as P

MIB = 1024 * 1024
TILE = 256
SMALL = pl.CostEstimate(flops=1, bytes_accessed=1, transcendentals=0)
ID_ROWS = 16


def attend_block(lengths, q_ref, k_ref, v_ref, kn_ref, vn_ref, first, acc_ref):
    slots = len(lengths)
    heads, width = q_ref.shape[1:]
    kv_local, cache = k_ref.shape[1], k_ref.shape[2]
    group = heads // kv_local
    inverse = 1.0 / math.sqrt(width)
    lane = lax.broadcasted_iota(jnp.int32, (group, cache), 1)
    parts = []
    for s in range(slots):
        scores = lax.dot_general(
            q_ref[first + s],
            k_ref[first + s].reshape(kv_local * cache, width),
            (((1,), (1,)), ((), ())),
            preferred_element_type=jnp.float32,
        )
        valid = lane < lengths[s]
        for g in range(kv_local):
            part = scores[g * group : (g + 1) * group, g * cache : (g + 1) * cache]
            parts.append(jnp.where(valid, part * inverse, -jnp.inf))
    cached = jnp.concatenate(parts, axis=0)
    block = pl.ds(first, slots)
    q_all = q_ref[block].astype(jnp.float32).reshape(slots * kv_local, group, width)
    kn = kn_ref[block].astype(jnp.float32).reshape(slots * kv_local, 1, width)
    vn = vn_ref[block].astype(jnp.float32).reshape(slots * kv_local, 1, width)
    fresh = (jnp.sum(q_all * kn, axis=-1, keepdims=True) * inverse).reshape(slots * heads, 1)
    top = jnp.maximum(jnp.max(cached, axis=-1, keepdims=True), fresh)
    cached_exp = jnp.exp(cached - top)
    fresh_exp = jnp.exp(fresh - top)
    scale = 1.0 / (jnp.sum(cached_exp, axis=-1, keepdims=True) + fresh_exp)
    weights = (cached_exp * scale).astype(jnp.bfloat16)
    fresh_w = (fresh_exp * scale).astype(jnp.bfloat16).astype(jnp.float32)
    new_part = (fresh_w.reshape(slots * kv_local, group, 1) * vn).reshape(slots * heads, width)
    for s in range(slots):
        values = jnp.concatenate([v_ref[first + s, g] for g in range(kv_local)], axis=1)
        summed = jnp.dot(
            weights[s * heads : (s + 1) * heads], values, preferred_element_type=jnp.float32
        )
        for g in range(kv_local):
            row = s * heads + g * group
            acc_ref[row : row + group, :] = (
                summed[g * group : (g + 1) * group, g * width : (g + 1) * width]
                + new_part[row : row + group]
            )


def fetch(w_ref, buffer_ref, sem_ref, slot, column):
    return pltpu.make_async_copy(
        w_ref.at[:, pl.ds(pl.multiple_of(column, TILE), TILE)],
        buffer_ref.at[slot],
        sem_ref.at[slot],
    )


def project_tiles(a_ref, w_ref, buffer_ref, sem_ref, out_ref, first_slot, column):
    tiles = out_ref.shape[1] // TILE

    def tile(j, carry):
        slot = first_slot + j
        fetch(w_ref, buffer_ref, sem_ref, slot, column + j * TILE).wait()
        out_ref[:, pl.ds(pl.multiple_of(j * TILE, TILE), TILE)] = jnp.dot(
            a_ref[: out_ref.shape[0]], buffer_ref[slot], preferred_element_type=jnp.float32
        ).astype(out_ref.dtype)
        return carry

    lax.fori_loop(0, tiles, tile, 0)


def fetch_all(sources, targets, sems):
    copies = [
        pltpu.make_async_copy(source, target, sems.at[i])
        for i, (source, target) in enumerate(zip(sources, targets))
    ]
    for copy in copies:
        copy.start()
    return copies


def look_up(requests, adapters):
    slots, known = requests.shape[1], adapters.shape[1]
    matches = lax.broadcasted_iota(jnp.int32, (known, slots), 0) == requests
    numbers = jnp.broadcast_to(adapters.astype(jnp.float32), (ID_ROWS, known))
    return jnp.dot(
        numbers.astype(jnp.bfloat16),
        matches.astype(jnp.float32).astype(jnp.bfloat16),
        preferred_element_type=jnp.float32,
    )


def attend_kernel(
    block,
    lengths_ref,
    chunk_ref,
    q_hbm,
    k_hbm,
    v_hbm,
    kn_hbm,
    vn_hbm,
    request_hbm,
    adapter_hbm,
    w_ref,
    out_ref,
    piece_ref,
    q_ref,
    k_ref,
    v_ref,
    kn_ref,
    vn_ref,
    request_ref,
    adapter_ref,
    acc_ref,
    buffer_ref,
    new_sem,
    block_sem,
    sem_ref,
):
    rows, heads, width = q_ref.shape
    blocks = rows // block
    tiles = piece_ref.shape[1] // TILE
    column = chunk_ref[0] * piece_ref.shape[1]

    def block_copies(i):
        part = pl.ds(pl.multiple_of(i * block, block), block)
        return [
            pltpu.make_async_copy(source.at[part], target.at[part], block_sem.at[j, i])
            for j, (source, target) in enumerate(
                ((q_hbm, q_ref), (k_hbm, k_ref), (v_hbm, v_ref))
            )
        ]

    new_copies = fetch_all(
        (kn_hbm, vn_hbm, request_hbm, adapter_hbm),
        (kn_ref, vn_ref, request_ref, adapter_ref),
        new_sem,
    )

    def begin(i, carry):
        for copy in block_copies(i):
            copy.start()
        return carry

    lax.fori_loop(0, blocks, begin, 0)
    for j in range(tiles):
        fetch(w_ref, buffer_ref, sem_ref, j, column + j * TILE).start()
    for copy in new_copies:
        copy.wait()
    out_ref[pl.ds(rows, ID_ROWS), :] = jnp.zeros((ID_ROWS, out_ref.shape[1]), out_ref.dtype)
    out_ref[pl.ds(rows, ID_ROWS), :rows] = look_up(request_ref[...], adapter_ref[...]).astype(
        out_ref.dtype
    )

    def one_block(i, carry):
        for copy in block_copies(i):
            copy.wait()
        first = pl.multiple_of(i * block, block)
        attend_block(
            [lengths_ref[first + s] for s in range(block)],
            q_ref,
            k_ref,
            v_ref,
            kn_ref,
            vn_ref,
            first,
            acc_ref,
        )
        for h in range(heads):
            out_ref[pl.ds(first, block), h * width : (h + 1) * width] = acc_ref[
                pl.ds(h, block, stride=heads), :
            ].astype(out_ref.dtype)
        return carry

    lax.fori_loop(0, blocks, one_block, 0)
    project_tiles(out_ref, w_ref, buffer_ref, sem_ref, piece_ref, 0, column)


def attend(arrays, lengths, out_weight, chunk, out_local):
    queries, key_cache = arrays[:2]
    rows, heads, width = queries.shape
    cache = key_cache.shape[2]
    block = min(16, rows)
    depth = heads * width
    tiles = out_local // TILE
    smem = pl.BlockSpec(memory_space=pltpu.SMEM)
    hbm = pl.BlockSpec(memory_space=pltpu.HBM)
    vmem = pl.BlockSpec(memory_space=pltpu.VMEM)
    return pl.pallas_call(
        functools.partial(attend_kernel, block),
        in_specs=[smem, smem] + [hbm] * (len(arrays) + 1),
        out_specs=[vmem, vmem],
        scratch_shapes=[pltpu.VMEM(a.shape, a.dtype) for a in arrays]
        + [
            pltpu.VMEM((block * heads, width), jnp.float32),
            pltpu.VMEM((tiles, depth, TILE), jnp.bfloat16),
            pltpu.SemaphoreType.DMA((4,)),
            pltpu.SemaphoreType.DMA((3, rows // block)),
            pltpu.SemaphoreType.DMA((tiles,)),
        ],
        out_shape=[
            jax.ShapeDtypeStruct((rows + ID_ROWS, depth), jnp.bfloat16),
            jax.ShapeDtypeStruct((rows, out_local), jnp.bfloat16),
        ],
        compiler_params=pltpu.CompilerParams(vmem_limit_bytes=60 * MIB),
        cost_estimate=SMALL,
        name="attend",
    )(lengths, chunk.reshape(1), *arrays, out_weight)


def project_kernel(chunks_ref, a_hbm, w_ref, *refs):
    *out_refs, a_ref, buffer_ref, a_sem, sem_ref = refs
    out_local = out_refs[0].shape[1]
    tiles = out_local // TILE
    copy = pltpu.make_async_copy(a_hbm, a_ref, a_sem.at[0])
    copy.start()
    for i in range(len(out_refs)):
        for j in range(tiles):
            column = chunks_ref[i] * out_local + j * TILE
            fetch(w_ref, buffer_ref, sem_ref, i * tiles + j, column).start()
    copy.wait()
    for i, out_ref in enumerate(out_refs):
        project_tiles(
            a_ref, w_ref, buffer_ref, sem_ref, out_ref, i * tiles, chunks_ref[i] * out_local
        )


def project(attended, out_weight, chunks, out_local, dtypes):
    rows, depth = attended.shape[0] - ID_ROWS, attended.shape[1]
    slots = len(dtypes) * (out_local // TILE)
    vmem = pl.BlockSpec(memory_space=pltpu.VMEM)
    hbm = pl.BlockSpec(memory_space=pl.ANY)
    return pl.pallas_call(
        project_kernel,
        in_specs=[pl.BlockSpec(memory_space=pltpu.SMEM), hbm, hbm],
        out_specs=[vmem for _ in dtypes],
        scratch_shapes=[
            pltpu.VMEM(attended.shape, attended.dtype),
            pltpu.VMEM((slots, depth, TILE), jnp.bfloat16),
            pltpu.SemaphoreType.DMA((1,)),
            pltpu.SemaphoreType.DMA((slots,)),
        ],
        out_shape=[jax.ShapeDtypeStruct((rows, out_local), dtype) for dtype in dtypes],
        compiler_params=pltpu.CompilerParams(vmem_limit_bytes=60 * MIB),
        cost_estimate=SMALL,
        name="project",
    )(jnp.stack(chunks), attended, out_weight)


def masked(low, owner, adapters, ranks, adapters_here):
    terms = jnp.concatenate([low] * adapters_here, axis=0)
    row = lax.broadcasted_iota(jnp.int32, terms.shape, 0)
    return jnp.where(row // ranks + owner * adapters_here == adapters, terms, 0.0)


def block_parts(blocks):
    arrays, places = [], []
    for i, parts in enumerate(blocks):
        first = 0
        for part in parts:
            arrays.append(part)
            places.append((i, first, part.shape[0]))
            first += part.shape[0]
    return arrays, places


def fetch_blocks(sources, places, column, target, sems, offset):
    columns = pl.ds(column, target.shape[2])
    return [
        pltpu.make_async_copy(
            source.at[:, columns], target.at[i, pl.ds(first, count)], sems.at[offset + j]
        )
        for j, (source, (i, first, count)) in enumerate(zip(sources, places))
    ]


def low_kernel(ranks, places, owners_ref, *refs):
    sides, sources = refs[:2], refs[2 : 2 + len(places)]
    out_ref, adapters_ref, side_ref, block_ref, sems = refs[2 + len(places) :]
    copies = fetch_all(sides, [side_ref.at[i] for i in range(2)], sems)
    parts = fetch_blocks(sources, places, 0, block_ref, sems, 2)
    for copy in parts:
        copy.start()
    blocks, pair = block_ref.shape[:2]
    rows = side_ref.shape[1] - ID_ROWS
    sides_t, adapters = [], []
    for i, copy in enumerate(copies):
        copy.wait()
        sides_t.append(side_ref[i, :rows].astype(jnp.float32).T.astype(jnp.bfloat16))
        ids = side_ref[i, rows:, :rows].astype(jnp.float32)
        adapters.append(ids[:8].astype(jnp.int32))
    a_t = jnp.concatenate(sides_t, axis=1)
    adapters_ref[...] = jnp.concatenate(adapters, axis=1)
    adapters = adapters_ref[:1, :]
    row = lax.broadcasted_iota(jnp.int32, (pair, a_t.shape[1]), 0)
    total = jnp.zeros(row.shape, jnp.float32)
    for i in range(blocks):
        for copy, place in zip(parts, places):
            if place[0] == i:
                copy.wait()
        part = jnp.dot(block_ref[i], a_t, preferred_element_type=jnp.float32)
        first = owners_ref[i] * (pair // ranks)
        total += jnp.where(row // ranks + first == adapters, part, 0.0)
    low = total[:ranks]
    for a in range(1, pair // ranks):
        low += total[a * ranks : (a + 1) * ranks]
    out_ref[...] = low.astype(out_ref.dtype)


def low_rank(sides, blocks, depth, owners, rank):
    rows = sides[0].shape[0] - ID_ROWS
    arrays, places = block_parts(blocks)
    pair = sum(part.shape[0] for part in blocks[0])
    vmem = pl.BlockSpec(memory_space=pltpu.VMEM)
    return pl.pallas_call(
        functools.partial(low_kernel, rank, places),
        in_specs=[pl.BlockSpec(memory_space=pltpu.SMEM)]
        + [pl.BlockSpec(memory_space=pl.ANY)] * (2 + len(arrays)),
        out_specs=[vmem, vmem],
        out_shape=[
            jax.ShapeDtypeStruct((rank, 2 * rows), jnp.bfloat16),
            jax.ShapeDtypeStruct((8, 2 * rows), jnp.int32),
        ],
        scratch_shapes=[
            pltpu.VMEM((2, *sides[0].shape), jnp.bfloat16),
            pltpu.VMEM((len(blocks), pair, depth), jnp.bfloat16),
            pltpu.SemaphoreType.DMA((2 + len(arrays),)),
        ],
        compiler_params=pltpu.CompilerParams(vmem_limit_bytes=32 * MIB),
        cost_estimate=SMALL,
        name="low_rank",
    )(jnp.stack(owners), *sides, *arrays)


def delta_kernel(ranks, places, column, owners_ref, adapters_ref, low_ref, *refs):
    sources = refs[: len(places)]
    here_ref, other_ref, block_ref, sems = refs[len(places) :]
    parts = fetch_blocks(sources, places, column, block_ref, sems, 0)
    for copy in parts:
        copy.start()
    blocks, pair, width = block_ref.shape
    low = low_ref[...].astype(jnp.float32)
    sides = []
    for i in range(blocks):
        mine = masked(low, owners_ref[i], adapters_ref[:1, :], ranks, pair // ranks)
        sides.append(mine.T.astype(jnp.bfloat16))
    for copy in parts:
        copy.wait()
    delta = jnp.dot(
        jnp.concatenate(sides, axis=1),
        block_ref[...].reshape(blocks * pair, width),
        preferred_element_type=jnp.float32,
    )
    delta = (0.5 * delta).astype(jnp.bfloat16)
    rows = here_ref.shape[0]
    here_ref[...] = delta[:rows]
    other_ref[...] = delta[rows:]


def correct(low, adapters, blocks, column, out_local, owners, rank):
    slots = adapters.shape[1]
    arrays, places = block_parts(blocks)
    pair = sum(part.shape[0] for part in blocks[0])
    vmem = pl.BlockSpec(memory_space=pltpu.VMEM)
    out = jax.ShapeDtypeStruct((slots // 2, out_local), jnp.bfloat16)
    return pl.pallas_call(
        functools.partial(delta_kernel, rank, places, column),
        in_specs=[pl.BlockSpec(memory_space=pltpu.SMEM), vmem, vmem]
        + [pl.BlockSpec(memory_space=pl.ANY)] * len(arrays),
        out_specs=[vmem, vmem],
        out_shape=[out, out],
        scratch_shapes=[
            pltpu.VMEM((len(blocks), pair, out_local), jnp.bfloat16),
            pltpu.SemaphoreType.DMA((len(arrays),)),
        ],
        compiler_params=pltpu.CompilerParams(vmem_limit_bytes=32 * MIB),
        cost_estimate=SMALL,
        name="correct",
    )(jnp.stack(owners), adapters, low, *arrays)


def finish_kernel(occupied_ref, own_ref, *refs):
    *part_refs, out_ref = refs
    rows = out_ref.shape[0]
    live = jnp.broadcast_to(occupied_ref[...].astype(jnp.float32), (128, rows)).T
    for j in range(0, out_ref.shape[1], 128):
        columns = slice(j, j + 128)
        total = own_ref[:, columns]
        for ref in part_refs:
            total += ref[:, columns].astype(jnp.float32)
        out_ref[:, columns] = (live * total).astype(out_ref.dtype)


def finish(own, parts, occupied):
    rows, out_local = own.shape
    vmem = pl.BlockSpec(memory_space=pltpu.VMEM)
    return pl.pallas_call(
        finish_kernel,
        in_specs=[vmem] * (2 + len(parts)),
        out_specs=vmem,
        out_shape=jax.ShapeDtypeStruct((rows, out_local), jnp.bfloat16),
        compiler_params=pltpu.CompilerParams(vmem_limit_bytes=32 * MIB),
        cost_estimate=SMALL,
        name="finish",
    )(occupied.reshape(1, rows), own, *parts)


def exchange(value, axis, step):
    count = lax.axis_size(axis)
    return lax.ppermute(value, axis, [(i, i ^ step) for i in range(count)])


def neighbours():
    return [1 << i for i in range(1, lax.axis_size("dp").bit_length() - 1)]


def near_blocks(own):
    return {0: [own], **{bit: [exchange(own, "dp", bit)] for bit in neighbours()[:2]}}


def far_blocks(blocks):
    blocks = dict(blocks)
    a, b, *others = neighbours()
    half = blocks[0][0].shape[0] // 2
    blocks[a | b] = [
        exchange(blocks[a][0][:half], "dp", b),
        exchange(blocks[b][0][half:], "dp", a),
    ]
    for bit in others:
        for key in list(blocks):
            blocks[key | bit] = [exchange(part, "dp", bit) for part in blocks[key]]
    return blocks


def together(*values):
    return lax.optimization_barrier(values)


def body(
    queries,
    key_cache,
    value_cache,
    key_new,
    value_new,
    lengths,
    occupied,
    slot_request,
    request_adapter,
    out_weight,
    shrink_weight,
    expand_weight,
):
    adapters_here, depth, rank = shrink_weight.shape
    out_local = expand_weight.shape[2]
    shares = lax.axis_size("mp")
    me = lax.axis_index("mp")
    here = lax.axis_index("dp")
    pair = adapters_here * rank
    steps = list(range(shares - 1, 0, -1))

    own_block = jnp.concatenate(
        [
            jnp.swapaxes(shrink_weight, 1, 2).reshape(pair, depth),
            expand_weight.reshape(pair, out_local),
        ],
        axis=1,
    )
    blocks = near_blocks(own_block)
    attended, piece = attend(
        (
            queries,
            key_cache,
            value_cache,
            key_new,
            value_new,
            slot_request.reshape(1, -1),
            request_adapter.reshape(1, -1),
        ),
        lengths,
        out_weight,
        me ^ steps[0],
        out_local,
    )
    chained = shares == 4
    if chained:
        passed = lax.ppermute(piece, "mp", [(0, 1), (3, 2)])
        received = [lax.ppermute(piece, "mp", [(1, 2), (2, 1)])]
    else:
        received = [exchange(piece, "mp", steps[0])]
    (piece,) = project(attended, out_weight, [me ^ steps[1]], out_local, [jnp.bfloat16])
    if chained:
        piece, passed, received = together(piece, passed, received)
        piece = (piece.astype(jnp.float32) + passed.astype(jnp.float32)).astype(jnp.bfloat16)
    blocks, attended, piece = together(blocks, attended, piece)
    received.append(exchange(piece, "mp", steps[1]))
    blocks = far_blocks(blocks)
    beside = exchange(attended, "dp", 1)
    *pieces, own = project(
        attended,
        out_weight,
        [me ^ step for step in steps[2:]] + [me],
        out_local,
        [jnp.bfloat16] * (shares - 3) + [jnp.float32],
    )
    attended, own = together(attended, own)

    owners = [here ^ key for key in blocks]
    blocks = list(blocks.values())
    low, adapters = low_rank([attended, beside], blocks, depth, owners, rank)
    received += [exchange(piece, "mp", step) for piece, step in zip(pieces, steps[2:])]
    low, received = together(low, received)
    step = 1
    while step < shares:
        arrived = exchange(low, "mp", step)
        low = (low.astype(jnp.float32) + arrived.astype(jnp.float32)).astype(jnp.bfloat16)
        step *= 2
    correction, other = correct(low, adapters, blocks, depth, out_local, owners, rank)
    return finish(own, [*received, correction, exchange(other, "dp", 1)], occupied)


def solution(mesh):
    placed = (
        P("dp", "mp", None),
        P("dp", "mp", None, None),
        P("dp", "mp", None, None),
        P("dp", "mp", None),
        P("dp", "mp", None),
        P("dp"),
        P("dp"),
        P("dp"),
        P(),
        P("mp", None),
        P("dp", "mp", None),
        P("dp", None, "mp"),
    )
    return jax.shard_map(body, mesh=mesh, in_specs=placed, out_specs=P("dp", "mp"), check_vma=False)
```

```python
import functools
import math

import jax
import jax.numpy as jnp
from jax import lax
from jax.experimental import pallas as pl
from jax.experimental.pallas import tpu as pltpu
from jax.sharding import PartitionSpec as P

MIB = 1024 * 1024
TILE = 256
SMALL = pl.CostEstimate(flops=1, bytes_accessed=1, transcendentals=0)
ID_ROWS = 16


def attend_block(lengths, q_ref, k_ref, v_ref, kn_ref, vn_ref, first, acc_ref):
    slots = len(lengths)
    heads, width = q_ref.shape[1:]
    kv_local, cache = k_ref.shape[1], k_ref.shape[2]
    group = heads // kv_local
    inverse = 1.0 / math.sqrt(width)
    lane = lax.broadcasted_iota(jnp.int32, (group, cache), 1)
    parts = []
    for s in range(slots):
        scores = lax.dot_general(
            q_ref[first + s],
            k_ref[first + s].reshape(kv_local * cache, width),
            (((1,), (1,)), ((), ())),
            preferred_element_type=jnp.float32,
        )
        valid = lane < lengths[s]
        for g in range(kv_local):
            part = scores[g * group : (g + 1) * group, g * cache : (g + 1) * cache]
            parts.append(jnp.where(valid, part * inverse, -jnp.inf))
    cached = jnp.concatenate(parts, axis=0)
    block = pl.ds(first, slots)
    q_all = q_ref[block].astype(jnp.float32).reshape(slots * kv_local, group, width)
    kn = kn_ref[block].astype(jnp.float32).reshape(slots * kv_local, 1, width)
    vn = vn_ref[block].astype(jnp.float32).reshape(slots * kv_local, 1, width)
    fresh = (jnp.sum(q_all * kn, axis=-1, keepdims=True) * inverse).reshape(slots * heads, 1)
    top = jnp.maximum(jnp.max(cached, axis=-1, keepdims=True), fresh)
    cached_exp = jnp.exp(cached - top)
    fresh_exp = jnp.exp(fresh - top)
    scale = 1.0 / (jnp.sum(cached_exp, axis=-1, keepdims=True) + fresh_exp)
    weights = (cached_exp * scale).astype(jnp.bfloat16)
    fresh_w = (fresh_exp * scale).astype(jnp.bfloat16).astype(jnp.float32)
    new_part = (fresh_w.reshape(slots * kv_local, group, 1) * vn).reshape(slots * heads, width)
    for s in range(slots):
        values = jnp.concatenate([v_ref[first + s, g] for g in range(kv_local)], axis=1)
        summed = jnp.dot(
            weights[s * heads : (s + 1) * heads], values, preferred_element_type=jnp.float32
        )
        for g in range(kv_local):
            row = s * heads + g * group
            acc_ref[row : row + group, :] = (
                summed[g * group : (g + 1) * group, g * width : (g + 1) * width]
                + new_part[row : row + group]
            )


def fetch(w_ref, buffer_ref, sem_ref, slot, column):
    return pltpu.make_async_copy(
        w_ref.at[:, pl.ds(pl.multiple_of(column, TILE), TILE)],
        buffer_ref.at[slot],
        sem_ref.at[slot],
    )


def project_tiles(a_ref, w_ref, buffer_ref, sem_ref, out_ref, first_slot, column):
    tiles = out_ref.shape[1] // TILE

    def tile(j, carry):
        slot = first_slot + j
        fetch(w_ref, buffer_ref, sem_ref, slot, column + j * TILE).wait()
        out_ref[:, pl.ds(pl.multiple_of(j * TILE, TILE), TILE)] = jnp.dot(
            a_ref[: out_ref.shape[0]], buffer_ref[slot], preferred_element_type=jnp.float32
        ).astype(out_ref.dtype)
        return carry

    lax.fori_loop(0, tiles, tile, 0)


def fetch_all(sources, targets, sems):
    copies = [
        pltpu.make_async_copy(source, target, sems.at[i])
        for i, (source, target) in enumerate(zip(sources, targets))
    ]
    for copy in copies:
        copy.start()
    return copies


def look_up(requests, adapters):
    slots, known = requests.shape[1], adapters.shape[1]
    matches = lax.broadcasted_iota(jnp.int32, (known, slots), 0) == requests
    numbers = jnp.broadcast_to(adapters.astype(jnp.float32), (ID_ROWS, known))
    return jnp.dot(
        numbers.astype(jnp.bfloat16),
        matches.astype(jnp.float32).astype(jnp.bfloat16),
        preferred_element_type=jnp.float32,
    )


def attend_kernel(
    block,
    lengths_ref,
    chunks_ref,
    q_hbm,
    k_hbm,
    v_hbm,
    kn_hbm,
    vn_hbm,
    request_hbm,
    adapter_hbm,
    w_ref,
    out_ref,
    first_ref,
    second_ref,
    q_ref,
    k_ref,
    v_ref,
    kn_ref,
    vn_ref,
    request_ref,
    adapter_ref,
    acc_ref,
    buffer_ref,
    new_sem,
    block_sem,
    sem_ref,
):
    rows, heads, width = q_ref.shape
    blocks = rows // block
    piece_refs = (first_ref, second_ref)
    out_local = first_ref.shape[1]
    tiles = out_local // TILE

    def block_copies(i):
        part = pl.ds(pl.multiple_of(i * block, block), block)
        return [
            pltpu.make_async_copy(source.at[part], target.at[part], block_sem.at[j, i])
            for j, (source, target) in enumerate(
                ((q_hbm, q_ref), (k_hbm, k_ref), (v_hbm, v_ref))
            )
        ]

    new_copies = fetch_all(
        (kn_hbm, vn_hbm, request_hbm, adapter_hbm),
        (kn_ref, vn_ref, request_ref, adapter_ref),
        new_sem,
    )

    def begin(i, carry):
        for copy in block_copies(i):
            copy.start()
        return carry

    lax.fori_loop(0, blocks, begin, 0)
    for i in range(len(piece_refs)):
        for j in range(tiles):
            column = chunks_ref[i] * out_local + j * TILE
            fetch(w_ref, buffer_ref, sem_ref, i * tiles + j, column).start()
    for copy in new_copies:
        copy.wait()
    out_ref[pl.ds(rows, ID_ROWS), :] = jnp.zeros((ID_ROWS, out_ref.shape[1]), out_ref.dtype)
    out_ref[pl.ds(rows, ID_ROWS), :rows] = look_up(request_ref[...], adapter_ref[...]).astype(
        out_ref.dtype
    )

    def one_block(i, carry):
        for copy in block_copies(i):
            copy.wait()
        first = pl.multiple_of(i * block, block)
        attend_block(
            [lengths_ref[first + s] for s in range(block)],
            q_ref,
            k_ref,
            v_ref,
            kn_ref,
            vn_ref,
            first,
            acc_ref,
        )
        for h in range(heads):
            out_ref[pl.ds(first, block), h * width : (h + 1) * width] = acc_ref[
                pl.ds(h, block, stride=heads), :
            ].astype(out_ref.dtype)
        return carry

    lax.fori_loop(0, blocks, one_block, 0)
    for i, piece_ref in enumerate(piece_refs):
        column = chunks_ref[i] * out_local
        project_tiles(out_ref, w_ref, buffer_ref, sem_ref, piece_ref, i * tiles, column)


def attend(arrays, lengths, out_weight, chunks, out_local):
    queries, key_cache = arrays[:2]
    rows, heads, width = queries.shape
    cache = key_cache.shape[2]
    block = min(16, rows)
    depth = heads * width
    tiles = len(chunks) * (out_local // TILE)
    smem = pl.BlockSpec(memory_space=pltpu.SMEM)
    hbm = pl.BlockSpec(memory_space=pltpu.HBM)
    vmem = pl.BlockSpec(memory_space=pltpu.VMEM)
    return pl.pallas_call(
        functools.partial(attend_kernel, block),
        in_specs=[smem, smem] + [hbm] * (len(arrays) + 1),
        out_specs=[vmem, vmem, vmem],
        scratch_shapes=[pltpu.VMEM(a.shape, a.dtype) for a in arrays]
        + [
            pltpu.VMEM((block * heads, width), jnp.float32),
            pltpu.VMEM((tiles, depth, TILE), jnp.bfloat16),
            pltpu.SemaphoreType.DMA((4,)),
            pltpu.SemaphoreType.DMA((3, rows // block)),
            pltpu.SemaphoreType.DMA((tiles,)),
        ],
        out_shape=[
            jax.ShapeDtypeStruct((rows + ID_ROWS, depth), jnp.bfloat16),
        ]
        + [jax.ShapeDtypeStruct((rows, out_local), jnp.bfloat16) for _ in chunks],
        compiler_params=pltpu.CompilerParams(vmem_limit_bytes=57 * MIB),
        cost_estimate=SMALL,
        name="attend",
    )(lengths, jnp.stack(chunks), *arrays, out_weight)


def project_kernel(chunks_ref, a_hbm, w_ref, *refs):
    *out_refs, a_ref, buffer_ref, a_sem, sem_ref = refs
    out_local = out_refs[0].shape[1]
    tiles = out_local // TILE
    copy = pltpu.make_async_copy(a_hbm, a_ref, a_sem.at[0])
    copy.start()
    for i in range(len(out_refs)):
        for j in range(tiles):
            column = chunks_ref[i] * out_local + j * TILE
            fetch(w_ref, buffer_ref, sem_ref, i * tiles + j, column).start()
    copy.wait()
    for i, out_ref in enumerate(out_refs):
        project_tiles(
            a_ref, w_ref, buffer_ref, sem_ref, out_ref, i * tiles, chunks_ref[i] * out_local
        )


def project(attended, out_weight, chunks, out_local, dtypes):
    rows, depth = attended.shape[0] - ID_ROWS, attended.shape[1]
    slots = len(dtypes) * (out_local // TILE)
    vmem = pl.BlockSpec(memory_space=pltpu.VMEM)
    hbm = pl.BlockSpec(memory_space=pl.ANY)
    return pl.pallas_call(
        project_kernel,
        in_specs=[pl.BlockSpec(memory_space=pltpu.SMEM), hbm, hbm],
        out_specs=[vmem for _ in dtypes],
        scratch_shapes=[
            pltpu.VMEM(attended.shape, attended.dtype),
            pltpu.VMEM((slots, depth, TILE), jnp.bfloat16),
            pltpu.SemaphoreType.DMA((1,)),
            pltpu.SemaphoreType.DMA((slots,)),
        ],
        out_shape=[jax.ShapeDtypeStruct((rows, out_local), dtype) for dtype in dtypes],
        compiler_params=pltpu.CompilerParams(vmem_limit_bytes=52 * MIB),
        cost_estimate=SMALL,
        name="project",
    )(jnp.stack(chunks), attended, out_weight)


def masked(low, owner, adapters, ranks, adapters_here):
    terms = jnp.concatenate([low] * adapters_here, axis=0)
    row = lax.broadcasted_iota(jnp.int32, terms.shape, 0)
    return jnp.where(row // ranks + owner * adapters_here == adapters, terms, 0.0)


def block_parts(blocks):
    arrays, places = [], []
    for i, parts in enumerate(blocks):
        first = 0
        for part in parts:
            arrays.append(part)
            places.append((i, first, part.shape[0]))
            first += part.shape[0]
    return arrays, places


def fetch_blocks(sources, places, column, target, sems, offset):
    columns = pl.ds(column, target.shape[2])
    return [
        pltpu.make_async_copy(
            source.at[:, columns], target.at[i, pl.ds(first, count)], sems.at[offset + j]
        )
        for j, (source, (i, first, count)) in enumerate(zip(sources, places))
    ]


def low_kernel(ranks, places, owners_ref, *refs):
    sides, sources = refs[:2], refs[2 : 2 + len(places)]
    out_ref, adapters_ref, side_ref, block_ref, sems = refs[2 + len(places) :]
    copies = fetch_all(sides, [side_ref.at[i] for i in range(2)], sems)
    parts = fetch_blocks(sources, places, 0, block_ref, sems, 2)
    for copy in parts:
        copy.start()
    blocks, pair = block_ref.shape[:2]
    rows = side_ref.shape[1] - ID_ROWS
    sides_t, adapters = [], []
    for i, copy in enumerate(copies):
        copy.wait()
        sides_t.append(side_ref[i, :rows].astype(jnp.float32).T.astype(jnp.bfloat16))
        ids = side_ref[i, rows:, :rows].astype(jnp.float32)
        adapters.append(ids[:8].astype(jnp.int32))
    a_t = jnp.concatenate(sides_t, axis=1)
    adapters_ref[...] = jnp.concatenate(adapters, axis=1)
    adapters = adapters_ref[:1, :]
    row = lax.broadcasted_iota(jnp.int32, (pair, a_t.shape[1]), 0)
    total = jnp.zeros(row.shape, jnp.float32)
    for i in range(blocks):
        for copy, place in zip(parts, places):
            if place[0] == i:
                copy.wait()
        part = jnp.dot(block_ref[i], a_t, preferred_element_type=jnp.float32)
        first = owners_ref[i] * (pair // ranks)
        total += jnp.where(row // ranks + first == adapters, part, 0.0)
    low = total[:ranks]
    for a in range(1, pair // ranks):
        low += total[a * ranks : (a + 1) * ranks]
    out_ref[...] = low.astype(out_ref.dtype)


def low_rank(sides, blocks, depth, owners, rank):
    rows = sides[0].shape[0] - ID_ROWS
    arrays, places = block_parts(blocks)
    pair = sum(part.shape[0] for part in blocks[0])
    vmem = pl.BlockSpec(memory_space=pltpu.VMEM)
    return pl.pallas_call(
        functools.partial(low_kernel, rank, places),
        in_specs=[pl.BlockSpec(memory_space=pltpu.SMEM)]
        + [pl.BlockSpec(memory_space=pl.ANY)] * (2 + len(arrays)),
        out_specs=[vmem, vmem],
        out_shape=[
            jax.ShapeDtypeStruct((rank, 2 * rows), jnp.bfloat16),
            jax.ShapeDtypeStruct((8, 2 * rows), jnp.int32),
        ],
        scratch_shapes=[
            pltpu.VMEM((2, *sides[0].shape), jnp.bfloat16),
            pltpu.VMEM((len(blocks), pair, depth), jnp.bfloat16),
            pltpu.SemaphoreType.DMA((2 + len(arrays),)),
        ],
        compiler_params=pltpu.CompilerParams(vmem_limit_bytes=32 * MIB),
        cost_estimate=SMALL,
        name="low_rank",
    )(jnp.stack(owners), *sides, *arrays)


def delta_kernel(ranks, places, column, owners_ref, adapters_ref, low_ref, *refs):
    sources = refs[: len(places)]
    here_ref, other_ref, block_ref, sems = refs[len(places) :]
    parts = fetch_blocks(sources, places, column, block_ref, sems, 0)
    for copy in parts:
        copy.start()
    blocks, pair, width = block_ref.shape
    low = low_ref[...].astype(jnp.float32)
    sides = []
    for i in range(blocks):
        mine = masked(low, owners_ref[i], adapters_ref[:1, :], ranks, pair // ranks)
        sides.append(mine.T.astype(jnp.bfloat16))
    for copy in parts:
        copy.wait()
    delta = jnp.dot(
        jnp.concatenate(sides, axis=1),
        block_ref[...].reshape(blocks * pair, width),
        preferred_element_type=jnp.float32,
    )
    delta = (0.5 * delta).astype(jnp.bfloat16)
    rows = here_ref.shape[0]
    here_ref[...] = delta[:rows]
    other_ref[...] = delta[rows:]


def correct(low, adapters, blocks, column, out_local, owners, rank):
    slots = adapters.shape[1]
    arrays, places = block_parts(blocks)
    pair = sum(part.shape[0] for part in blocks[0])
    vmem = pl.BlockSpec(memory_space=pltpu.VMEM)
    out = jax.ShapeDtypeStruct((slots // 2, out_local), jnp.bfloat16)
    return pl.pallas_call(
        functools.partial(delta_kernel, rank, places, column),
        in_specs=[pl.BlockSpec(memory_space=pltpu.SMEM), vmem, vmem]
        + [pl.BlockSpec(memory_space=pl.ANY)] * len(arrays),
        out_specs=[vmem, vmem],
        out_shape=[out, out],
        scratch_shapes=[
            pltpu.VMEM((len(blocks), pair, out_local), jnp.bfloat16),
            pltpu.SemaphoreType.DMA((len(arrays),)),
        ],
        compiler_params=pltpu.CompilerParams(vmem_limit_bytes=32 * MIB),
        cost_estimate=SMALL,
        name="correct",
    )(jnp.stack(owners), adapters, low, *arrays)


def finish_kernel(occupied_ref, own_ref, *refs):
    *part_refs, out_ref = refs
    rows = out_ref.shape[0]
    live = jnp.broadcast_to(occupied_ref[...].astype(jnp.float32), (128, rows)).T
    for j in range(0, out_ref.shape[1], 128):
        columns = slice(j, j + 128)
        total = own_ref[:, columns]
        for ref in part_refs:
            total += ref[:, columns].astype(jnp.float32)
        out_ref[:, columns] = (live * total).astype(out_ref.dtype)


def finish(own, parts, occupied):
    rows, out_local = own.shape
    vmem = pl.BlockSpec(memory_space=pltpu.VMEM)
    return pl.pallas_call(
        finish_kernel,
        in_specs=[vmem] * (2 + len(parts)),
        out_specs=vmem,
        out_shape=jax.ShapeDtypeStruct((rows, out_local), jnp.bfloat16),
        compiler_params=pltpu.CompilerParams(vmem_limit_bytes=32 * MIB),
        cost_estimate=SMALL,
        name="finish",
    )(occupied.reshape(1, rows), own, *parts)


def exchange(value, axis, step):
    count = lax.axis_size(axis)
    return lax.ppermute(value, axis, [(i, i ^ step) for i in range(count)])


def neighbours():
    return [1 << i for i in range(1, lax.axis_size("dp").bit_length() - 1)]


def near_blocks(own):
    return {0: [own], **{bit: [exchange(own, "dp", bit)] for bit in neighbours()[:2]}}


def far_blocks(blocks):
    blocks = dict(blocks)
    a, b, *others = neighbours()
    half = blocks[0][0].shape[0] // 2
    blocks[a | b] = [
        exchange(blocks[a][0][:half], "dp", b),
        exchange(blocks[b][0][half:], "dp", a),
    ]
    for bit in others:
        for key in list(blocks):
            blocks[key | bit] = [exchange(part, "dp", bit) for part in blocks[key]]
    return blocks


def together(*values):
    return lax.optimization_barrier(values)


def body(
    queries,
    key_cache,
    value_cache,
    key_new,
    value_new,
    lengths,
    occupied,
    slot_request,
    request_adapter,
    out_weight,
    shrink_weight,
    expand_weight,
):
    adapters_here, depth, rank = shrink_weight.shape
    out_local = expand_weight.shape[2]
    shares = lax.axis_size("mp")
    me = lax.axis_index("mp")
    here = lax.axis_index("dp")
    pair = adapters_here * rank
    steps = list(range(shares - 1, 0, -1))

    own_block = jnp.concatenate(
        [
            jnp.swapaxes(shrink_weight, 1, 2).reshape(pair, depth),
            expand_weight.reshape(pair, out_local),
        ],
        axis=1,
    )
    blocks = near_blocks(own_block)
    attended, piece, second = attend(
        (
            queries,
            key_cache,
            value_cache,
            key_new,
            value_new,
            slot_request.reshape(1, -1),
            request_adapter.reshape(1, -1),
        ),
        lengths,
        out_weight,
        [me ^ step for step in steps[:2]],
        out_local,
    )
    chained = shares == 4
    if chained:
        passed = lax.ppermute(piece, "mp", [(0, 1), (3, 2)])
        received = [lax.ppermute(piece, "mp", [(1, 2), (2, 1)])]
    else:
        received = [exchange(piece, "mp", steps[0])]
    *pieces, own = project(
        attended,
        out_weight,
        [me ^ step for step in steps[2:]] + [me],
        out_local,
        [jnp.bfloat16] * (shares - 3) + [jnp.float32],
    )
    if chained:
        passed, received, second, own = together(passed, received, second, own)
        second = (second.astype(jnp.float32) + passed.astype(jnp.float32)).astype(jnp.bfloat16)
    blocks, attended, own = together(blocks, attended, own)
    received.append(exchange(second, "mp", steps[1]))
    received += [exchange(piece, "mp", step) for piece, step in zip(pieces, steps[2:])]
    blocks = far_blocks(blocks)
    beside = exchange(attended, "dp", 1)

    owners = [here ^ key for key in blocks]
    blocks = list(blocks.values())
    low, adapters = low_rank([attended, beside], blocks, depth, owners, rank)
    low, received = together(low, received)
    lows = [low] + [exchange(low, "mp", step) for step in range(1, shares)]
    low = sum(part.astype(jnp.float32) for part in lows).astype(jnp.bfloat16)
    correction, other = correct(low, adapters, blocks, depth, out_local, owners, rank)
    return finish(own, [*received, correction, exchange(other, "dp", 1)], occupied)


def solution(mesh):
    placed = (
        P("dp", "mp", None),
        P("dp", "mp", None, None),
        P("dp", "mp", None, None),
        P("dp", "mp", None),
        P("dp", "mp", None),
        P("dp"),
        P("dp"),
        P("dp"),
        P(),
        P("mp", None),
        P("dp", "mp", None),
        P("dp", None, "mp"),
    )
    return jax.shard_map(body, mesh=mesh, in_specs=placed, out_specs=P("dp", "mp"), check_vma=False)
```

```python
import functools
import math

import jax
import jax.numpy as jnp
from jax import lax
from jax.experimental import pallas as pl
from jax.experimental.pallas import tpu as pltpu
from jax.sharding import PartitionSpec as P

MIB = 1024 * 1024
TILE = 256
SMALL = pl.CostEstimate(flops=1, bytes_accessed=1, transcendentals=0)
ID_ROWS = 16


def attend_block(lengths, q_ref, k_ref, v_ref, kn_ref, vn_ref, first, acc_ref):
    slots = len(lengths)
    heads, width = q_ref.shape[1:]
    kv_local, cache = k_ref.shape[1], k_ref.shape[2]
    group = heads // kv_local
    inverse = 1.0 / math.sqrt(width)
    lane = lax.broadcasted_iota(jnp.int32, (group, cache), 1)
    parts = []
    for s in range(slots):
        scores = lax.dot_general(
            q_ref[first + s],
            k_ref[first + s].reshape(kv_local * cache, width),
            (((1,), (1,)), ((), ())),
            preferred_element_type=jnp.float32,
        )
        valid = lane < lengths[s]
        for g in range(kv_local):
            part = scores[g * group : (g + 1) * group, g * cache : (g + 1) * cache]
            parts.append(jnp.where(valid, part * inverse, -jnp.inf))
    cached = jnp.concatenate(parts, axis=0)
    block = pl.ds(first, slots)
    q_all = q_ref[block].astype(jnp.float32).reshape(slots * kv_local, group, width)
    kn = kn_ref[block].astype(jnp.float32).reshape(slots * kv_local, 1, width)
    vn = vn_ref[block].astype(jnp.float32).reshape(slots * kv_local, 1, width)
    fresh = (jnp.sum(q_all * kn, axis=-1, keepdims=True) * inverse).reshape(slots * heads, 1)
    top = jnp.maximum(jnp.max(cached, axis=-1, keepdims=True), fresh)
    cached_exp = jnp.exp(cached - top)
    fresh_exp = jnp.exp(fresh - top)
    scale = 1.0 / (jnp.sum(cached_exp, axis=-1, keepdims=True) + fresh_exp)
    weights = (cached_exp * scale).astype(jnp.bfloat16)
    fresh_w = (fresh_exp * scale).astype(jnp.bfloat16).astype(jnp.float32)
    new_part = (fresh_w.reshape(slots * kv_local, group, 1) * vn).reshape(slots * heads, width)
    for s in range(slots):
        values = jnp.concatenate([v_ref[first + s, g] for g in range(kv_local)], axis=1)
        summed = jnp.dot(
            weights[s * heads : (s + 1) * heads], values, preferred_element_type=jnp.float32
        )
        for g in range(kv_local):
            row = s * heads + g * group
            acc_ref[row : row + group, :] = (
                summed[g * group : (g + 1) * group, g * width : (g + 1) * width]
                + new_part[row : row + group]
            )


def fetch(w_ref, buffer_ref, sem_ref, slot, column):
    return pltpu.make_async_copy(
        w_ref.at[:, pl.ds(pl.multiple_of(column, TILE), TILE)],
        buffer_ref.at[slot],
        sem_ref.at[slot],
    )


def project_tiles(a_ref, w_ref, buffer_ref, sem_ref, out_ref, first_slot, column):
    tiles = out_ref.shape[1] // TILE

    def tile(j, carry):
        slot = first_slot + j
        fetch(w_ref, buffer_ref, sem_ref, slot, column + j * TILE).wait()
        out_ref[:, pl.ds(pl.multiple_of(j * TILE, TILE), TILE)] = jnp.dot(
            a_ref[: out_ref.shape[0]], buffer_ref[slot], preferred_element_type=jnp.float32
        ).astype(out_ref.dtype)
        return carry

    lax.fori_loop(0, tiles, tile, 0)


def fetch_all(sources, targets, sems):
    copies = [
        pltpu.make_async_copy(source, target, sems.at[i])
        for i, (source, target) in enumerate(zip(sources, targets))
    ]
    for copy in copies:
        copy.start()
    return copies


def look_up(requests, adapters):
    slots, known = requests.shape[1], adapters.shape[1]
    matches = lax.broadcasted_iota(jnp.int32, (known, slots), 0) == requests
    numbers = jnp.broadcast_to(adapters.astype(jnp.float32), (ID_ROWS, known))
    return jnp.dot(
        numbers.astype(jnp.bfloat16),
        matches.astype(jnp.float32).astype(jnp.bfloat16),
        preferred_element_type=jnp.float32,
    )


def attend_kernel(
    block,
    steps,
    lengths_ref,
    me_ref,
    q_hbm,
    k_hbm,
    v_hbm,
    kn_hbm,
    vn_hbm,
    request_hbm,
    adapter_hbm,
    w_ref,
    out_ref,
    first_ref,
    second_ref,
    q_ref,
    k_ref,
    v_ref,
    kn_ref,
    vn_ref,
    request_ref,
    adapter_ref,
    acc_ref,
    buffer_ref,
    new_sem,
    block_sem,
    sem_ref,
):
    rows, heads, width = q_ref.shape
    blocks = rows // block
    piece_refs = (first_ref, second_ref)
    out_local = first_ref.shape[1]
    tiles = out_local // TILE

    def block_copies(i):
        part = pl.ds(pl.multiple_of(i * block, block), block)
        return [
            pltpu.make_async_copy(source.at[part], target.at[part], block_sem.at[j, i])
            for j, (source, target) in enumerate(
                ((q_hbm, q_ref), (k_hbm, k_ref), (v_hbm, v_ref))
            )
        ]

    new_copies = fetch_all(
        (kn_hbm, vn_hbm, request_hbm, adapter_hbm),
        (kn_ref, vn_ref, request_ref, adapter_ref),
        new_sem,
    )

    def begin(i, carry):
        for copy in block_copies(i):
            copy.start()
        return carry

    lax.fori_loop(0, blocks, begin, 0)
    for i, step in enumerate(steps):
        for j in range(tiles):
            column = (me_ref[0] ^ step) * out_local + j * TILE
            fetch(w_ref, buffer_ref, sem_ref, i * tiles + j, column).start()
    for copy in new_copies:
        copy.wait()
    out_ref[pl.ds(rows, ID_ROWS), :] = jnp.zeros((ID_ROWS, out_ref.shape[1]), out_ref.dtype)
    out_ref[pl.ds(rows, ID_ROWS), :rows] = look_up(request_ref[...], adapter_ref[...]).astype(
        out_ref.dtype
    )

    def one_block(i, carry):
        for copy in block_copies(i):
            copy.wait()
        first = pl.multiple_of(i * block, block)
        attend_block(
            [lengths_ref[first + s] for s in range(block)],
            q_ref,
            k_ref,
            v_ref,
            kn_ref,
            vn_ref,
            first,
            acc_ref,
        )
        for h in range(heads):
            out_ref[pl.ds(first, block), h * width : (h + 1) * width] = acc_ref[
                pl.ds(h, block, stride=heads), :
            ].astype(out_ref.dtype)
        return carry

    lax.fori_loop(0, blocks, one_block, 0)
    for i, (step, piece_ref) in enumerate(zip(steps, piece_refs)):
        column = (me_ref[0] ^ step) * out_local
        project_tiles(out_ref, w_ref, buffer_ref, sem_ref, piece_ref, i * tiles, column)


def attend(arrays, lengths, out_weight, me, steps, out_local):
    queries, key_cache = arrays[:2]
    rows, heads, width = queries.shape
    cache = key_cache.shape[2]
    block = min(16, rows)
    depth = heads * width
    tiles = len(steps) * (out_local // TILE)
    smem = pl.BlockSpec(memory_space=pltpu.SMEM)
    hbm = pl.BlockSpec(memory_space=pltpu.HBM)
    vmem = pl.BlockSpec(memory_space=pltpu.VMEM)
    return pl.pallas_call(
        functools.partial(attend_kernel, block, steps),
        in_specs=[smem, smem] + [hbm] * (len(arrays) + 1),
        out_specs=[vmem, vmem, vmem],
        scratch_shapes=[pltpu.VMEM(a.shape, a.dtype) for a in arrays]
        + [
            pltpu.VMEM((block * heads, width), jnp.float32),
            pltpu.VMEM((tiles, depth, TILE), jnp.bfloat16),
            pltpu.SemaphoreType.DMA((4,)),
            pltpu.SemaphoreType.DMA((3, rows // block)),
            pltpu.SemaphoreType.DMA((tiles,)),
        ],
        out_shape=[
            jax.ShapeDtypeStruct((rows + ID_ROWS, depth), jnp.bfloat16),
        ]
        + [jax.ShapeDtypeStruct((rows, out_local), jnp.bfloat16) for _ in steps],
        compiler_params=pltpu.CompilerParams(vmem_limit_bytes=57 * MIB),
        cost_estimate=SMALL,
        name="attend",
    )(lengths, me.reshape(1), *arrays, out_weight)


def masked(low, owner, adapters, ranks, adapters_here):
    terms = jnp.concatenate([low] * adapters_here, axis=0)
    row = lax.broadcasted_iota(jnp.int32, terms.shape, 0)
    return jnp.where(row // ranks + owner * adapters_here == adapters, terms, 0.0)


def block_parts(blocks):
    arrays, places = [], []
    for i, parts in enumerate(blocks):
        first = 0
        for part in parts:
            arrays.append(part)
            places.append((i, first, part.shape[0]))
            first += part.shape[0]
    return arrays, places


def fetch_blocks(sources, places, column, target, sems, offset):
    columns = pl.ds(column, target.shape[2])
    return [
        pltpu.make_async_copy(
            source.at[:, columns], target.at[i, pl.ds(first, count)], sems.at[offset + j]
        )
        for j, (source, (i, first, count)) in enumerate(zip(sources, places))
    ]


def low_kernel(ranks, places, keys, here_ref, *refs):
    sides, sources = refs[:2], refs[2 : 2 + len(places)]
    out_ref, adapters_ref, side_ref, block_ref, sems = refs[2 + len(places) :]
    copies = fetch_all(sides, [side_ref.at[i] for i in range(2)], sems)
    parts = fetch_blocks(sources, places, 0, block_ref, sems, 2)
    for copy in parts:
        copy.start()
    blocks, pair = block_ref.shape[:2]
    rows = side_ref.shape[1] - ID_ROWS
    sides_t, adapters = [], []
    for i, copy in enumerate(copies):
        copy.wait()
        sides_t.append(side_ref[i, :rows].astype(jnp.float32).T.astype(jnp.bfloat16))
        ids = side_ref[i, rows:, :rows].astype(jnp.float32)
        adapters.append(ids[:8].astype(jnp.int32))
    a_t = jnp.concatenate(sides_t, axis=1)
    adapters_ref[...] = jnp.concatenate(adapters, axis=1)
    adapters = adapters_ref[:1, :]
    row = lax.broadcasted_iota(jnp.int32, (pair, a_t.shape[1]), 0)
    total = jnp.zeros(row.shape, jnp.float32)
    for i in range(blocks):
        for copy, place in zip(parts, places):
            if place[0] == i:
                copy.wait()
        part = jnp.dot(block_ref[i], a_t, preferred_element_type=jnp.float32)
        first = (here_ref[0] ^ keys[i]) * (pair // ranks)
        total += jnp.where(row // ranks + first == adapters, part, 0.0)
    low = total[:ranks]
    for a in range(1, pair // ranks):
        low += total[a * ranks : (a + 1) * ranks]
    out_ref[...] = low.astype(out_ref.dtype)


def low_rank(sides, blocks, depth, here, keys, rank):
    rows = sides[0].shape[0] - ID_ROWS
    arrays, places = block_parts(blocks)
    pair = sum(part.shape[0] for part in blocks[0])
    vmem = pl.BlockSpec(memory_space=pltpu.VMEM)
    return pl.pallas_call(
        functools.partial(low_kernel, rank, places, keys),
        in_specs=[pl.BlockSpec(memory_space=pltpu.SMEM)]
        + [pl.BlockSpec(memory_space=pl.ANY)] * (2 + len(arrays)),
        out_specs=[vmem, vmem],
        out_shape=[
            jax.ShapeDtypeStruct((rank, 2 * rows), jnp.bfloat16),
            jax.ShapeDtypeStruct((8, 2 * rows), jnp.int32),
        ],
        scratch_shapes=[
            pltpu.VMEM((2, *sides[0].shape), jnp.bfloat16),
            pltpu.VMEM((len(blocks), pair, depth), jnp.bfloat16),
            pltpu.SemaphoreType.DMA((2 + len(arrays),)),
        ],
        compiler_params=pltpu.CompilerParams(vmem_limit_bytes=16 * MIB),
        cost_estimate=SMALL,
        name="low_rank",
    )(here.reshape(1), *sides, *arrays)


def delta_kernel(ranks, places, column, keys, here_ref, adapters_ref, low_ref, *refs):
    sources = refs[: len(places)]
    mine_ref, other_ref, block_ref, sems = refs[len(places) :]
    parts = fetch_blocks(sources, places, column, block_ref, sems, 0)
    for copy in parts:
        copy.start()
    blocks, pair, width = block_ref.shape
    low = low_ref[...].astype(jnp.float32)
    sides = []
    for i in range(blocks):
        mine = masked(low, here_ref[0] ^ keys[i], adapters_ref[:1, :], ranks, pair // ranks)
        sides.append(mine.T.astype(jnp.bfloat16))
    for copy in parts:
        copy.wait()
    delta = jnp.dot(
        jnp.concatenate(sides, axis=1),
        block_ref[...].reshape(blocks * pair, width),
        preferred_element_type=jnp.float32,
    )
    delta = (0.5 * delta).astype(jnp.bfloat16)
    rows = mine_ref.shape[0]
    mine_ref[...] = delta[:rows]
    other_ref[...] = delta[rows:]


def correct(low, adapters, blocks, column, out_local, here, keys, rank):
    slots = adapters.shape[1]
    arrays, places = block_parts(blocks)
    pair = sum(part.shape[0] for part in blocks[0])
    vmem = pl.BlockSpec(memory_space=pltpu.VMEM)
    out = jax.ShapeDtypeStruct((slots // 2, out_local), jnp.bfloat16)
    return pl.pallas_call(
        functools.partial(delta_kernel, rank, places, column, keys),
        in_specs=[pl.BlockSpec(memory_space=pltpu.SMEM), vmem, vmem]
        + [pl.BlockSpec(memory_space=pl.ANY)] * len(arrays),
        out_specs=[vmem, vmem],
        out_shape=[out, out],
        scratch_shapes=[
            pltpu.VMEM((len(blocks), pair, out_local), jnp.bfloat16),
            pltpu.SemaphoreType.DMA((len(arrays),)),
        ],
        compiler_params=pltpu.CompilerParams(vmem_limit_bytes=16 * MIB),
        cost_estimate=SMALL,
        name="correct",
    )(here.reshape(1), adapters, low, *arrays)


def finish_kernel(occupied_ref, own_ref, *refs):
    *part_refs, out_ref = refs
    rows = out_ref.shape[0]
    live = jnp.broadcast_to(occupied_ref[...].astype(jnp.float32), (128, rows)).T
    for j in range(0, out_ref.shape[1], 128):
        columns = slice(j, j + 128)
        total = own_ref[:, columns]
        for ref in part_refs:
            total += ref[:, columns].astype(jnp.float32)
        out_ref[:, columns] = (live * total).astype(out_ref.dtype)


def finish(own, parts, occupied):
    rows, out_local = own.shape
    vmem = pl.BlockSpec(memory_space=pltpu.VMEM)
    return pl.pallas_call(
        finish_kernel,
        in_specs=[vmem] * (2 + len(parts)),
        out_specs=vmem,
        out_shape=jax.ShapeDtypeStruct((rows, out_local), jnp.bfloat16),
        compiler_params=pltpu.CompilerParams(vmem_limit_bytes=16 * MIB),
        cost_estimate=SMALL,
        name="finish",
    )(occupied.reshape(1, rows), own, *parts)


def exchange(value, axis, step):
    count = lax.axis_size(axis)
    return lax.ppermute(value, axis, [(i, i ^ step) for i in range(count)])


def neighbours():
    return [1 << i for i in range(1, lax.axis_size("dp").bit_length() - 1)]


def near_blocks(own):
    return {0: [own], **{bit: [exchange(own, "dp", bit)] for bit in neighbours()[:2]}}


def far_blocks(blocks):
    blocks = dict(blocks)
    a, b, *others = neighbours()
    half = blocks[0][0].shape[0] // 2
    blocks[a | b] = [
        exchange(blocks[a][0][:half], "dp", b),
        exchange(blocks[b][0][half:], "dp", a),
    ]
    for bit in others:
        for key in list(blocks):
            blocks[key | bit] = [exchange(part, "dp", bit) for part in blocks[key]]
    return blocks


def together(*values):
    return lax.optimization_barrier(values)


def body(
    queries,
    key_cache,
    value_cache,
    key_new,
    value_new,
    lengths,
    occupied,
    slot_request,
    request_adapter,
    out_weight,
    shrink_weight,
    expand_weight,
):
    adapters_here, depth, rank = shrink_weight.shape
    out_local = expand_weight.shape[2]
    shares = lax.axis_size("mp")
    me = lax.axis_index("mp")
    here = lax.axis_index("dp")
    pair = adapters_here * rank

    own_block = jnp.concatenate(
        [
            jnp.swapaxes(shrink_weight, 1, 2).reshape(pair, depth),
            expand_weight.reshape(pair, out_local),
        ],
        axis=1,
    )
    blocks = near_blocks(own_block)
    halved = shares == 4
    early = (3, 1) if halved else (shares - 1, shares - 2)
    late = (2, 0) if halved else tuple(range(shares - 3, -1, -1))
    attended, *pieces = attend(
        (
            queries,
            key_cache,
            value_cache,
            key_new,
            value_new,
            slot_request.reshape(1, -1),
            request_adapter.reshape(1, -1),
        ),
        lengths,
        out_weight,
        me,
        early,
        out_local,
    )
    received = [
        exchange(piece, "mp", 1 if halved else step) for piece, step in zip(pieces, early)
    ]
    blocks, attended = together(blocks, attended)
    blocks = far_blocks(blocks)
    beside = exchange(attended, "dp", 1)
    rows = queries.shape[0]
    *pieces, own = [
        jnp.dot(
            attended[:rows],
            lax.dynamic_slice_in_dim(out_weight, (me ^ step) * out_local, out_local, 1),
            preferred_element_type=jnp.float32,
        )
        for step in late
    ]
    if not halved:
        pieces = [piece.astype(jnp.bfloat16) for piece in pieces]
    if halved:
        passed = received.pop(0)
        passed, attended, own, *pieces = together(passed, attended, own, *pieces)
        pieces = [(pieces[0] + passed.astype(jnp.float32)).astype(jnp.bfloat16)]
    received += [exchange(piece, "mp", step) for piece, step in zip(pieces, late)]

    keys = tuple(blocks)
    blocks = list(blocks.values())
    low, adapters = low_rank([attended, beside], blocks, depth, here, keys, rank)
    lows = [low] + [exchange(low, "mp", step) for step in range(1, shares)]
    lows, received = together(lows, received)
    low = sum(part.astype(jnp.float32) for part in lows).astype(jnp.bfloat16)
    correction, other = correct(low, adapters, blocks, depth, out_local, here, keys, rank)
    return finish(own, [*received, correction, exchange(other, "dp", 1)], occupied)


def solution(mesh):
    placed = (
        P("dp", "mp", None),
        P("dp", "mp", None, None),
        P("dp", "mp", None, None),
        P("dp", "mp", None),
        P("dp", "mp", None),
        P("dp"),
        P("dp"),
        P("dp"),
        P(),
        P("mp", None),
        P("dp", "mp", None),
        P("dp", None, "mp"),
    )
    return jax.shard_map(body, mesh=mesh, in_specs=placed, out_specs=P("dp", "mp"), check_vma=False)
```

```python
import functools
import math

import jax
import jax.numpy as jnp
from jax import lax
from jax.experimental import pallas as pl
from jax.experimental.pallas import tpu as pltpu
from jax.sharding import PartitionSpec as P

MIB = 1024 * 1024
TILE = 256
SMALL = pl.CostEstimate(flops=1, bytes_accessed=1, transcendentals=0)
ID_ROWS = 16


def attend_block(lengths, q_ref, k_ref, v_ref, kn_ref, vn_ref, first, acc_ref):
    slots = len(lengths)
    heads, width = q_ref.shape[1:]
    kv_local, cache = k_ref.shape[1], k_ref.shape[2]
    group = heads // kv_local
    inverse = 1.0 / math.sqrt(width)
    lane = lax.broadcasted_iota(jnp.int32, (group, cache), 1)
    parts = []
    for s in range(slots):
        scores = lax.dot_general(
            q_ref[first + s],
            k_ref[first + s].reshape(kv_local * cache, width),
            (((1,), (1,)), ((), ())),
            preferred_element_type=jnp.float32,
        )
        valid = lane < lengths[s]
        for g in range(kv_local):
            part = scores[g * group : (g + 1) * group, g * cache : (g + 1) * cache]
            parts.append(jnp.where(valid, part * inverse, -jnp.inf))
    cached = jnp.concatenate(parts, axis=0)
    block = pl.ds(first, slots)
    q_all = q_ref[block].astype(jnp.float32).reshape(slots * kv_local, group, width)
    kn = kn_ref[block].astype(jnp.float32).reshape(slots * kv_local, 1, width)
    vn = vn_ref[block].astype(jnp.float32).reshape(slots * kv_local, 1, width)
    fresh = (jnp.sum(q_all * kn, axis=-1, keepdims=True) * inverse).reshape(slots * heads, 1)
    top = jnp.maximum(jnp.max(cached, axis=-1, keepdims=True), fresh)
    cached_exp = jnp.exp(cached - top)
    fresh_exp = jnp.exp(fresh - top)
    scale = 1.0 / (jnp.sum(cached_exp, axis=-1, keepdims=True) + fresh_exp)
    weights = (cached_exp * scale).astype(jnp.bfloat16)
    fresh_w = (fresh_exp * scale).astype(jnp.bfloat16).astype(jnp.float32)
    new_part = (fresh_w.reshape(slots * kv_local, group, 1) * vn).reshape(slots * heads, width)
    for s in range(slots):
        values = jnp.concatenate([v_ref[first + s, g] for g in range(kv_local)], axis=1)
        summed = jnp.dot(
            weights[s * heads : (s + 1) * heads], values, preferred_element_type=jnp.float32
        )
        for g in range(kv_local):
            row = s * heads + g * group
            acc_ref[row : row + group, :] = (
                summed[g * group : (g + 1) * group, g * width : (g + 1) * width]
                + new_part[row : row + group]
            )


def fetch(w_ref, buffer_ref, sem_ref, slot, column):
    return pltpu.make_async_copy(
        w_ref.at[:, pl.ds(pl.multiple_of(column, TILE), TILE)],
        buffer_ref.at[slot],
        sem_ref.at[slot],
    )


def project_tiles(a_ref, w_ref, buffer_ref, sem_ref, out_ref, column):
    tiles = out_ref.shape[1] // TILE

    def tile(j, carry):
        fetch(w_ref, buffer_ref, sem_ref, j, column + j * TILE).wait()
        out_ref[:, pl.ds(pl.multiple_of(j * TILE, TILE), TILE)] = jnp.dot(
            a_ref[: out_ref.shape[0]], buffer_ref[j], preferred_element_type=jnp.float32
        ).astype(out_ref.dtype)
        return carry

    lax.fori_loop(0, tiles, tile, 0)


def fetch_all(sources, targets, sems):
    copies = [
        pltpu.make_async_copy(source, target, sems.at[i])
        for i, (source, target) in enumerate(zip(sources, targets))
    ]
    for copy in copies:
        copy.start()
    return copies


def look_up(requests, adapters):
    slots, known = requests.shape[1], adapters.shape[1]
    matches = lax.broadcasted_iota(jnp.int32, (known, slots), 0) == requests
    numbers = jnp.broadcast_to(adapters.astype(jnp.float32), (ID_ROWS, known))
    return jnp.dot(
        numbers.astype(jnp.bfloat16),
        matches.astype(jnp.float32).astype(jnp.bfloat16),
        preferred_element_type=jnp.float32,
    )


def attend_kernel(
    block,
    step,
    lengths_ref,
    me_ref,
    q_hbm,
    k_hbm,
    v_hbm,
    kn_hbm,
    vn_hbm,
    request_hbm,
    adapter_hbm,
    w_ref,
    out_ref,
    piece_ref,
    q_ref,
    k_ref,
    v_ref,
    kn_ref,
    vn_ref,
    request_ref,
    adapter_ref,
    acc_ref,
    buffer_ref,
    new_sem,
    block_sem,
    sem_ref,
):
    rows, heads, width = q_ref.shape
    blocks = rows // block
    out_local = piece_ref.shape[1]
    tiles = out_local // TILE

    def block_copies(i):
        part = pl.ds(pl.multiple_of(i * block, block), block)
        return [
            pltpu.make_async_copy(source.at[part], target.at[part], block_sem.at[j, i])
            for j, (source, target) in enumerate(
                ((q_hbm, q_ref), (k_hbm, k_ref), (v_hbm, v_ref))
            )
        ]

    new_copies = fetch_all(
        (kn_hbm, vn_hbm, request_hbm, adapter_hbm),
        (kn_ref, vn_ref, request_ref, adapter_ref),
        new_sem,
    )

    def begin(i, carry):
        for copy in block_copies(i):
            copy.start()
        return carry

    lax.fori_loop(0, blocks, begin, 0)
    column = (me_ref[0] ^ step) * out_local
    for j in range(tiles):
        fetch(w_ref, buffer_ref, sem_ref, j, column + j * TILE).start()
    for copy in new_copies:
        copy.wait()
    out_ref[pl.ds(rows, ID_ROWS), :] = jnp.zeros((ID_ROWS, out_ref.shape[1]), out_ref.dtype)
    out_ref[pl.ds(rows, ID_ROWS), :rows] = look_up(request_ref[...], adapter_ref[...]).astype(
        out_ref.dtype
    )

    def one_block(i, carry):
        for copy in block_copies(i):
            copy.wait()
        first = pl.multiple_of(i * block, block)
        attend_block(
            [lengths_ref[first + s] for s in range(block)],
            q_ref,
            k_ref,
            v_ref,
            kn_ref,
            vn_ref,
            first,
            acc_ref,
        )
        for h in range(heads):
            out_ref[pl.ds(first, block), h * width : (h + 1) * width] = acc_ref[
                pl.ds(h, block, stride=heads), :
            ].astype(out_ref.dtype)
        return carry

    lax.fori_loop(0, blocks, one_block, 0)
    project_tiles(out_ref, w_ref, buffer_ref, sem_ref, piece_ref, column)


def attend(arrays, lengths, out_weight, me, step, out_local):
    queries, key_cache = arrays[:2]
    rows, heads, width = queries.shape
    cache = key_cache.shape[2]
    block = min(16, rows)
    depth = heads * width
    tiles = out_local // TILE
    smem = pl.BlockSpec(memory_space=pltpu.SMEM)
    hbm = pl.BlockSpec(memory_space=pltpu.HBM)
    vmem = pl.BlockSpec(memory_space=pltpu.VMEM)
    return pl.pallas_call(
        functools.partial(attend_kernel, block, step),
        in_specs=[smem, smem] + [hbm] * (len(arrays) + 1),
        out_specs=[vmem, vmem],
        scratch_shapes=[pltpu.VMEM(a.shape, a.dtype) for a in arrays]
        + [
            pltpu.VMEM((block * heads, width), jnp.float32),
            pltpu.VMEM((tiles, depth, TILE), jnp.bfloat16),
            pltpu.SemaphoreType.DMA((4,)),
            pltpu.SemaphoreType.DMA((3, rows // block)),
            pltpu.SemaphoreType.DMA((tiles,)),
        ],
        out_shape=[
            jax.ShapeDtypeStruct((rows + ID_ROWS, depth), jnp.bfloat16),
            jax.ShapeDtypeStruct((rows, out_local), jnp.bfloat16),
        ],
        compiler_params=pltpu.CompilerParams(vmem_limit_bytes=57 * MIB),
        cost_estimate=SMALL,
        name="attend",
    )(lengths, me.reshape(1), *arrays, out_weight)


def masked(low, owner, adapters, ranks, adapters_here):
    terms = jnp.concatenate([low] * adapters_here, axis=0)
    row = lax.broadcasted_iota(jnp.int32, terms.shape, 0)
    return jnp.where(row // ranks + owner * adapters_here == adapters, terms, 0.0)


def block_parts(blocks):
    arrays, places = [], []
    for i, parts in enumerate(blocks):
        first = 0
        for part in parts:
            arrays.append(part)
            places.append((i, first, part.shape[0]))
            first += part.shape[0]
    return arrays, places


def fetch_blocks(sources, places, column, target, sems, offset):
    columns = pl.ds(column, target.shape[2])
    return [
        pltpu.make_async_copy(
            source.at[:, columns], target.at[i, pl.ds(first, count)], sems.at[offset + j]
        )
        for j, (source, (i, first, count)) in enumerate(zip(sources, places))
    ]


def low_kernel(ranks, places, keys, here_ref, *refs):
    sides, sources = refs[:2], refs[2 : 2 + len(places)]
    out_ref, adapters_ref, side_ref, block_ref, sems = refs[2 + len(places) :]
    copies = fetch_all(sides, [side_ref.at[i] for i in range(2)], sems)
    parts = fetch_blocks(sources, places, 0, block_ref, sems, 2)
    for copy in parts:
        copy.start()
    blocks, pair = block_ref.shape[:2]
    rows = side_ref.shape[1] - ID_ROWS
    sides_t, adapters = [], []
    for i, copy in enumerate(copies):
        copy.wait()
        sides_t.append(side_ref[i, :rows].astype(jnp.float32).T.astype(jnp.bfloat16))
        ids = side_ref[i, rows:, :rows].astype(jnp.float32)
        adapters.append(ids[:8].astype(jnp.int32))
    a_t = jnp.concatenate(sides_t, axis=1)
    adapters_ref[...] = jnp.concatenate(adapters, axis=1)
    adapters = adapters_ref[:1, :]
    row = lax.broadcasted_iota(jnp.int32, (pair, a_t.shape[1]), 0)
    total = jnp.zeros(row.shape, jnp.float32)
    for i in range(blocks):
        for copy, place in zip(parts, places):
            if place[0] == i:
                copy.wait()
        part = jnp.dot(block_ref[i], a_t, preferred_element_type=jnp.float32)
        first = (here_ref[0] ^ keys[i]) * (pair // ranks)
        total += jnp.where(row // ranks + first == adapters, part, 0.0)
    low = total[:ranks]
    for a in range(1, pair // ranks):
        low += total[a * ranks : (a + 1) * ranks]
    out_ref[...] = low.astype(out_ref.dtype)


def low_rank(sides, blocks, depth, here, keys, rank):
    rows = sides[0].shape[0] - ID_ROWS
    arrays, places = block_parts(blocks)
    pair = sum(part.shape[0] for part in blocks[0])
    vmem = pl.BlockSpec(memory_space=pltpu.VMEM)
    return pl.pallas_call(
        functools.partial(low_kernel, rank, places, keys),
        in_specs=[pl.BlockSpec(memory_space=pltpu.SMEM)]
        + [pl.BlockSpec(memory_space=pl.ANY)] * (2 + len(arrays)),
        out_specs=[vmem, vmem],
        out_shape=[
            jax.ShapeDtypeStruct((rank, 2 * rows), jnp.bfloat16),
            jax.ShapeDtypeStruct((8, 2 * rows), jnp.int32),
        ],
        scratch_shapes=[
            pltpu.VMEM((2, *sides[0].shape), jnp.bfloat16),
            pltpu.VMEM((len(blocks), pair, depth), jnp.bfloat16),
            pltpu.SemaphoreType.DMA((2 + len(arrays),)),
        ],
        compiler_params=pltpu.CompilerParams(vmem_limit_bytes=16 * MIB),
        cost_estimate=SMALL,
        name="low_rank",
    )(here.reshape(1), *sides, *arrays)


def delta_kernel(ranks, places, column, keys, here_ref, adapters_ref, low_ref, *refs):
    sources = refs[: len(places)]
    mine_ref, other_ref, block_ref, sems = refs[len(places) :]
    parts = fetch_blocks(sources, places, column, block_ref, sems, 0)
    for copy in parts:
        copy.start()
    blocks, pair, width = block_ref.shape
    low = low_ref[...].astype(jnp.float32)
    sides = []
    for i in range(blocks):
        mine = masked(low, here_ref[0] ^ keys[i], adapters_ref[:1, :], ranks, pair // ranks)
        sides.append(mine.T.astype(jnp.bfloat16))
    for copy in parts:
        copy.wait()
    delta = jnp.dot(
        jnp.concatenate(sides, axis=1),
        block_ref[...].reshape(blocks * pair, width),
        preferred_element_type=jnp.float32,
    )
    delta = (0.5 * delta).astype(jnp.bfloat16)
    rows = mine_ref.shape[0]
    mine_ref[...] = delta[:rows]
    other_ref[...] = delta[rows:]


def correct(low, adapters, blocks, column, out_local, here, keys, rank):
    slots = adapters.shape[1]
    arrays, places = block_parts(blocks)
    pair = sum(part.shape[0] for part in blocks[0])
    vmem = pl.BlockSpec(memory_space=pltpu.VMEM)
    out = jax.ShapeDtypeStruct((slots // 2, out_local), jnp.bfloat16)
    return pl.pallas_call(
        functools.partial(delta_kernel, rank, places, column, keys),
        in_specs=[pl.BlockSpec(memory_space=pltpu.SMEM), vmem, vmem]
        + [pl.BlockSpec(memory_space=pl.ANY)] * len(arrays),
        out_specs=[vmem, vmem],
        out_shape=[out, out],
        scratch_shapes=[
            pltpu.VMEM((len(blocks), pair, out_local), jnp.bfloat16),
            pltpu.SemaphoreType.DMA((len(arrays),)),
        ],
        compiler_params=pltpu.CompilerParams(vmem_limit_bytes=16 * MIB),
        cost_estimate=SMALL,
        name="correct",
    )(here.reshape(1), adapters, low, *arrays)


def finish_kernel(occupied_ref, own_ref, *refs):
    *part_refs, out_ref = refs
    rows = out_ref.shape[0]
    live = jnp.broadcast_to(occupied_ref[...].astype(jnp.float32), (128, rows)).T
    for j in range(0, out_ref.shape[1], 128):
        columns = slice(j, j + 128)
        total = own_ref[:, columns]
        for ref in part_refs:
            total += ref[:, columns].astype(jnp.float32)
        out_ref[:, columns] = (live * total).astype(out_ref.dtype)


def finish(own, parts, occupied):
    rows, out_local = own.shape
    vmem = pl.BlockSpec(memory_space=pltpu.VMEM)
    return pl.pallas_call(
        finish_kernel,
        in_specs=[vmem] * (2 + len(parts)),
        out_specs=vmem,
        out_shape=jax.ShapeDtypeStruct((rows, out_local), jnp.bfloat16),
        compiler_params=pltpu.CompilerParams(vmem_limit_bytes=16 * MIB),
        cost_estimate=SMALL,
        name="finish",
    )(occupied.reshape(1, rows), own, *parts)


def exchange(value, axis, step):
    count = lax.axis_size(axis)
    return lax.ppermute(value, axis, [(i, i ^ step) for i in range(count)])


def neighbours():
    return [1 << i for i in range(1, lax.axis_size("dp").bit_length() - 1)]


def near_blocks(own):
    return {0: [own], **{bit: [exchange(own, "dp", bit)] for bit in neighbours()[:2]}}


def farther_blocks(blocks):
    for bit in neighbours()[2:]:
        for key in list(blocks):
            blocks[key | bit] = [exchange(part, "dp", bit) for part in blocks[key]]
    return blocks


def forwarded_blocks(blocks):
    a, b = neighbours()[:2]
    half = blocks[0][0].shape[0] // 2
    diagonal = [
        exchange(blocks[a][0][:half], "dp", b),
        exchange(blocks[b][0][half:], "dp", a),
    ]
    return farther_blocks({**blocks, a | b: diagonal})


def together(*values):
    return lax.optimization_barrier(values)


def body(
    queries,
    key_cache,
    value_cache,
    key_new,
    value_new,
    lengths,
    occupied,
    slot_request,
    request_adapter,
    out_weight,
    shrink_weight,
    expand_weight,
):
    adapters_here, depth, rank = shrink_weight.shape
    out_local = expand_weight.shape[2]
    shares = lax.axis_size("mp")
    me = lax.axis_index("mp")
    here = lax.axis_index("dp")
    pair = adapters_here * rank

    shrink = near_blocks(jnp.swapaxes(shrink_weight, 1, 2).reshape(pair, depth))
    expand = expand_weight.reshape(pair, out_local)

    halved = shares == 4
    attended, piece = attend(
        (
            queries,
            key_cache,
            value_cache,
            key_new,
            value_new,
            slot_request.reshape(1, -1),
            request_adapter.reshape(1, -1),
        ),
        lengths,
        out_weight,
        me,
        shares - 1,
        out_local,
    )
    passed = exchange(piece, "mp", 1 if halved else shares - 1)
    shrink, attended = together(shrink, attended)
    shrink = forwarded_blocks(shrink)
    beside = exchange(attended, "dp", 1)

    def chunk(rows, step, dtype):
        columns = lax.dynamic_slice_in_dim(out_weight, (me ^ step) * out_local, out_local, 1)
        return jnp.dot(
            rows[: queries.shape[0]], columns, preferred_element_type=jnp.float32
        ).astype(dtype)

    pieces = {step: chunk(attended, step, jnp.bfloat16) for step in range(shares - 2, 0, -1)}
    pieces, passed, attended, shrink, expand = together(
        pieces, passed, attended, shrink, expand
    )
    expand = near_blocks(expand)
    if halved:
        received = []
        pieces[2] = (pieces[2].astype(jnp.float32) + passed.astype(jnp.float32)).astype(
            jnp.bfloat16
        )
    else:
        received = [passed]
    received += [exchange(piece, "mp", step) for step, piece in pieces.items()]

    keys = tuple(shrink)
    low, adapters = low_rank(
        [attended, beside], list(shrink.values()), depth, here, keys, rank
    )
    expand, low = together(expand, low)
    expand = forwarded_blocks(expand)
    attended, low = together(attended, low)
    own = chunk(attended, 0, jnp.float32)
    step = 1
    while step < shares:
        arrived = exchange(low, "mp", step)
        low = (low.astype(jnp.float32) + arrived.astype(jnp.float32)).astype(jnp.bfloat16)
        step *= 2
    blocks = [expand[key] for key in keys]
    correction, other = correct(low, adapters, blocks, 0, out_local, here, keys, rank)
    return finish(own, [*received, correction, exchange(other, "dp", 1)], occupied)


def solution(mesh):
    placed = (
        P("dp", "mp", None),
        P("dp", "mp", None, None),
        P("dp", "mp", None, None),
        P("dp", "mp", None),
        P("dp", "mp", None),
        P("dp"),
        P("dp"),
        P("dp"),
        P(),
        P("mp", None),
        P("dp", "mp", None),
        P("dp", None, "mp"),
    )
    return jax.shard_map(body, mesh=mesh, in_specs=placed, out_specs=P("dp", "mp"), check_vma=False)
```

```python
import functools
import math

import jax
import jax.numpy as jnp
from jax import lax
from jax.experimental import pallas as pl
from jax.experimental.pallas import tpu as pltpu
from jax.sharding import PartitionSpec as P

MIB = 1024 * 1024
TILE = 256
SMALL = pl.CostEstimate(flops=1, bytes_accessed=1, transcendentals=0)
ID_ROWS = 16


def attend_block(lengths, q_ref, k_ref, v_ref, kn_ref, vn_ref, first, acc_ref):
    slots = len(lengths)
    heads, width = q_ref.shape[1:]
    kv_local, cache = k_ref.shape[1], k_ref.shape[2]
    group = heads // kv_local
    inverse = 1.0 / math.sqrt(width)
    lane = lax.broadcasted_iota(jnp.int32, (group, cache), 1)
    parts = []
    for s in range(slots):
        scores = lax.dot_general(
            q_ref[first + s],
            k_ref[first + s].reshape(kv_local * cache, width),
            (((1,), (1,)), ((), ())),
            preferred_element_type=jnp.float32,
        )
        valid = lane < lengths[s]
        for g in range(kv_local):
            part = scores[g * group : (g + 1) * group, g * cache : (g + 1) * cache]
            parts.append(jnp.where(valid, part * inverse, -jnp.inf))
    cached = jnp.concatenate(parts, axis=0)
    block = pl.ds(first, slots)
    q_all = q_ref[block].astype(jnp.float32).reshape(slots * kv_local, group, width)
    kn = kn_ref[block].astype(jnp.float32).reshape(slots * kv_local, 1, width)
    vn = vn_ref[block].astype(jnp.float32).reshape(slots * kv_local, 1, width)
    fresh = (jnp.sum(q_all * kn, axis=-1, keepdims=True) * inverse).reshape(slots * heads, 1)
    top = jnp.maximum(jnp.max(cached, axis=-1, keepdims=True), fresh)
    cached_exp = jnp.exp(cached - top)
    fresh_exp = jnp.exp(fresh - top)
    scale = 1.0 / (jnp.sum(cached_exp, axis=-1, keepdims=True) + fresh_exp)
    weights = (cached_exp * scale).astype(jnp.bfloat16)
    fresh_w = (fresh_exp * scale).astype(jnp.bfloat16).astype(jnp.float32)
    new_part = (fresh_w.reshape(slots * kv_local, group, 1) * vn).reshape(slots * heads, width)
    for s in range(slots):
        values = jnp.concatenate([v_ref[first + s, g] for g in range(kv_local)], axis=1)
        summed = jnp.dot(
            weights[s * heads : (s + 1) * heads], values, preferred_element_type=jnp.float32
        )
        for g in range(kv_local):
            row = s * heads + g * group
            acc_ref[row : row + group, :] = (
                summed[g * group : (g + 1) * group, g * width : (g + 1) * width]
                + new_part[row : row + group]
            )


def fetch(w_ref, buffer_ref, sem_ref, slot, column):
    return pltpu.make_async_copy(
        w_ref.at[:, pl.ds(pl.multiple_of(column, TILE), TILE)],
        buffer_ref.at[slot],
        sem_ref.at[slot],
    )


def project_tiles(
    a_ref, w_ref, buffer_ref, sem_ref, out_ref, tiles, first_slot, column, out_column
):
    def tile(j, carry):
        slot = first_slot + j
        fetch(w_ref, buffer_ref, sem_ref, slot, column + j * TILE).wait()
        out_ref[:, pl.ds(pl.multiple_of(out_column + j * TILE, TILE), TILE)] = jnp.dot(
            a_ref[: out_ref.shape[0]], buffer_ref[slot], preferred_element_type=jnp.float32
        ).astype(out_ref.dtype)
        return carry

    lax.fori_loop(0, tiles, tile, 0)


def fetch_all(sources, targets, sems):
    copies = [
        pltpu.make_async_copy(source, target, sems.at[i])
        for i, (source, target) in enumerate(zip(sources, targets))
    ]
    for copy in copies:
        copy.start()
    return copies


def look_up(requests, adapters):
    slots, known = requests.shape[1], adapters.shape[1]
    matches = lax.broadcasted_iota(jnp.int32, (known, slots), 0) == requests
    numbers = jnp.broadcast_to(adapters.astype(jnp.float32), (ID_ROWS, known))
    return jnp.dot(
        numbers.astype(jnp.bfloat16),
        matches.astype(jnp.float32).astype(jnp.bfloat16),
        preferred_element_type=jnp.float32,
    )


def attend_kernel(
    block,
    steps,
    lengths_ref,
    me_ref,
    q_hbm,
    k_hbm,
    v_hbm,
    kn_hbm,
    vn_hbm,
    request_hbm,
    adapter_hbm,
    w_ref,
    out_ref,
    piece_ref,
    q_ref,
    k_ref,
    v_ref,
    kn_ref,
    vn_ref,
    request_ref,
    adapter_ref,
    acc_ref,
    buffer_ref,
    new_sem,
    block_sem,
    sem_ref,
):
    rows, heads, width = q_ref.shape
    blocks = rows // block
    out_local = piece_ref.shape[1] // len(steps)
    tiles = out_local // TILE

    def block_copies(i):
        part = pl.ds(pl.multiple_of(i * block, block), block)
        return [
            pltpu.make_async_copy(source.at[part], target.at[part], block_sem.at[j, i])
            for j, (source, target) in enumerate(
                ((q_hbm, q_ref), (k_hbm, k_ref), (v_hbm, v_ref))
            )
        ]

    new_copies = fetch_all(
        (kn_hbm, vn_hbm, request_hbm, adapter_hbm),
        (kn_ref, vn_ref, request_ref, adapter_ref),
        new_sem,
    )

    def begin(i, carry):
        for copy in block_copies(i):
            copy.start()
        return carry

    lax.fori_loop(0, blocks, begin, 0)
    columns = [(me_ref[0] ^ step) * out_local for step in steps]
    for i, column in enumerate(columns):
        for j in range(tiles):
            fetch(w_ref, buffer_ref, sem_ref, i * tiles + j, column + j * TILE).start()
    for copy in new_copies:
        copy.wait()
    out_ref[pl.ds(rows, ID_ROWS), :] = jnp.zeros((ID_ROWS, out_ref.shape[1]), out_ref.dtype)
    out_ref[pl.ds(rows, ID_ROWS), :rows] = look_up(request_ref[...], adapter_ref[...]).astype(
        out_ref.dtype
    )

    def one_block(i, carry):
        for copy in block_copies(i):
            copy.wait()
        first = pl.multiple_of(i * block, block)
        attend_block(
            [lengths_ref[first + s] for s in range(block)],
            q_ref,
            k_ref,
            v_ref,
            kn_ref,
            vn_ref,
            first,
            acc_ref,
        )
        for h in range(heads):
            out_ref[pl.ds(first, block), h * width : (h + 1) * width] = acc_ref[
                pl.ds(h, block, stride=heads), :
            ].astype(out_ref.dtype)
        return carry

    lax.fori_loop(0, blocks, one_block, 0)
    for i, column in enumerate(columns):
        project_tiles(
            out_ref, w_ref, buffer_ref, sem_ref, piece_ref, tiles, i * tiles, column, i * out_local
        )


def attend(arrays, lengths, out_weight, me, steps, out_local):
    queries, key_cache = arrays[:2]
    rows, heads, width = queries.shape
    cache = key_cache.shape[2]
    block = min(16, rows)
    depth = heads * width
    tiles = len(steps) * (out_local // TILE)
    smem = pl.BlockSpec(memory_space=pltpu.SMEM)
    hbm = pl.BlockSpec(memory_space=pltpu.HBM)
    vmem = pl.BlockSpec(memory_space=pltpu.VMEM)
    return pl.pallas_call(
        functools.partial(attend_kernel, block, steps),
        in_specs=[smem, smem] + [hbm] * (len(arrays) + 1),
        out_specs=[vmem, vmem],
        scratch_shapes=[pltpu.VMEM(a.shape, a.dtype) for a in arrays]
        + [
            pltpu.VMEM((block * heads, width), jnp.float32),
            pltpu.VMEM((tiles, depth, TILE), jnp.bfloat16),
            pltpu.SemaphoreType.DMA((4,)),
            pltpu.SemaphoreType.DMA((3, rows // block)),
            pltpu.SemaphoreType.DMA((tiles,)),
        ],
        out_shape=[
            jax.ShapeDtypeStruct((rows + ID_ROWS, depth), jnp.bfloat16),
            jax.ShapeDtypeStruct((rows, len(steps) * out_local), jnp.bfloat16),
        ],
        compiler_params=pltpu.CompilerParams(vmem_limit_bytes=57 * MIB),
        cost_estimate=SMALL,
        name="attend",
    )(lengths, me.reshape(1), *arrays, out_weight)


def project_kernel(steps, me_ref, a_hbm, w_ref, *refs):
    *out_refs, a_ref, buffer_ref, a_sem, sem_ref = refs
    out_local = out_refs[0].shape[1]
    tiles = out_local // TILE
    copy = pltpu.make_async_copy(a_hbm, a_ref, a_sem.at[0])
    copy.start()
    for i, step in enumerate(steps):
        for j in range(tiles):
            column = (me_ref[0] ^ step) * out_local + j * TILE
            fetch(w_ref, buffer_ref, sem_ref, i * tiles + j, column).start()
    copy.wait()
    for i, (step, out_ref) in enumerate(zip(steps, out_refs)):
        column = (me_ref[0] ^ step) * out_local
        project_tiles(a_ref, w_ref, buffer_ref, sem_ref, out_ref, tiles, i * tiles, column, 0)


def project(attended, out_weight, me, steps, out_local, dtypes):
    rows, depth = attended.shape[0] - ID_ROWS, attended.shape[1]
    slots = len(dtypes) * (out_local // TILE)
    vmem = pl.BlockSpec(memory_space=pltpu.VMEM)
    hbm = pl.BlockSpec(memory_space=pl.ANY)
    return pl.pallas_call(
        functools.partial(project_kernel, steps),
        in_specs=[pl.BlockSpec(memory_space=pltpu.SMEM), hbm, hbm],
        out_specs=[vmem for _ in dtypes],
        scratch_shapes=[
            pltpu.VMEM(attended.shape, attended.dtype),
            pltpu.VMEM((slots, depth, TILE), jnp.bfloat16),
            pltpu.SemaphoreType.DMA((1,)),
            pltpu.SemaphoreType.DMA((slots,)),
        ],
        out_shape=[jax.ShapeDtypeStruct((rows, out_local), dtype) for dtype in dtypes],
        compiler_params=pltpu.CompilerParams(vmem_limit_bytes=40 * MIB),
        cost_estimate=SMALL,
        name="project",
    )(me.reshape(1), attended, out_weight)


def masked(low, owner, adapters, ranks, adapters_here):
    terms = jnp.concatenate([low] * adapters_here, axis=0)
    row = lax.broadcasted_iota(jnp.int32, terms.shape, 0)
    return jnp.where(row // ranks + owner * adapters_here == adapters, terms, 0.0)


def block_parts(blocks):
    arrays, places = [], []
    for i, parts in enumerate(blocks):
        first = 0
        for part in parts:
            arrays.append(part)
            places.append((i, first, part.shape[0]))
            first += part.shape[0]
    return arrays, places


def fetch_blocks(sources, places, column, target, sems, offset):
    columns = pl.ds(column, target.shape[2])
    return [
        pltpu.make_async_copy(
            source.at[:, columns], target.at[i, pl.ds(first, count)], sems.at[offset + j]
        )
        for j, (source, (i, first, count)) in enumerate(zip(sources, places))
    ]


def low_kernel(ranks, places, keys, here_ref, *refs):
    sides, sources = refs[:2], refs[2 : 2 + len(places)]
    out_ref, adapters_ref, side_ref, block_ref, sems = refs[2 + len(places) :]
    copies = fetch_all(sides, [side_ref.at[i] for i in range(2)], sems)
    parts = fetch_blocks(sources, places, 0, block_ref, sems, 2)
    for copy in parts:
        copy.start()
    blocks, pair = block_ref.shape[:2]
    rows = side_ref.shape[1] - ID_ROWS
    sides_t, adapters = [], []
    for i, copy in enumerate(copies):
        copy.wait()
        sides_t.append(side_ref[i, :rows].astype(jnp.float32).T.astype(jnp.bfloat16))
        ids = side_ref[i, rows:, :rows].astype(jnp.float32)
        adapters.append(ids[:8].astype(jnp.int32))
    a_t = jnp.concatenate(sides_t, axis=1)
    adapters_ref[...] = jnp.concatenate(adapters, axis=1)
    adapters = adapters_ref[:1, :]
    row = lax.broadcasted_iota(jnp.int32, (pair, a_t.shape[1]), 0)
    total = jnp.zeros(row.shape, jnp.float32)
    for i in range(blocks):
        for copy, place in zip(parts, places):
            if place[0] == i:
                copy.wait()
        part = jnp.dot(block_ref[i], a_t, preferred_element_type=jnp.float32)
        first = (here_ref[0] ^ keys[i]) * (pair // ranks)
        total += jnp.where(row // ranks + first == adapters, part, 0.0)
    low = total[:ranks]
    for a in range(1, pair // ranks):
        low += total[a * ranks : (a + 1) * ranks]
    out_ref[...] = low.astype(out_ref.dtype)


def low_rank(sides, blocks, depth, here, keys, rank):
    rows = sides[0].shape[0] - ID_ROWS
    arrays, places = block_parts(blocks)
    pair = sum(part.shape[0] for part in blocks[0])
    vmem = pl.BlockSpec(memory_space=pltpu.VMEM)
    return pl.pallas_call(
        functools.partial(low_kernel, rank, places, keys),
        in_specs=[pl.BlockSpec(memory_space=pltpu.SMEM)]
        + [pl.BlockSpec(memory_space=pl.ANY)] * (2 + len(arrays)),
        out_specs=[vmem, vmem],
        out_shape=[
            jax.ShapeDtypeStruct((rank, 2 * rows), jnp.bfloat16),
            jax.ShapeDtypeStruct((8, 2 * rows), jnp.int32),
        ],
        scratch_shapes=[
            pltpu.VMEM((2, *sides[0].shape), jnp.bfloat16),
            pltpu.VMEM((len(blocks), pair, depth), jnp.bfloat16),
            pltpu.SemaphoreType.DMA((2 + len(arrays),)),
        ],
        compiler_params=pltpu.CompilerParams(vmem_limit_bytes=16 * MIB),
        cost_estimate=SMALL,
        name="low_rank",
    )(here.reshape(1), *sides, *arrays)


def delta_kernel(ranks, places, column, keys, here_ref, adapters_ref, low_ref, *refs):
    sources = refs[: len(places)]
    mine_ref, other_ref, block_ref, sems = refs[len(places) :]
    parts = fetch_blocks(sources, places, column, block_ref, sems, 0)
    for copy in parts:
        copy.start()
    blocks, pair, width = block_ref.shape
    low = low_ref[...].astype(jnp.float32)
    sides = []
    for i in range(blocks):
        mine = masked(low, here_ref[0] ^ keys[i], adapters_ref[:1, :], ranks, pair // ranks)
        sides.append(mine.T.astype(jnp.bfloat16))
    for copy in parts:
        copy.wait()
    delta = jnp.dot(
        jnp.concatenate(sides, axis=1),
        block_ref[...].reshape(blocks * pair, width),
        preferred_element_type=jnp.float32,
    )
    delta = (0.5 * delta).astype(jnp.bfloat16)
    rows = mine_ref.shape[0]
    mine_ref[...] = delta[:rows]
    other_ref[...] = delta[rows:]


def correct(low, adapters, blocks, column, out_local, here, keys, rank):
    slots = adapters.shape[1]
    arrays, places = block_parts(blocks)
    pair = sum(part.shape[0] for part in blocks[0])
    vmem = pl.BlockSpec(memory_space=pltpu.VMEM)
    out = jax.ShapeDtypeStruct((slots // 2, out_local), jnp.bfloat16)
    return pl.pallas_call(
        functools.partial(delta_kernel, rank, places, column, keys),
        in_specs=[pl.BlockSpec(memory_space=pltpu.SMEM), vmem, vmem]
        + [pl.BlockSpec(memory_space=pl.ANY)] * len(arrays),
        out_specs=[vmem, vmem],
        out_shape=[out, out],
        scratch_shapes=[
            pltpu.VMEM((len(blocks), pair, out_local), jnp.bfloat16),
            pltpu.SemaphoreType.DMA((len(arrays),)),
        ],
        compiler_params=pltpu.CompilerParams(vmem_limit_bytes=16 * MIB),
        cost_estimate=SMALL,
        name="correct",
    )(here.reshape(1), adapters, low, *arrays)


def finish_kernel(occupied_ref, own_ref, *refs):
    *part_refs, out_ref = refs
    rows = out_ref.shape[0]
    live = jnp.broadcast_to(occupied_ref[...].astype(jnp.float32), (128, rows)).T
    for j in range(0, out_ref.shape[1], 128):
        columns = slice(j, j + 128)
        total = own_ref[:, columns]
        for ref in part_refs:
            first = ref.shape[1] - out_ref.shape[1] + j
            total += ref[:, first : first + 128].astype(jnp.float32)
        out_ref[:, columns] = (live * total).astype(out_ref.dtype)


def finish(own, parts, occupied):
    rows, out_local = own.shape
    vmem = pl.BlockSpec(memory_space=pltpu.VMEM)
    return pl.pallas_call(
        finish_kernel,
        in_specs=[vmem] * (2 + len(parts)),
        out_specs=vmem,
        out_shape=jax.ShapeDtypeStruct((rows, out_local), jnp.bfloat16),
        compiler_params=pltpu.CompilerParams(vmem_limit_bytes=16 * MIB),
        cost_estimate=SMALL,
        name="finish",
    )(occupied.reshape(1, rows), own, *parts)


def exchange(value, axis, step):
    count = lax.axis_size(axis)
    return lax.ppermute(value, axis, [(i, i ^ step) for i in range(count)])


def neighbours():
    return [1 << i for i in range(1, lax.axis_size("dp").bit_length() - 1)]


def near_blocks(own):
    return {0: [own], **{bit: [exchange(own, "dp", bit)] for bit in neighbours()[:2]}}


def farther_blocks(blocks):
    for bit in neighbours()[2:]:
        for key in list(blocks):
            blocks[key | bit] = [exchange(part, "dp", bit) for part in blocks[key]]
    return blocks


def forwarded_blocks(blocks):
    a, b = neighbours()[:2]
    half = blocks[0][0].shape[0] // 2
    diagonal = [
        exchange(blocks[a][0][:half], "dp", b),
        exchange(blocks[b][0][half:], "dp", a),
    ]
    return farther_blocks({**blocks, a | b: diagonal})


def direct_blocks(own):
    a, b = neighbours()[:2]
    return farther_blocks({**near_blocks(own), a | b: [exchange(own, "dp", a | b)]})


def together(*values):
    return lax.optimization_barrier(values)


def body(
    queries,
    key_cache,
    value_cache,
    key_new,
    value_new,
    lengths,
    occupied,
    slot_request,
    request_adapter,
    out_weight,
    shrink_weight,
    expand_weight,
):
    adapters_here, depth, rank = shrink_weight.shape
    out_local = expand_weight.shape[2]
    shares = lax.axis_size("mp")
    me = lax.axis_index("mp")
    here = lax.axis_index("dp")
    pair = adapters_here * rank

    shrink = near_blocks(jnp.swapaxes(shrink_weight, 1, 2).reshape(pair, depth))
    expand = expand_weight.reshape(pair, out_local)

    halved = shares == 4
    early = (3, 1) if halved else (shares - 1, shares - 2)
    late = (2, 0) if halved else tuple(range(shares - 3, -1, -1))
    attended, piece = attend(
        (
            queries,
            key_cache,
            value_cache,
            key_new,
            value_new,
            slot_request.reshape(1, -1),
            request_adapter.reshape(1, -1),
        ),
        lengths,
        out_weight,
        me,
        early,
        out_local,
    )
    if halved:
        received = [exchange(piece, "mp", 1)]
    else:
        received = [
            exchange(part, "mp", step) for part, step in zip(jnp.split(piece, 2, 1), early)
        ]
    shrink, attended = together(shrink, attended)
    shrink = forwarded_blocks(shrink)
    beside = exchange(attended, "dp", 1)
    *pieces, own = project(
        attended,
        out_weight,
        me,
        late,
        out_local,
        [jnp.float32 if halved else jnp.bfloat16] * (len(late) - 1) + [jnp.float32],
    )
    pieces, own, received, attended, shrink, expand = together(
        pieces, own, received, attended, shrink, expand
    )
    expand = direct_blocks(expand)
    if halved:
        passed = received[0][:, :out_local].astype(jnp.float32)
        pieces = [(pieces[0] + passed).astype(jnp.bfloat16)]
    last = [exchange(part, "mp", step) for part, step in zip(pieces, late)]

    keys = tuple(shrink)
    low, adapters = low_rank(
        [attended, beside], list(shrink.values()), depth, here, keys, rank
    )
    step = 1
    while step < shares:
        arrived = exchange(low, "mp", step)
        low = (low.astype(jnp.float32) + arrived.astype(jnp.float32)).astype(jnp.bfloat16)
        step *= 2
    low, last = together(low, last)
    blocks = [expand[key] for key in keys]
    correction, other = correct(low, adapters, blocks, 0, out_local, here, keys, rank)
    parts = [*received, *last, correction, exchange(other, "dp", 1)]
    return finish(own, parts, occupied)


def solution(mesh):
    placed = (
        P("dp", "mp", None),
        P("dp", "mp", None, None),
        P("dp", "mp", None, None),
        P("dp", "mp", None),
        P("dp", "mp", None),
        P("dp"),
        P("dp"),
        P("dp"),
        P(),
        P("mp", None),
        P("dp", "mp", None),
        P("dp", None, "mp"),
    )
    return jax.shard_map(body, mesh=mesh, in_specs=placed, out_specs=P("dp", "mp"), check_vma=False)
```

```python
import functools
import math

import jax
import jax.numpy as jnp
from jax import lax
from jax.experimental import pallas as pl
from jax.experimental.pallas import tpu as pltpu
from jax.sharding import PartitionSpec as P

MIB = 1024 * 1024
TILE = 256
SMALL = pl.CostEstimate(flops=1, bytes_accessed=1, transcendentals=0)
ID_ROWS = 16


def attend_block(lengths, q_ref, k_ref, v_ref, kn_ref, vn_ref, first, acc_ref):
    slots = len(lengths)
    heads, width = q_ref.shape[1:]
    kv_local, cache = k_ref.shape[1], k_ref.shape[2]
    group = heads // kv_local
    inverse = 1.0 / math.sqrt(width)
    lane = lax.broadcasted_iota(jnp.int32, (group, cache), 1)
    parts = []
    for s in range(slots):
        scores = lax.dot_general(
            q_ref[first + s],
            k_ref[first + s].reshape(kv_local * cache, width),
            (((1,), (1,)), ((), ())),
            preferred_element_type=jnp.float32,
        )
        valid = lane < lengths[s]
        for g in range(kv_local):
            part = scores[g * group : (g + 1) * group, g * cache : (g + 1) * cache]
            parts.append(jnp.where(valid, part * inverse, -jnp.inf))
    cached = jnp.concatenate(parts, axis=0)
    block = pl.ds(first, slots)
    q_all = q_ref[block].astype(jnp.float32).reshape(slots * kv_local, group, width)
    kn = kn_ref[block].astype(jnp.float32).reshape(slots * kv_local, 1, width)
    vn = vn_ref[block].astype(jnp.float32).reshape(slots * kv_local, 1, width)
    fresh = (jnp.sum(q_all * kn, axis=-1, keepdims=True) * inverse).reshape(slots * heads, 1)
    top = jnp.maximum(jnp.max(cached, axis=-1, keepdims=True), fresh)
    cached_exp = jnp.exp(cached - top)
    fresh_exp = jnp.exp(fresh - top)
    scale = 1.0 / (jnp.sum(cached_exp, axis=-1, keepdims=True) + fresh_exp)
    weights = (cached_exp * scale).astype(jnp.bfloat16)
    fresh_w = (fresh_exp * scale).astype(jnp.bfloat16).astype(jnp.float32)
    new_part = (fresh_w.reshape(slots * kv_local, group, 1) * vn).reshape(slots * heads, width)
    for s in range(slots):
        values = jnp.concatenate([v_ref[first + s, g] for g in range(kv_local)], axis=1)
        summed = jnp.dot(
            weights[s * heads : (s + 1) * heads], values, preferred_element_type=jnp.float32
        )
        for g in range(kv_local):
            row = s * heads + g * group
            acc_ref[row : row + group, :] = (
                summed[g * group : (g + 1) * group, g * width : (g + 1) * width]
                + new_part[row : row + group]
            )


def fetch(w_ref, buffer_ref, sem_ref, slot, column):
    return pltpu.make_async_copy(
        w_ref.at[:, pl.ds(pl.multiple_of(column, TILE), TILE)],
        buffer_ref.at[slot],
        sem_ref.at[slot],
    )


def project_tiles(a_ref, w_ref, buffer_ref, sem_ref, out_ref, tiles, first_slot, column):
    def tile(j, carry):
        slot = first_slot + j
        fetch(w_ref, buffer_ref, sem_ref, slot, column + j * TILE).wait()
        out_ref[:, pl.ds(pl.multiple_of(j * TILE, TILE), TILE)] = jnp.dot(
            a_ref[: out_ref.shape[0]], buffer_ref[slot], preferred_element_type=jnp.float32
        ).astype(out_ref.dtype)
        return carry

    lax.fori_loop(0, tiles, tile, 0)


def fetch_all(sources, targets, sems):
    copies = [
        pltpu.make_async_copy(source, target, sems.at[i])
        for i, (source, target) in enumerate(zip(sources, targets))
    ]
    for copy in copies:
        copy.start()
    return copies


def look_up(requests, adapters):
    slots, known = requests.shape[1], adapters.shape[1]
    matches = lax.broadcasted_iota(jnp.int32, (known, slots), 0) == requests
    numbers = jnp.broadcast_to(adapters.astype(jnp.float32), (ID_ROWS, known))
    return jnp.dot(
        numbers.astype(jnp.bfloat16),
        matches.astype(jnp.float32).astype(jnp.bfloat16),
        preferred_element_type=jnp.float32,
    )


def attend_kernel(
    block,
    steps,
    lengths_ref,
    me_ref,
    q_hbm,
    k_hbm,
    v_hbm,
    kn_hbm,
    vn_hbm,
    request_hbm,
    adapter_hbm,
    w_ref,
    out_ref,
    first_ref,
    second_ref,
    q_ref,
    k_ref,
    v_ref,
    kn_ref,
    vn_ref,
    request_ref,
    adapter_ref,
    acc_ref,
    buffer_ref,
    new_sem,
    block_sem,
    sem_ref,
):
    rows, heads, width = q_ref.shape
    blocks = rows // block
    out_local = first_ref.shape[1]
    tiles = out_local // TILE

    def block_copies(i):
        part = pl.ds(pl.multiple_of(i * block, block), block)
        return [
            pltpu.make_async_copy(source.at[part], target.at[part], block_sem.at[j, i])
            for j, (source, target) in enumerate(
                ((q_hbm, q_ref), (k_hbm, k_ref), (v_hbm, v_ref))
            )
        ]

    new_copies = fetch_all(
        (kn_hbm, vn_hbm, request_hbm, adapter_hbm),
        (kn_ref, vn_ref, request_ref, adapter_ref),
        new_sem,
    )

    def begin(i, carry):
        for copy in block_copies(i):
            copy.start()
        return carry

    lax.fori_loop(0, blocks, begin, 0)
    columns = [(me_ref[0] ^ step) * out_local for step in steps]
    for i, column in enumerate(columns):
        for j in range(tiles):
            fetch(w_ref, buffer_ref, sem_ref, i * tiles + j, column + j * TILE).start()
    for copy in new_copies:
        copy.wait()
    out_ref[pl.ds(rows, ID_ROWS), :] = jnp.zeros((ID_ROWS, out_ref.shape[1]), out_ref.dtype)
    out_ref[pl.ds(rows, ID_ROWS), :rows] = look_up(request_ref[...], adapter_ref[...]).astype(
        out_ref.dtype
    )

    def one_block(i, carry):
        for copy in block_copies(i):
            copy.wait()
        first = pl.multiple_of(i * block, block)
        attend_block(
            [lengths_ref[first + s] for s in range(block)],
            q_ref,
            k_ref,
            v_ref,
            kn_ref,
            vn_ref,
            first,
            acc_ref,
        )
        for h in range(heads):
            out_ref[pl.ds(first, block), h * width : (h + 1) * width] = acc_ref[
                pl.ds(h, block, stride=heads), :
            ].astype(out_ref.dtype)
        return carry

    lax.fori_loop(0, blocks, one_block, 0)
    for i, (column, piece_ref) in enumerate(zip(columns, (first_ref, second_ref))):
        project_tiles(out_ref, w_ref, buffer_ref, sem_ref, piece_ref, tiles, i * tiles, column)


def attend(arrays, lengths, out_weight, me, steps, out_local):
    queries, key_cache = arrays[:2]
    rows, heads, width = queries.shape
    cache = key_cache.shape[2]
    block = min(16, rows)
    depth = heads * width
    tiles = len(steps) * (out_local // TILE)
    smem = pl.BlockSpec(memory_space=pltpu.SMEM)
    hbm = pl.BlockSpec(memory_space=pltpu.HBM)
    vmem = pl.BlockSpec(memory_space=pltpu.VMEM)
    return pl.pallas_call(
        functools.partial(attend_kernel, block, steps),
        in_specs=[smem, smem] + [hbm] * (len(arrays) + 1),
        out_specs=[vmem, vmem, vmem],
        scratch_shapes=[pltpu.VMEM(a.shape, a.dtype) for a in arrays]
        + [
            pltpu.VMEM((block * heads, width), jnp.float32),
            pltpu.VMEM((tiles, depth, TILE), jnp.bfloat16),
            pltpu.SemaphoreType.DMA((4,)),
            pltpu.SemaphoreType.DMA((3, rows // block)),
            pltpu.SemaphoreType.DMA((tiles,)),
        ],
        out_shape=[
            jax.ShapeDtypeStruct((rows + ID_ROWS, depth), jnp.bfloat16),
        ]
        + [jax.ShapeDtypeStruct((rows, out_local), jnp.bfloat16) for _ in steps],
        compiler_params=pltpu.CompilerParams(vmem_limit_bytes=57 * MIB),
        cost_estimate=SMALL,
        name="attend",
    )(lengths, me.reshape(1), *arrays, out_weight)


def project_kernel(steps, me_ref, a_hbm, w_ref, *refs):
    *out_refs, a_ref, buffer_ref, a_sem, sem_ref = refs
    out_local = out_refs[0].shape[1]
    tiles = out_local // TILE
    copy = pltpu.make_async_copy(a_hbm, a_ref, a_sem.at[0])
    copy.start()
    for i, step in enumerate(steps):
        for j in range(tiles):
            column = (me_ref[0] ^ step) * out_local + j * TILE
            fetch(w_ref, buffer_ref, sem_ref, i * tiles + j, column).start()
    copy.wait()
    for i, (step, out_ref) in enumerate(zip(steps, out_refs)):
        column = (me_ref[0] ^ step) * out_local
        project_tiles(a_ref, w_ref, buffer_ref, sem_ref, out_ref, tiles, i * tiles, column)


def project(attended, out_weight, me, steps, out_local, dtypes):
    rows, depth = attended.shape[0] - ID_ROWS, attended.shape[1]
    slots = len(dtypes) * (out_local // TILE)
    vmem = pl.BlockSpec(memory_space=pltpu.VMEM)
    hbm = pl.BlockSpec(memory_space=pl.ANY)
    return pl.pallas_call(
        functools.partial(project_kernel, steps),
        in_specs=[pl.BlockSpec(memory_space=pltpu.SMEM), hbm, hbm],
        out_specs=[vmem for _ in dtypes],
        scratch_shapes=[
            pltpu.VMEM(attended.shape, attended.dtype),
            pltpu.VMEM((slots, depth, TILE), jnp.bfloat16),
            pltpu.SemaphoreType.DMA((1,)),
            pltpu.SemaphoreType.DMA((slots,)),
        ],
        out_shape=[jax.ShapeDtypeStruct((rows, out_local), dtype) for dtype in dtypes],
        compiler_params=pltpu.CompilerParams(vmem_limit_bytes=40 * MIB),
        cost_estimate=SMALL,
        name="project",
    )(me.reshape(1), attended, out_weight)


def masked(low, owner, adapters, ranks, adapters_here):
    terms = jnp.concatenate([low] * adapters_here, axis=0)
    row = lax.broadcasted_iota(jnp.int32, terms.shape, 0)
    return jnp.where(row // ranks + owner * adapters_here == adapters, terms, 0.0)


def block_parts(blocks):
    arrays, places = [], []
    for i, parts in enumerate(blocks):
        first = 0
        for part in parts:
            arrays.append(part)
            places.append((i, first, part.shape[0]))
            first += part.shape[0]
    return arrays, places


def fetch_blocks(sources, places, column, target, sems, offset):
    columns = pl.ds(column, target.shape[2])
    return [
        pltpu.make_async_copy(
            source.at[:, columns], target.at[i, pl.ds(first, count)], sems.at[offset + j]
        )
        for j, (source, (i, first, count)) in enumerate(zip(sources, places))
    ]


def low_kernel(ranks, places, keys, here_ref, *refs):
    sides, sources = refs[:2], refs[2 : 2 + len(places)]
    out_ref, adapters_ref, side_ref, block_ref, sems = refs[2 + len(places) :]
    copies = fetch_all(sides, [side_ref.at[i] for i in range(2)], sems)
    parts = fetch_blocks(sources, places, 0, block_ref, sems, 2)
    for copy in parts:
        copy.start()
    blocks, pair = block_ref.shape[:2]
    rows = side_ref.shape[1] - ID_ROWS
    sides_t, adapters = [], []
    for i, copy in enumerate(copies):
        copy.wait()
        sides_t.append(side_ref[i, :rows].astype(jnp.float32).T.astype(jnp.bfloat16))
        ids = side_ref[i, rows:, :rows].astype(jnp.float32)
        adapters.append(ids[:8].astype(jnp.int32))
    a_t = jnp.concatenate(sides_t, axis=1)
    adapters_ref[...] = jnp.concatenate(adapters, axis=1)
    adapters = adapters_ref[:1, :]
    row = lax.broadcasted_iota(jnp.int32, (pair, a_t.shape[1]), 0)
    total = jnp.zeros(row.shape, jnp.float32)
    for i in range(blocks):
        for copy, place in zip(parts, places):
            if place[0] == i:
                copy.wait()
        part = jnp.dot(block_ref[i], a_t, preferred_element_type=jnp.float32)
        first = (here_ref[0] ^ keys[i]) * (pair // ranks)
        total += jnp.where(row // ranks + first == adapters, part, 0.0)
    low = total[:ranks]
    for a in range(1, pair // ranks):
        low += total[a * ranks : (a + 1) * ranks]
    out_ref[...] = low.astype(out_ref.dtype)


def low_rank(sides, blocks, depth, here, keys, rank):
    rows = sides[0].shape[0] - ID_ROWS
    arrays, places = block_parts(blocks)
    pair = sum(part.shape[0] for part in blocks[0])
    vmem = pl.BlockSpec(memory_space=pltpu.VMEM)
    return pl.pallas_call(
        functools.partial(low_kernel, rank, places, keys),
        in_specs=[pl.BlockSpec(memory_space=pltpu.SMEM)]
        + [pl.BlockSpec(memory_space=pl.ANY)] * (2 + len(arrays)),
        out_specs=[vmem, vmem],
        out_shape=[
            jax.ShapeDtypeStruct((rank, 2 * rows), jnp.bfloat16),
            jax.ShapeDtypeStruct((8, 2 * rows), jnp.int32),
        ],
        scratch_shapes=[
            pltpu.VMEM((2, *sides[0].shape), jnp.bfloat16),
            pltpu.VMEM((len(blocks), pair, depth), jnp.bfloat16),
            pltpu.SemaphoreType.DMA((2 + len(arrays),)),
        ],
        compiler_params=pltpu.CompilerParams(vmem_limit_bytes=16 * MIB),
        cost_estimate=SMALL,
        name="low_rank",
    )(here.reshape(1), *sides, *arrays)


def delta_kernel(ranks, places, column, keys, here_ref, adapters_ref, low_ref, *refs):
    sources = refs[: len(places)]
    mine_ref, other_ref, block_ref, sems = refs[len(places) :]
    parts = fetch_blocks(sources, places, column, block_ref, sems, 0)
    for copy in parts:
        copy.start()
    blocks, pair, width = block_ref.shape
    low = low_ref[...].astype(jnp.float32)
    sides = []
    for i in range(blocks):
        mine = masked(low, here_ref[0] ^ keys[i], adapters_ref[:1, :], ranks, pair // ranks)
        sides.append(mine.T.astype(jnp.bfloat16))
    for copy in parts:
        copy.wait()
    delta = jnp.dot(
        jnp.concatenate(sides, axis=1),
        block_ref[...].reshape(blocks * pair, width),
        preferred_element_type=jnp.float32,
    )
    delta = (0.5 * delta).astype(jnp.bfloat16)
    rows = mine_ref.shape[0]
    mine_ref[...] = delta[:rows]
    other_ref[...] = delta[rows:]


def correct(low, adapters, blocks, column, out_local, here, keys, rank):
    slots = adapters.shape[1]
    arrays, places = block_parts(blocks)
    pair = sum(part.shape[0] for part in blocks[0])
    vmem = pl.BlockSpec(memory_space=pltpu.VMEM)
    out = jax.ShapeDtypeStruct((slots // 2, out_local), jnp.bfloat16)
    return pl.pallas_call(
        functools.partial(delta_kernel, rank, places, column, keys),
        in_specs=[pl.BlockSpec(memory_space=pltpu.SMEM), vmem, vmem]
        + [pl.BlockSpec(memory_space=pl.ANY)] * len(arrays),
        out_specs=[vmem, vmem],
        out_shape=[out, out],
        scratch_shapes=[
            pltpu.VMEM((len(blocks), pair, out_local), jnp.bfloat16),
            pltpu.SemaphoreType.DMA((len(arrays),)),
        ],
        compiler_params=pltpu.CompilerParams(vmem_limit_bytes=16 * MIB),
        cost_estimate=SMALL,
        name="correct",
    )(here.reshape(1), adapters, low, *arrays)


def finish_kernel(occupied_ref, own_ref, *refs):
    *part_refs, out_ref = refs
    rows = out_ref.shape[0]
    live = jnp.broadcast_to(occupied_ref[...].astype(jnp.float32), (128, rows)).T
    for j in range(0, out_ref.shape[1], 128):
        columns = slice(j, j + 128)
        total = own_ref[:, columns]
        for ref in part_refs:
            total += ref[:, columns].astype(jnp.float32)
        out_ref[:, columns] = (live * total).astype(out_ref.dtype)


def finish(own, parts, occupied):
    rows, out_local = own.shape
    vmem = pl.BlockSpec(memory_space=pltpu.VMEM)
    return pl.pallas_call(
        finish_kernel,
        in_specs=[vmem] * (2 + len(parts)),
        out_specs=vmem,
        out_shape=jax.ShapeDtypeStruct((rows, out_local), jnp.bfloat16),
        compiler_params=pltpu.CompilerParams(vmem_limit_bytes=16 * MIB),
        cost_estimate=SMALL,
        name="finish",
    )(occupied.reshape(1, rows), own, *parts)


def exchange(value, axis, step):
    count = lax.axis_size(axis)
    return lax.ppermute(value, axis, [(i, i ^ step) for i in range(count)])


def neighbours():
    return [1 << i for i in range(1, lax.axis_size("dp").bit_length() - 1)]


def near_blocks(own):
    return {0: [own], **{bit: [exchange(own, "dp", bit)] for bit in neighbours()[:2]}}


def farther_blocks(blocks):
    for bit in neighbours()[2:]:
        for key in list(blocks):
            blocks[key | bit] = [exchange(part, "dp", bit) for part in blocks[key]]
    return blocks


def forwarded_blocks(blocks):
    a, b = neighbours()[:2]
    half = blocks[0][0].shape[0] // 2
    diagonal = [
        exchange(blocks[a][0][:half], "dp", b),
        exchange(blocks[b][0][half:], "dp", a),
    ]
    return farther_blocks({**blocks, a | b: diagonal})


def direct_blocks(own):
    a, b = neighbours()[:2]
    return farther_blocks({**near_blocks(own), a | b: [exchange(own, "dp", a | b)]})


def together(*values):
    return lax.optimization_barrier(values)


def body(
    queries,
    key_cache,
    value_cache,
    key_new,
    value_new,
    lengths,
    occupied,
    slot_request,
    request_adapter,
    out_weight,
    shrink_weight,
    expand_weight,
):
    adapters_here, depth, rank = shrink_weight.shape
    out_local = expand_weight.shape[2]
    shares = lax.axis_size("mp")
    me = lax.axis_index("mp")
    here = lax.axis_index("dp")
    pair = adapters_here * rank

    shrink = near_blocks(jnp.swapaxes(shrink_weight, 1, 2).reshape(pair, depth))
    expand = expand_weight.reshape(pair, out_local)

    halved = shares == 4
    early = (3, 1) if halved else (shares - 1, shares - 2)
    late = (2, 0) if halved else tuple(range(shares - 3, -1, -1))
    attended, *pieces = attend(
        (
            queries,
            key_cache,
            value_cache,
            key_new,
            value_new,
            slot_request.reshape(1, -1),
            request_adapter.reshape(1, -1),
        ),
        lengths,
        out_weight,
        me,
        early,
        out_local,
    )
    received = [
        exchange(piece, "mp", 1 if halved else step) for piece, step in zip(pieces, early)
    ]
    shrink, attended = together(shrink, attended)
    shrink = forwarded_blocks(shrink)
    beside = exchange(attended, "dp", 1)
    *pieces, own = project(
        attended,
        out_weight,
        me,
        late,
        out_local,
        [jnp.float32 if halved else jnp.bfloat16] * (len(late) - 1) + [jnp.float32],
    )
    pieces, received[0], attended, shrink, expand = together(
        pieces, received[0], attended, shrink, expand
    )
    expand = direct_blocks(expand)
    if halved:
        passed = received.pop(0).astype(jnp.float32)
        pieces = [(pieces[0] + passed).astype(jnp.bfloat16)]
    last = [exchange(part, "mp", step) for part, step in zip(pieces, late)]

    keys = tuple(shrink)
    low, adapters = low_rank(
        [attended, beside], list(shrink.values()), depth, here, keys, rank
    )
    low, received = together(low, received)
    step = shares // 2
    while step:
        arrived = exchange(low, "mp", step)
        low = (low.astype(jnp.float32) + arrived.astype(jnp.float32)).astype(jnp.bfloat16)
        step //= 2
    low, last = together(low, last)
    blocks = [expand[key] for key in keys]
    correction, other = correct(low, adapters, blocks, 0, out_local, here, keys, rank)
    parts = [*received, *last, correction, exchange(other, "dp", 1)]
    return finish(own, parts, occupied)


def solution(mesh):
    placed = (
        P("dp", "mp", None),
        P("dp", "mp", None, None),
        P("dp", "mp", None, None),
        P("dp", "mp", None),
        P("dp", "mp", None),
        P("dp"),
        P("dp"),
        P("dp"),
        P(),
        P("mp", None),
        P("dp", "mp", None),
        P("dp", None, "mp"),
    )
    return jax.shard_map(body, mesh=mesh, in_specs=placed, out_specs=P("dp", "mp"), check_vma=False)
```

```python
import functools
import math

import jax
import jax.numpy as jnp
from jax import lax
from jax.experimental import pallas as pl
from jax.experimental.pallas import tpu as pltpu
from jax.sharding import PartitionSpec as P

MIB = 1024 * 1024
TILE = 256
SMALL = pl.CostEstimate(flops=1, bytes_accessed=1, transcendentals=0)
ID_ROWS = 16


def attend_block(lengths, q_ref, k_ref, v_ref, kn_ref, vn_ref, first, acc_ref):
    slots = len(lengths)
    heads, width = q_ref.shape[1:]
    kv_local, cache = k_ref.shape[1], k_ref.shape[2]
    group = heads // kv_local
    inverse = 1.0 / math.sqrt(width)
    lane = lax.broadcasted_iota(jnp.int32, (group, cache), 1)
    parts = []
    for s in range(slots):
        scores = lax.dot_general(
            q_ref[first + s],
            k_ref[first + s].reshape(kv_local * cache, width),
            (((1,), (1,)), ((), ())),
            preferred_element_type=jnp.float32,
        )
        valid = lane < lengths[s]
        for g in range(kv_local):
            part = scores[g * group : (g + 1) * group, g * cache : (g + 1) * cache]
            parts.append(jnp.where(valid, part * inverse, -jnp.inf))
    cached = jnp.concatenate(parts, axis=0)
    block = pl.ds(first, slots)
    q_all = q_ref[block].astype(jnp.float32).reshape(slots * kv_local, group, width)
    kn = kn_ref[block].astype(jnp.float32).reshape(slots * kv_local, 1, width)
    vn = vn_ref[block].astype(jnp.float32).reshape(slots * kv_local, 1, width)
    fresh = (jnp.sum(q_all * kn, axis=-1, keepdims=True) * inverse).reshape(slots * heads, 1)
    top = jnp.maximum(jnp.max(cached, axis=-1, keepdims=True), fresh)
    cached_exp = jnp.exp(cached - top)
    fresh_exp = jnp.exp(fresh - top)
    scale = 1.0 / (jnp.sum(cached_exp, axis=-1, keepdims=True) + fresh_exp)
    weights = (cached_exp * scale).astype(jnp.bfloat16)
    fresh_w = (fresh_exp * scale).astype(jnp.bfloat16).astype(jnp.float32)
    new_part = (fresh_w.reshape(slots * kv_local, group, 1) * vn).reshape(slots * heads, width)
    for s in range(slots):
        values = jnp.concatenate([v_ref[first + s, g] for g in range(kv_local)], axis=1)
        summed = jnp.dot(
            weights[s * heads : (s + 1) * heads], values, preferred_element_type=jnp.float32
        )
        for g in range(kv_local):
            row = s * heads + g * group
            acc_ref[row : row + group, :] = (
                summed[g * group : (g + 1) * group, g * width : (g + 1) * width]
                + new_part[row : row + group]
            )


def fetch(w_ref, buffer_ref, sem_ref, slot, column):
    return pltpu.make_async_copy(
        w_ref.at[:, pl.ds(pl.multiple_of(column, TILE), TILE)],
        buffer_ref.at[slot],
        sem_ref.at[slot],
    )


def project_tiles(a_ref, w_ref, buffer_ref, sem_ref, out_ref, tiles, first_slot, column):
    def tile(j, carry):
        slot = first_slot + j
        fetch(w_ref, buffer_ref, sem_ref, slot, column + j * TILE).wait()
        out_ref[:, pl.ds(pl.multiple_of(j * TILE, TILE), TILE)] = jnp.dot(
            a_ref[: out_ref.shape[0]], buffer_ref[slot], preferred_element_type=jnp.float32
        ).astype(out_ref.dtype)
        return carry

    lax.fori_loop(0, tiles, tile, 0)


def fetch_all(sources, targets, sems):
    copies = [
        pltpu.make_async_copy(source, target, sems.at[i])
        for i, (source, target) in enumerate(zip(sources, targets))
    ]
    for copy in copies:
        copy.start()
    return copies


def look_up(requests, adapters):
    slots, known = requests.shape[1], adapters.shape[1]
    matches = lax.broadcasted_iota(jnp.int32, (known, slots), 0) == requests
    numbers = jnp.broadcast_to(adapters.astype(jnp.float32), (ID_ROWS, known))
    return jnp.dot(
        numbers.astype(jnp.bfloat16),
        matches.astype(jnp.float32).astype(jnp.bfloat16),
        preferred_element_type=jnp.float32,
    )


def attend_kernel(
    block,
    steps,
    lengths_ref,
    me_ref,
    q_hbm,
    k_hbm,
    v_hbm,
    kn_hbm,
    vn_hbm,
    request_hbm,
    adapter_hbm,
    w_ref,
    out_ref,
    first_ref,
    second_ref,
    q_ref,
    k_ref,
    v_ref,
    kn_ref,
    vn_ref,
    request_ref,
    adapter_ref,
    acc_ref,
    buffer_ref,
    new_sem,
    block_sem,
    sem_ref,
):
    rows, heads, width = q_ref.shape
    blocks = rows // block
    out_local = first_ref.shape[1]
    tiles = out_local // TILE

    def block_copies(i):
        part = pl.ds(pl.multiple_of(i * block, block), block)
        return [
            pltpu.make_async_copy(source.at[part], target.at[part], block_sem.at[j, i])
            for j, (source, target) in enumerate(
                ((q_hbm, q_ref), (k_hbm, k_ref), (v_hbm, v_ref))
            )
        ]

    new_copies = fetch_all(
        (kn_hbm, vn_hbm, request_hbm, adapter_hbm),
        (kn_ref, vn_ref, request_ref, adapter_ref),
        new_sem,
    )

    def begin(i, carry):
        for copy in block_copies(i):
            copy.start()
        return carry

    lax.fori_loop(0, blocks, begin, 0)
    columns = [(me_ref[0] ^ step) * out_local for step in steps]
    for i, column in enumerate(columns):
        for j in range(tiles):
            fetch(w_ref, buffer_ref, sem_ref, i * tiles + j, column + j * TILE).start()
    for copy in new_copies:
        copy.wait()
    out_ref[pl.ds(rows, ID_ROWS), :] = jnp.zeros((ID_ROWS, out_ref.shape[1]), out_ref.dtype)
    out_ref[pl.ds(rows, ID_ROWS), :rows] = look_up(request_ref[...], adapter_ref[...]).astype(
        out_ref.dtype
    )

    def one_block(i, carry):
        for copy in block_copies(i):
            copy.wait()
        first = pl.multiple_of(i * block, block)
        attend_block(
            [lengths_ref[first + s] for s in range(block)],
            q_ref,
            k_ref,
            v_ref,
            kn_ref,
            vn_ref,
            first,
            acc_ref,
        )
        for h in range(heads):
            out_ref[pl.ds(first, block), h * width : (h + 1) * width] = acc_ref[
                pl.ds(h, block, stride=heads), :
            ].astype(out_ref.dtype)
        return carry

    lax.fori_loop(0, blocks, one_block, 0)
    for i, (column, piece_ref) in enumerate(zip(columns, (first_ref, second_ref))):
        project_tiles(out_ref, w_ref, buffer_ref, sem_ref, piece_ref, tiles, i * tiles, column)


def attend(arrays, lengths, out_weight, me, steps, out_local):
    queries, key_cache = arrays[:2]
    rows, heads, width = queries.shape
    cache = key_cache.shape[2]
    block = min(16, rows)
    depth = heads * width
    tiles = len(steps) * (out_local // TILE)
    smem = pl.BlockSpec(memory_space=pltpu.SMEM)
    hbm = pl.BlockSpec(memory_space=pltpu.HBM)
    vmem = pl.BlockSpec(memory_space=pltpu.VMEM)
    return pl.pallas_call(
        functools.partial(attend_kernel, block, steps),
        in_specs=[smem, smem] + [hbm] * (len(arrays) + 1),
        out_specs=[vmem, vmem, vmem],
        scratch_shapes=[pltpu.VMEM(a.shape, a.dtype) for a in arrays]
        + [
            pltpu.VMEM((block * heads, width), jnp.float32),
            pltpu.VMEM((tiles, depth, TILE), jnp.bfloat16),
            pltpu.SemaphoreType.DMA((4,)),
            pltpu.SemaphoreType.DMA((3, rows // block)),
            pltpu.SemaphoreType.DMA((tiles,)),
        ],
        out_shape=[
            jax.ShapeDtypeStruct((rows + ID_ROWS, depth), jnp.bfloat16),
        ]
        + [jax.ShapeDtypeStruct((rows, out_local), jnp.bfloat16) for _ in steps],
        compiler_params=pltpu.CompilerParams(vmem_limit_bytes=57 * MIB),
        cost_estimate=SMALL,
        name="attend",
    )(lengths, me.reshape(1), *arrays, out_weight)


def project_kernel(steps, me_ref, a_hbm, w_ref, *refs):
    *out_refs, a_ref, buffer_ref, a_sem, sem_ref = refs
    out_local = out_refs[0].shape[1]
    tiles = out_local // TILE
    copy = pltpu.make_async_copy(a_hbm, a_ref, a_sem.at[0])
    copy.start()
    for i, step in enumerate(steps):
        for j in range(tiles):
            column = (me_ref[0] ^ step) * out_local + j * TILE
            fetch(w_ref, buffer_ref, sem_ref, i * tiles + j, column).start()
    copy.wait()
    for i, (step, out_ref) in enumerate(zip(steps, out_refs)):
        column = (me_ref[0] ^ step) * out_local
        project_tiles(a_ref, w_ref, buffer_ref, sem_ref, out_ref, tiles, i * tiles, column)


def project(attended, out_weight, me, steps, out_local, dtypes):
    rows, depth = attended.shape[0] - ID_ROWS, attended.shape[1]
    slots = len(dtypes) * (out_local // TILE)
    vmem = pl.BlockSpec(memory_space=pltpu.VMEM)
    hbm = pl.BlockSpec(memory_space=pl.ANY)
    return pl.pallas_call(
        functools.partial(project_kernel, steps),
        in_specs=[pl.BlockSpec(memory_space=pltpu.SMEM), hbm, hbm],
        out_specs=[vmem for _ in dtypes],
        scratch_shapes=[
            pltpu.VMEM(attended.shape, attended.dtype),
            pltpu.VMEM((slots, depth, TILE), jnp.bfloat16),
            pltpu.SemaphoreType.DMA((1,)),
            pltpu.SemaphoreType.DMA((slots,)),
        ],
        out_shape=[jax.ShapeDtypeStruct((rows, out_local), dtype) for dtype in dtypes],
        compiler_params=pltpu.CompilerParams(vmem_limit_bytes=40 * MIB),
        cost_estimate=SMALL,
        name="project",
    )(me.reshape(1), attended, out_weight)


def masked(low, owner, adapters, ranks, adapters_here):
    terms = jnp.concatenate([low] * adapters_here, axis=0)
    row = lax.broadcasted_iota(jnp.int32, terms.shape, 0)
    return jnp.where(row // ranks + owner * adapters_here == adapters, terms, 0.0)


def block_parts(blocks):
    arrays, places = [], []
    for i, parts in enumerate(blocks):
        first = 0
        for part in parts:
            arrays.append(part)
            places.append((i, first, part.shape[0]))
            first += part.shape[0]
    return arrays, places


def fetch_blocks(sources, places, column, target, sems, offset):
    columns = pl.ds(column, target.shape[2])
    return [
        pltpu.make_async_copy(
            source.at[:, columns], target.at[i, pl.ds(first, count)], sems.at[offset + j]
        )
        for j, (source, (i, first, count)) in enumerate(zip(sources, places))
    ]


def low_kernel(ranks, places, keys, here_ref, *refs):
    sides, sources = refs[:2], refs[2 : 2 + len(places)]
    out_ref, adapters_ref, side_ref, block_ref, sems = refs[2 + len(places) :]
    copies = fetch_all(sides, [side_ref.at[i] for i in range(2)], sems)
    parts = fetch_blocks(sources, places, 0, block_ref, sems, 2)
    for copy in parts:
        copy.start()
    blocks, pair = block_ref.shape[:2]
    rows = side_ref.shape[1] - ID_ROWS
    sides_t, adapters = [], []
    for i, copy in enumerate(copies):
        copy.wait()
        sides_t.append(side_ref[i, :rows].astype(jnp.float32).T.astype(jnp.bfloat16))
        ids = side_ref[i, rows:, :rows].astype(jnp.float32)
        adapters.append(ids[:8].astype(jnp.int32))
    a_t = jnp.concatenate(sides_t, axis=1)
    adapters_ref[...] = jnp.concatenate(adapters, axis=1)
    adapters = adapters_ref[:1, :]
    row = lax.broadcasted_iota(jnp.int32, (pair, a_t.shape[1]), 0)
    total = jnp.zeros(row.shape, jnp.float32)
    for i in range(blocks):
        for copy, place in zip(parts, places):
            if place[0] == i:
                copy.wait()
        part = jnp.dot(block_ref[i], a_t, preferred_element_type=jnp.float32)
        first = (here_ref[0] ^ keys[i]) * (pair // ranks)
        total += jnp.where(row // ranks + first == adapters, part, 0.0)
    low = total[:ranks]
    for a in range(1, pair // ranks):
        low += total[a * ranks : (a + 1) * ranks]
    out_ref[...] = low.astype(out_ref.dtype)


def low_rank(sides, blocks, depth, here, keys, rank):
    rows = sides[0].shape[0] - ID_ROWS
    arrays, places = block_parts(blocks)
    pair = sum(part.shape[0] for part in blocks[0])
    vmem = pl.BlockSpec(memory_space=pltpu.VMEM)
    return pl.pallas_call(
        functools.partial(low_kernel, rank, places, keys),
        in_specs=[pl.BlockSpec(memory_space=pltpu.SMEM)]
        + [pl.BlockSpec(memory_space=pl.ANY)] * (2 + len(arrays)),
        out_specs=[vmem, vmem],
        out_shape=[
            jax.ShapeDtypeStruct((rank, 2 * rows), jnp.bfloat16),
            jax.ShapeDtypeStruct((8, 2 * rows), jnp.int32),
        ],
        scratch_shapes=[
            pltpu.VMEM((2, *sides[0].shape), jnp.bfloat16),
            pltpu.VMEM((len(blocks), pair, depth), jnp.bfloat16),
            pltpu.SemaphoreType.DMA((2 + len(arrays),)),
        ],
        compiler_params=pltpu.CompilerParams(vmem_limit_bytes=16 * MIB),
        cost_estimate=SMALL,
        name="low_rank",
    )(here.reshape(1), *sides, *arrays)


def delta_kernel(ranks, places, column, keys, here_ref, adapters_ref, low_ref, *refs):
    sources = refs[: len(places)]
    mine_ref, other_ref, block_ref, sems = refs[len(places) :]
    parts = fetch_blocks(sources, places, column, block_ref, sems, 0)
    for copy in parts:
        copy.start()
    blocks, pair, width = block_ref.shape
    low = low_ref[...].astype(jnp.float32)
    sides = []
    for i in range(blocks):
        mine = masked(low, here_ref[0] ^ keys[i], adapters_ref[:1, :], ranks, pair // ranks)
        sides.append(mine.T.astype(jnp.bfloat16))
    for copy in parts:
        copy.wait()
    delta = jnp.dot(
        jnp.concatenate(sides, axis=1),
        block_ref[...].reshape(blocks * pair, width),
        preferred_element_type=jnp.float32,
    )
    delta = (0.5 * delta).astype(jnp.bfloat16)
    rows = mine_ref.shape[0]
    mine_ref[...] = delta[:rows]
    other_ref[...] = delta[rows:]


def correct(low, adapters, blocks, column, out_local, here, keys, rank):
    slots = adapters.shape[1]
    arrays, places = block_parts(blocks)
    pair = sum(part.shape[0] for part in blocks[0])
    vmem = pl.BlockSpec(memory_space=pltpu.VMEM)
    out = jax.ShapeDtypeStruct((slots // 2, out_local), jnp.bfloat16)
    return pl.pallas_call(
        functools.partial(delta_kernel, rank, places, column, keys),
        in_specs=[pl.BlockSpec(memory_space=pltpu.SMEM), vmem, vmem]
        + [pl.BlockSpec(memory_space=pl.ANY)] * len(arrays),
        out_specs=[vmem, vmem],
        out_shape=[out, out],
        scratch_shapes=[
            pltpu.VMEM((len(blocks), pair, out_local), jnp.bfloat16),
            pltpu.SemaphoreType.DMA((len(arrays),)),
        ],
        compiler_params=pltpu.CompilerParams(vmem_limit_bytes=16 * MIB),
        cost_estimate=SMALL,
        name="correct",
    )(here.reshape(1), adapters, low, *arrays)


def finish_kernel(occupied_ref, own_ref, *refs):
    *part_refs, out_ref = refs
    rows = out_ref.shape[0]
    live = jnp.broadcast_to(occupied_ref[...].astype(jnp.float32), (128, rows)).T
    for j in range(0, out_ref.shape[1], 128):
        columns = slice(j, j + 128)
        total = own_ref[:, columns]
        for ref in part_refs:
            total += ref[:, columns].astype(jnp.float32)
        out_ref[:, columns] = (live * total).astype(out_ref.dtype)


def finish(own, parts, occupied):
    rows, out_local = own.shape
    vmem = pl.BlockSpec(memory_space=pltpu.VMEM)
    return pl.pallas_call(
        finish_kernel,
        in_specs=[vmem] * (2 + len(parts)),
        out_specs=vmem,
        out_shape=jax.ShapeDtypeStruct((rows, out_local), jnp.bfloat16),
        compiler_params=pltpu.CompilerParams(vmem_limit_bytes=16 * MIB),
        cost_estimate=SMALL,
        name="finish",
    )(occupied.reshape(1, rows), own, *parts)


def exchange(value, axis, step):
    count = lax.axis_size(axis)
    return lax.ppermute(value, axis, [(i, i ^ step) for i in range(count)])


def neighbours():
    return [1 << i for i in range(1, lax.axis_size("dp").bit_length() - 1)]


def near_blocks(own):
    return {0: [own], **{bit: [exchange(own, "dp", bit)] for bit in neighbours()[:2]}}


def farther_blocks(blocks):
    for bit in neighbours()[2:]:
        for key in list(blocks):
            blocks[key | bit] = [exchange(part, "dp", bit) for part in blocks[key]]
    return blocks


def forwarded_blocks(blocks):
    a, b = neighbours()[:2]
    half = blocks[0][0].shape[0] // 2
    diagonal = [
        exchange(blocks[a][0][:half], "dp", b),
        exchange(blocks[b][0][half:], "dp", a),
    ]
    return farther_blocks({**blocks, a | b: diagonal})


def direct_blocks(own):
    a, b = neighbours()[:2]
    return farther_blocks({**near_blocks(own), a | b: [exchange(own, "dp", a | b)]})


def together(*values):
    return lax.optimization_barrier(values)


def body(
    queries,
    key_cache,
    value_cache,
    key_new,
    value_new,
    lengths,
    occupied,
    slot_request,
    request_adapter,
    out_weight,
    shrink_weight,
    expand_weight,
):
    adapters_here, depth, rank = shrink_weight.shape
    out_local = expand_weight.shape[2]
    shares = lax.axis_size("mp")
    me = lax.axis_index("mp")
    here = lax.axis_index("dp")
    pair = adapters_here * rank

    shrink = near_blocks(jnp.swapaxes(shrink_weight, 1, 2).reshape(pair, depth))
    expand = expand_weight.reshape(pair, out_local)

    halved = shares == 4
    early = (3, 1) if halved else (shares - 1, shares - 2)
    late = (2, 0) if halved else tuple(range(shares - 3, -1, -1))
    attended, *pieces = attend(
        (
            queries,
            key_cache,
            value_cache,
            key_new,
            value_new,
            slot_request.reshape(1, -1),
            request_adapter.reshape(1, -1),
        ),
        lengths,
        out_weight,
        me,
        early,
        out_local,
    )
    received = [
        exchange(piece, "mp", 1 if halved else step) for piece, step in zip(pieces, early)
    ]
    shrink, attended = together(shrink, attended)
    shrink = forwarded_blocks(shrink)
    beside = exchange(attended, "dp", 1)
    *pieces, own = project(
        attended,
        out_weight,
        me,
        late,
        out_local,
        [jnp.float32 if halved else jnp.bfloat16] * (len(late) - 1) + [jnp.float32],
    )
    pieces, received[0], attended, shrink, expand = together(
        pieces, received[0], attended, shrink, expand
    )
    expand = direct_blocks(expand)
    if halved:
        passed = received.pop(0).astype(jnp.float32)
        pieces = [(pieces[0] + passed).astype(jnp.bfloat16)]
    last = [exchange(part, "mp", step) for part, step in zip(pieces, late)]

    keys = tuple(shrink)
    low, adapters = low_rank(
        [attended, beside], list(shrink.values()), depth, here, keys, rank
    )
    low, received = together(low, received)
    step = 1
    while step < shares:
        arrived = exchange(low, "mp", step)
        low = (low.astype(jnp.float32) + arrived.astype(jnp.float32)).astype(jnp.bfloat16)
        if step == 1:
            low, last, expand = together(low, last, expand)
        step *= 2
    blocks = [expand[key] for key in keys]
    correction, other = correct(low, adapters, blocks, 0, out_local, here, keys, rank)
    parts = [*received, *last, correction, exchange(other, "dp", 1)]
    return finish(own, parts, occupied)


def solution(mesh):
    placed = (
        P("dp", "mp", None),
        P("dp", "mp", None, None),
        P("dp", "mp", None, None),
        P("dp", "mp", None),
        P("dp", "mp", None),
        P("dp"),
        P("dp"),
        P("dp"),
        P(),
        P("mp", None),
        P("dp", "mp", None),
        P("dp", None, "mp"),
    )
    return jax.shard_map(body, mesh=mesh, in_specs=placed, out_specs=P("dp", "mp"), check_vma=False)
```

```python
import functools
import math

import jax
import jax.numpy as jnp
from jax import lax
from jax.experimental import pallas as pl
from jax.experimental.pallas import tpu as pltpu
from jax.sharding import PartitionSpec as P

MIB = 1024 * 1024
TILE = 256
SMALL = pl.CostEstimate(flops=1, bytes_accessed=1, transcendentals=0)
ID_ROWS = 16


def attend_block(lengths, q_ref, k_ref, v_ref, kn_ref, vn_ref, first, acc_ref):
    slots = len(lengths)
    heads, width = q_ref.shape[1:]
    kv_local, cache = k_ref.shape[1], k_ref.shape[2]
    group = heads // kv_local
    inverse = 1.0 / math.sqrt(width)
    lane = lax.broadcasted_iota(jnp.int32, (group, cache), 1)
    parts = []
    for s in range(slots):
        scores = lax.dot_general(
            q_ref[first + s],
            k_ref[first + s].reshape(kv_local * cache, width),
            (((1,), (1,)), ((), ())),
            preferred_element_type=jnp.float32,
        )
        valid = lane < lengths[s]
        for g in range(kv_local):
            part = scores[g * group : (g + 1) * group, g * cache : (g + 1) * cache]
            parts.append(jnp.where(valid, part * inverse, -jnp.inf))
    cached = jnp.concatenate(parts, axis=0)
    block = pl.ds(first, slots)
    q_all = q_ref[block].astype(jnp.float32).reshape(slots * kv_local, group, width)
    kn = kn_ref[block].astype(jnp.float32).reshape(slots * kv_local, 1, width)
    vn = vn_ref[block].astype(jnp.float32).reshape(slots * kv_local, 1, width)
    fresh = (jnp.sum(q_all * kn, axis=-1, keepdims=True) * inverse).reshape(slots * heads, 1)
    top = jnp.maximum(jnp.max(cached, axis=-1, keepdims=True), fresh)
    cached_exp = jnp.exp(cached - top)
    fresh_exp = jnp.exp(fresh - top)
    scale = 1.0 / (jnp.sum(cached_exp, axis=-1, keepdims=True) + fresh_exp)
    weights = (cached_exp * scale).astype(jnp.bfloat16)
    fresh_w = (fresh_exp * scale).astype(jnp.bfloat16).astype(jnp.float32)
    new_part = (fresh_w.reshape(slots * kv_local, group, 1) * vn).reshape(slots * heads, width)
    for s in range(slots):
        values = jnp.concatenate([v_ref[first + s, g] for g in range(kv_local)], axis=1)
        summed = jnp.dot(
            weights[s * heads : (s + 1) * heads], values, preferred_element_type=jnp.float32
        )
        for g in range(kv_local):
            row = s * heads + g * group
            acc_ref[row : row + group, :] = (
                summed[g * group : (g + 1) * group, g * width : (g + 1) * width]
                + new_part[row : row + group]
            )


def fetch(w_ref, buffer_ref, sem_ref, slot, column):
    return pltpu.make_async_copy(
        w_ref.at[:, pl.ds(pl.multiple_of(column, TILE), TILE)],
        buffer_ref.at[slot],
        sem_ref.at[slot],
    )


def project_tiles(a_ref, w_ref, buffer_ref, sem_ref, out_ref, tiles, first_slot, column):
    def tile(j, carry):
        slot = first_slot + j
        fetch(w_ref, buffer_ref, sem_ref, slot, column + j * TILE).wait()
        out_ref[:, pl.ds(pl.multiple_of(j * TILE, TILE), TILE)] = jnp.dot(
            a_ref[: out_ref.shape[0]], buffer_ref[slot], preferred_element_type=jnp.float32
        ).astype(out_ref.dtype)
        return carry

    lax.fori_loop(0, tiles, tile, 0)


def fetch_all(sources, targets, sems):
    copies = [
        pltpu.make_async_copy(source, target, sems.at[i])
        for i, (source, target) in enumerate(zip(sources, targets))
    ]
    for copy in copies:
        copy.start()
    return copies


def look_up(requests, adapters):
    slots, known = requests.shape[1], adapters.shape[1]
    matches = lax.broadcasted_iota(jnp.int32, (known, slots), 0) == requests
    numbers = jnp.broadcast_to(adapters.astype(jnp.float32), (ID_ROWS, known))
    return jnp.dot(
        numbers.astype(jnp.bfloat16),
        matches.astype(jnp.float32).astype(jnp.bfloat16),
        preferred_element_type=jnp.float32,
    )


def attend_kernel(
    block,
    steps,
    lengths_ref,
    me_ref,
    q_hbm,
    k_hbm,
    v_hbm,
    kn_hbm,
    vn_hbm,
    request_hbm,
    adapter_hbm,
    w_ref,
    out_ref,
    first_ref,
    second_ref,
    q_ref,
    k_ref,
    v_ref,
    kn_ref,
    vn_ref,
    request_ref,
    adapter_ref,
    acc_ref,
    buffer_ref,
    new_sem,
    block_sem,
    sem_ref,
):
    rows, heads, width = q_ref.shape
    blocks = rows // block
    out_local = first_ref.shape[1]
    tiles = out_local // TILE

    def block_copies(i):
        part = pl.ds(pl.multiple_of(i * block, block), block)
        return [
            pltpu.make_async_copy(source.at[part], target.at[part], block_sem.at[j, i])
            for j, (source, target) in enumerate(
                ((q_hbm, q_ref), (k_hbm, k_ref), (v_hbm, v_ref))
            )
        ]

    new_copies = fetch_all(
        (kn_hbm, vn_hbm, request_hbm, adapter_hbm),
        (kn_ref, vn_ref, request_ref, adapter_ref),
        new_sem,
    )

    def begin(i, carry):
        for copy in block_copies(i):
            copy.start()
        return carry

    lax.fori_loop(0, blocks, begin, 0)
    columns = [(me_ref[0] ^ step) * out_local for step in steps]
    for i, column in enumerate(columns):
        for j in range(tiles):
            fetch(w_ref, buffer_ref, sem_ref, i * tiles + j, column + j * TILE).start()
    for copy in new_copies:
        copy.wait()
    out_ref[pl.ds(rows, ID_ROWS), :] = jnp.zeros((ID_ROWS, out_ref.shape[1]), out_ref.dtype)
    out_ref[pl.ds(rows, ID_ROWS), :rows] = look_up(request_ref[...], adapter_ref[...]).astype(
        out_ref.dtype
    )

    def one_block(i, carry):
        for copy in block_copies(i):
            copy.wait()
        first = pl.multiple_of(i * block, block)
        attend_block(
            [lengths_ref[first + s] for s in range(block)],
            q_ref,
            k_ref,
            v_ref,
            kn_ref,
            vn_ref,
            first,
            acc_ref,
        )
        for h in range(heads):
            out_ref[pl.ds(first, block), h * width : (h + 1) * width] = acc_ref[
                pl.ds(h, block, stride=heads), :
            ].astype(out_ref.dtype)
        return carry

    lax.fori_loop(0, blocks, one_block, 0)
    for i, (column, piece_ref) in enumerate(zip(columns, (first_ref, second_ref))):
        project_tiles(out_ref, w_ref, buffer_ref, sem_ref, piece_ref, tiles, i * tiles, column)


def attend(arrays, lengths, out_weight, me, steps, out_local):
    queries, key_cache = arrays[:2]
    rows, heads, width = queries.shape
    cache = key_cache.shape[2]
    block = min(16, rows)
    depth = heads * width
    tiles = len(steps) * (out_local // TILE)
    smem = pl.BlockSpec(memory_space=pltpu.SMEM)
    hbm = pl.BlockSpec(memory_space=pltpu.HBM)
    vmem = pl.BlockSpec(memory_space=pltpu.VMEM)
    return pl.pallas_call(
        functools.partial(attend_kernel, block, steps),
        in_specs=[smem, smem] + [hbm] * (len(arrays) + 1),
        out_specs=[vmem, vmem, vmem],
        scratch_shapes=[pltpu.VMEM(a.shape, a.dtype) for a in arrays]
        + [
            pltpu.VMEM((block * heads, width), jnp.float32),
            pltpu.VMEM((tiles, depth, TILE), jnp.bfloat16),
            pltpu.SemaphoreType.DMA((4,)),
            pltpu.SemaphoreType.DMA((3, rows // block)),
            pltpu.SemaphoreType.DMA((tiles,)),
        ],
        out_shape=[
            jax.ShapeDtypeStruct((rows + ID_ROWS, depth), jnp.bfloat16),
        ]
        + [jax.ShapeDtypeStruct((rows, out_local), jnp.bfloat16) for _ in steps],
        compiler_params=pltpu.CompilerParams(vmem_limit_bytes=57 * MIB),
        cost_estimate=SMALL,
        name="attend",
    )(lengths, me.reshape(1), *arrays, out_weight)


def project_kernel(steps, me_ref, a_hbm, w_ref, *refs):
    *out_refs, a_ref, buffer_ref, a_sem, sem_ref = refs
    out_local = out_refs[0].shape[1]
    tiles = out_local // TILE
    copy = pltpu.make_async_copy(a_hbm, a_ref, a_sem.at[0])
    copy.start()
    for i, step in enumerate(steps):
        for j in range(tiles):
            column = (me_ref[0] ^ step) * out_local + j * TILE
            fetch(w_ref, buffer_ref, sem_ref, i * tiles + j, column).start()
    copy.wait()
    for i, (step, out_ref) in enumerate(zip(steps, out_refs)):
        column = (me_ref[0] ^ step) * out_local
        project_tiles(a_ref, w_ref, buffer_ref, sem_ref, out_ref, tiles, i * tiles, column)


def project(attended, out_weight, me, steps, out_local, dtypes):
    rows, depth = attended.shape[0] - ID_ROWS, attended.shape[1]
    slots = len(dtypes) * (out_local // TILE)
    vmem = pl.BlockSpec(memory_space=pltpu.VMEM)
    hbm = pl.BlockSpec(memory_space=pl.ANY)
    return pl.pallas_call(
        functools.partial(project_kernel, steps),
        in_specs=[pl.BlockSpec(memory_space=pltpu.SMEM), hbm, hbm],
        out_specs=[vmem for _ in dtypes],
        scratch_shapes=[
            pltpu.VMEM(attended.shape, attended.dtype),
            pltpu.VMEM((slots, depth, TILE), jnp.bfloat16),
            pltpu.SemaphoreType.DMA((1,)),
            pltpu.SemaphoreType.DMA((slots,)),
        ],
        out_shape=[jax.ShapeDtypeStruct((rows, out_local), dtype) for dtype in dtypes],
        compiler_params=pltpu.CompilerParams(vmem_limit_bytes=40 * MIB),
        cost_estimate=SMALL,
        name="project",
    )(me.reshape(1), attended, out_weight)


def masked(low, owner, adapters, ranks, adapters_here):
    terms = jnp.concatenate([low] * adapters_here, axis=0)
    row = lax.broadcasted_iota(jnp.int32, terms.shape, 0)
    return jnp.where(row // ranks + owner * adapters_here == adapters, terms, 0.0)


def block_parts(blocks):
    arrays, places = [], []
    for i, parts in enumerate(blocks):
        first = 0
        for part in parts:
            arrays.append(part)
            places.append((i, first, part.shape[0]))
            first += part.shape[0]
    return arrays, places


def fetch_blocks(sources, places, column, target, sems, offset):
    columns = pl.ds(column, target.shape[2])
    return [
        pltpu.make_async_copy(
            source.at[:, columns], target.at[i, pl.ds(first, count)], sems.at[offset + j]
        )
        for j, (source, (i, first, count)) in enumerate(zip(sources, places))
    ]


def low_kernel(ranks, places, keys, here_ref, *refs):
    sides, sources = refs[:2], refs[2 : 2 + len(places)]
    out_ref, adapters_ref, side_ref, block_ref, sems = refs[2 + len(places) :]
    copies = fetch_all(sides, [side_ref.at[i] for i in range(2)], sems)
    parts = fetch_blocks(sources, places, 0, block_ref, sems, 2)
    for copy in parts:
        copy.start()
    blocks, pair = block_ref.shape[:2]
    rows = side_ref.shape[1] - ID_ROWS
    sides_t, adapters = [], []
    for i, copy in enumerate(copies):
        copy.wait()
        sides_t.append(side_ref[i, :rows].astype(jnp.float32).T.astype(jnp.bfloat16))
        ids = side_ref[i, rows:, :rows].astype(jnp.float32)
        adapters.append(ids[:8].astype(jnp.int32))
    a_t = jnp.concatenate(sides_t, axis=1)
    adapters_ref[...] = jnp.concatenate(adapters, axis=1)
    adapters = adapters_ref[:1, :]
    row = lax.broadcasted_iota(jnp.int32, (pair, a_t.shape[1]), 0)
    total = jnp.zeros(row.shape, jnp.float32)
    for i in range(blocks):
        for copy, place in zip(parts, places):
            if place[0] == i:
                copy.wait()
        part = jnp.dot(block_ref[i], a_t, preferred_element_type=jnp.float32)
        first = (here_ref[0] ^ keys[i]) * (pair // ranks)
        total += jnp.where(row // ranks + first == adapters, part, 0.0)
    low = total[:ranks]
    for a in range(1, pair // ranks):
        low += total[a * ranks : (a + 1) * ranks]
    out_ref[...] = low.astype(out_ref.dtype)


def low_rank(sides, blocks, depth, here, keys, rank):
    rows = sides[0].shape[0] - ID_ROWS
    arrays, places = block_parts(blocks)
    pair = sum(part.shape[0] for part in blocks[0])
    vmem = pl.BlockSpec(memory_space=pltpu.VMEM)
    return pl.pallas_call(
        functools.partial(low_kernel, rank, places, keys),
        in_specs=[pl.BlockSpec(memory_space=pltpu.SMEM)]
        + [pl.BlockSpec(memory_space=pl.ANY)] * (2 + len(arrays)),
        out_specs=[vmem, vmem],
        out_shape=[
            jax.ShapeDtypeStruct((rank, 2 * rows), jnp.bfloat16),
            jax.ShapeDtypeStruct((8, 2 * rows), jnp.int32),
        ],
        scratch_shapes=[
            pltpu.VMEM((2, *sides[0].shape), jnp.bfloat16),
            pltpu.VMEM((len(blocks), pair, depth), jnp.bfloat16),
            pltpu.SemaphoreType.DMA((2 + len(arrays),)),
        ],
        compiler_params=pltpu.CompilerParams(vmem_limit_bytes=16 * MIB),
        cost_estimate=SMALL,
        name="low_rank",
    )(here.reshape(1), *sides, *arrays)


def delta_kernel(ranks, places, column, keys, here_ref, adapters_ref, low_ref, *refs):
    sources = refs[: len(places)]
    mine_ref, other_ref, block_ref, sems = refs[len(places) :]
    parts = fetch_blocks(sources, places, column, block_ref, sems, 0)
    for copy in parts:
        copy.start()
    blocks, pair, width = block_ref.shape
    low = low_ref[...].astype(jnp.float32)
    sides = []
    for i in range(blocks):
        mine = masked(low, here_ref[0] ^ keys[i], adapters_ref[:1, :], ranks, pair // ranks)
        sides.append(mine.T.astype(jnp.bfloat16))
    for copy in parts:
        copy.wait()
    delta = jnp.dot(
        jnp.concatenate(sides, axis=1),
        block_ref[...].reshape(blocks * pair, width),
        preferred_element_type=jnp.float32,
    )
    delta = (0.5 * delta).astype(jnp.bfloat16)
    rows = mine_ref.shape[0]
    mine_ref[...] = delta[:rows]
    other_ref[...] = delta[rows:]


def correct(low, adapters, blocks, column, out_local, here, keys, rank):
    slots = adapters.shape[1]
    arrays, places = block_parts(blocks)
    pair = sum(part.shape[0] for part in blocks[0])
    vmem = pl.BlockSpec(memory_space=pltpu.VMEM)
    out = jax.ShapeDtypeStruct((slots // 2, out_local), jnp.bfloat16)
    return pl.pallas_call(
        functools.partial(delta_kernel, rank, places, column, keys),
        in_specs=[pl.BlockSpec(memory_space=pltpu.SMEM), vmem, vmem]
        + [pl.BlockSpec(memory_space=pl.ANY)] * len(arrays),
        out_specs=[vmem, vmem],
        out_shape=[out, out],
        scratch_shapes=[
            pltpu.VMEM((len(blocks), pair, out_local), jnp.bfloat16),
            pltpu.SemaphoreType.DMA((len(arrays),)),
        ],
        compiler_params=pltpu.CompilerParams(vmem_limit_bytes=16 * MIB),
        cost_estimate=SMALL,
        name="correct",
    )(here.reshape(1), adapters, low, *arrays)


def finish_kernel(occupied_ref, own_ref, *refs):
    *part_refs, out_ref = refs
    rows = out_ref.shape[0]
    live = jnp.broadcast_to(occupied_ref[...].astype(jnp.float32), (128, rows)).T
    for j in range(0, out_ref.shape[1], 128):
        columns = slice(j, j + 128)
        total = own_ref[:, columns].astype(jnp.float32)
        for ref in part_refs:
            total += ref[:, columns].astype(jnp.float32)
        out_ref[:, columns] = (live * total).astype(out_ref.dtype)


def finish(own, parts, occupied):
    rows, out_local = own.shape
    vmem = pl.BlockSpec(memory_space=pltpu.VMEM)
    return pl.pallas_call(
        finish_kernel,
        in_specs=[vmem] * (2 + len(parts)),
        out_specs=vmem,
        out_shape=jax.ShapeDtypeStruct((rows, out_local), jnp.bfloat16),
        compiler_params=pltpu.CompilerParams(vmem_limit_bytes=16 * MIB),
        cost_estimate=SMALL,
        name="finish",
    )(occupied.reshape(1, rows), own, *parts)


def exchange(value, axis, step):
    count = lax.axis_size(axis)
    return lax.ppermute(value, axis, [(i, i ^ step) for i in range(count)])


def neighbours():
    return [1 << i for i in range(1, lax.axis_size("dp").bit_length() - 1)]


def near_blocks(own):
    return {0: [own], **{bit: [exchange(own, "dp", bit)] for bit in neighbours()[:2]}}


def farther_blocks(blocks):
    for bit in neighbours()[2:]:
        for key in list(blocks):
            blocks[key | bit] = [exchange(part, "dp", bit) for part in blocks[key]]
    return blocks


def forwarded_blocks(blocks):
    a, b = neighbours()[:2]
    half = blocks[0][0].shape[0] // 2
    diagonal = [
        exchange(blocks[a][0][:half], "dp", b),
        exchange(blocks[b][0][half:], "dp", a),
    ]
    return farther_blocks({**blocks, a | b: diagonal})


def direct_blocks(own):
    a, b = neighbours()[:2]
    return farther_blocks({**near_blocks(own), a | b: [exchange(own, "dp", a | b)]})


def together(*values):
    return lax.optimization_barrier(values)


def body(
    queries,
    key_cache,
    value_cache,
    key_new,
    value_new,
    lengths,
    occupied,
    slot_request,
    request_adapter,
    out_weight,
    shrink_weight,
    expand_weight,
):
    adapters_here, depth, rank = shrink_weight.shape
    out_local = expand_weight.shape[2]
    shares = lax.axis_size("mp")
    me = lax.axis_index("mp")
    here = lax.axis_index("dp")
    pair = adapters_here * rank

    shrink = near_blocks(jnp.swapaxes(shrink_weight, 1, 2).reshape(pair, depth))
    expand = expand_weight.reshape(pair, out_local)

    halved = shares == 4
    early = (3, 1) if halved else (shares - 1, shares - 2)
    late = (2, 0) if halved else tuple(range(shares - 3, -1, -1))
    attended, *pieces = attend(
        (
            queries,
            key_cache,
            value_cache,
            key_new,
            value_new,
            slot_request.reshape(1, -1),
            request_adapter.reshape(1, -1),
        ),
        lengths,
        out_weight,
        me,
        early,
        out_local,
    )
    received = [
        exchange(piece, "mp", 1 if halved else step) for piece, step in zip(pieces, early)
    ]
    shrink, attended = together(shrink, attended)
    shrink = forwarded_blocks(shrink)
    beside = exchange(attended, "dp", 1)
    *pieces, own = project(
        attended,
        out_weight,
        me,
        late,
        out_local,
        [jnp.bfloat16] * len(late),
    )
    pieces, received[0], attended, shrink, expand = together(
        pieces, received[0], attended, shrink, expand
    )
    expand = direct_blocks(expand)
    if halved:
        passed = received.pop(0).astype(jnp.float32)
        pieces = [(pieces[0].astype(jnp.float32) + passed).astype(jnp.bfloat16)]
    last = [exchange(part, "mp", step) for part, step in zip(pieces, late)]

    keys = tuple(shrink)
    low, adapters = low_rank(
        [attended, beside], list(shrink.values()), depth, here, keys, rank
    )
    low, received = together(low, received)
    step = 1
    while step < shares:
        arrived = exchange(low, "mp", step)
        low = (low.astype(jnp.float32) + arrived.astype(jnp.float32)).astype(jnp.bfloat16)
        if step == 1:
            low, last, expand = together(low, last, expand)
        step *= 2
    blocks = [expand[key] for key in keys]
    correction, other = correct(low, adapters, blocks, 0, out_local, here, keys, rank)
    parts = [*received, *last, correction, exchange(other, "dp", 1)]
    return finish(own, parts, occupied)


def solution(mesh):
    placed = (
        P("dp", "mp", None),
        P("dp", "mp", None, None),
        P("dp", "mp", None, None),
        P("dp", "mp", None),
        P("dp", "mp", None),
        P("dp"),
        P("dp"),
        P("dp"),
        P(),
        P("mp", None),
        P("dp", "mp", None),
        P("dp", None, "mp"),
    )
    return jax.shard_map(body, mesh=mesh, in_specs=placed, out_specs=P("dp", "mp"), check_vma=False)
```

```python
import functools
import math

import jax
import jax.numpy as jnp
from jax import lax
from jax.experimental import pallas as pl
from jax.experimental.pallas import tpu as pltpu
from jax.sharding import PartitionSpec as P

MIB = 1024 * 1024
TILE = 256
SMALL = pl.CostEstimate(flops=1, bytes_accessed=1, transcendentals=0)
ID_ROWS = 16


def attend_block(lengths, q_ref, k_ref, v_ref, kn_ref, vn_ref, first, acc_ref):
    slots = len(lengths)
    heads, width = q_ref.shape[1:]
    kv_local, cache = k_ref.shape[1], k_ref.shape[2]
    group = heads // kv_local
    inverse = 1.0 / math.sqrt(width)
    lane = lax.broadcasted_iota(jnp.int32, (group, cache), 1)
    parts = []
    for s in range(slots):
        scores = lax.dot_general(
            q_ref[first + s],
            k_ref[first + s].reshape(kv_local * cache, width),
            (((1,), (1,)), ((), ())),
            preferred_element_type=jnp.float32,
        )
        valid = lane < lengths[s]
        for g in range(kv_local):
            part = scores[g * group : (g + 1) * group, g * cache : (g + 1) * cache]
            parts.append(jnp.where(valid, part * inverse, -jnp.inf))
    cached = jnp.concatenate(parts, axis=0)
    block = pl.ds(first, slots)
    q_all = q_ref[block].astype(jnp.float32).reshape(slots * kv_local, group, width)
    kn = kn_ref[block].astype(jnp.float32).reshape(slots * kv_local, 1, width)
    vn = vn_ref[block].astype(jnp.float32).reshape(slots * kv_local, 1, width)
    fresh = (jnp.sum(q_all * kn, axis=-1, keepdims=True) * inverse).reshape(slots * heads, 1)
    top = jnp.maximum(jnp.max(cached, axis=-1, keepdims=True), fresh)
    cached_exp = jnp.exp(cached - top)
    fresh_exp = jnp.exp(fresh - top)
    scale = 1.0 / (jnp.sum(cached_exp, axis=-1, keepdims=True) + fresh_exp)
    weights = (cached_exp * scale).astype(jnp.bfloat16)
    fresh_w = (fresh_exp * scale).astype(jnp.bfloat16).astype(jnp.float32)
    new_part = (fresh_w.reshape(slots * kv_local, group, 1) * vn).reshape(slots * heads, width)
    for s in range(slots):
        values = jnp.concatenate([v_ref[first + s, g] for g in range(kv_local)], axis=1)
        summed = jnp.dot(
            weights[s * heads : (s + 1) * heads], values, preferred_element_type=jnp.float32
        )
        for g in range(kv_local):
            row = s * heads + g * group
            acc_ref[row : row + group, :] = (
                summed[g * group : (g + 1) * group, g * width : (g + 1) * width]
                + new_part[row : row + group]
            )


def fetch(w_ref, buffer_ref, sem_ref, slot, column):
    return pltpu.make_async_copy(
        w_ref.at[:, pl.ds(pl.multiple_of(column, TILE), TILE)],
        buffer_ref.at[slot],
        sem_ref.at[slot],
    )


def project_tiles(a_ref, w_ref, buffer_ref, sem_ref, out_ref, tiles, first_slot, column):
    def tile(j, carry):
        slot = first_slot + j
        fetch(w_ref, buffer_ref, sem_ref, slot, column + j * TILE).wait()
        out_ref[:, pl.ds(pl.multiple_of(j * TILE, TILE), TILE)] = jnp.dot(
            a_ref[: out_ref.shape[0]], buffer_ref[slot], preferred_element_type=jnp.float32
        ).astype(out_ref.dtype)
        return carry

    lax.fori_loop(0, tiles, tile, 0)


def fetch_all(sources, targets, sems):
    copies = [
        pltpu.make_async_copy(source, target, sems.at[i])
        for i, (source, target) in enumerate(zip(sources, targets))
    ]
    for copy in copies:
        copy.start()
    return copies


def look_up(requests, adapters):
    slots, known = requests.shape[1], adapters.shape[1]
    matches = lax.broadcasted_iota(jnp.int32, (known, slots), 0) == requests
    numbers = jnp.broadcast_to(adapters.astype(jnp.float32), (ID_ROWS, known))
    return jnp.dot(
        numbers.astype(jnp.bfloat16),
        matches.astype(jnp.float32).astype(jnp.bfloat16),
        preferred_element_type=jnp.float32,
    )


def attend_kernel(
    block,
    steps,
    lengths_ref,
    me_ref,
    q_hbm,
    k_hbm,
    v_hbm,
    kn_hbm,
    vn_hbm,
    request_hbm,
    adapter_hbm,
    w_ref,
    out_ref,
    first_ref,
    second_ref,
    q_ref,
    k_ref,
    v_ref,
    kn_ref,
    vn_ref,
    request_ref,
    adapter_ref,
    acc_ref,
    buffer_ref,
    new_sem,
    block_sem,
    sem_ref,
):
    rows, heads, width = q_ref.shape
    blocks = rows // block
    out_local = first_ref.shape[1]
    tiles = out_local // TILE

    def block_copies(i):
        part = pl.ds(pl.multiple_of(i * block, block), block)
        return [
            pltpu.make_async_copy(source.at[part], target.at[part], block_sem.at[j, i])
            for j, (source, target) in enumerate(
                ((q_hbm, q_ref), (k_hbm, k_ref), (v_hbm, v_ref))
            )
        ]

    new_copies = fetch_all(
        (kn_hbm, vn_hbm, request_hbm, adapter_hbm),
        (kn_ref, vn_ref, request_ref, adapter_ref),
        new_sem,
    )

    def begin(i, carry):
        for copy in block_copies(i):
            copy.start()
        return carry

    lax.fori_loop(0, blocks, begin, 0)
    columns = [(me_ref[0] ^ step) * out_local for step in steps]
    for i, column in enumerate(columns):
        for j in range(tiles):
            fetch(w_ref, buffer_ref, sem_ref, i * tiles + j, column + j * TILE).start()
    for copy in new_copies:
        copy.wait()
    out_ref[pl.ds(rows, ID_ROWS), :] = jnp.zeros((ID_ROWS, out_ref.shape[1]), out_ref.dtype)
    out_ref[pl.ds(rows, ID_ROWS), :rows] = look_up(request_ref[...], adapter_ref[...]).astype(
        out_ref.dtype
    )

    def one_block(i, carry):
        for copy in block_copies(i):
            copy.wait()
        first = pl.multiple_of(i * block, block)
        attend_block(
            [lengths_ref[first + s] for s in range(block)],
            q_ref,
            k_ref,
            v_ref,
            kn_ref,
            vn_ref,
            first,
            acc_ref,
        )
        for h in range(heads):
            out_ref[pl.ds(first, block), h * width : (h + 1) * width] = acc_ref[
                pl.ds(h, block, stride=heads), :
            ].astype(out_ref.dtype)
        return carry

    lax.fori_loop(0, blocks, one_block, 0)
    for i, (column, piece_ref) in enumerate(zip(columns, (first_ref, second_ref))):
        project_tiles(out_ref, w_ref, buffer_ref, sem_ref, piece_ref, tiles, i * tiles, column)


def attend(arrays, lengths, out_weight, me, steps, out_local):
    queries, key_cache = arrays[:2]
    rows, heads, width = queries.shape
    cache = key_cache.shape[2]
    block = min(16, rows)
    depth = heads * width
    tiles = len(steps) * (out_local // TILE)
    smem = pl.BlockSpec(memory_space=pltpu.SMEM)
    hbm = pl.BlockSpec(memory_space=pltpu.HBM)
    vmem = pl.BlockSpec(memory_space=pltpu.VMEM)
    return pl.pallas_call(
        functools.partial(attend_kernel, block, steps),
        in_specs=[smem, smem] + [hbm] * (len(arrays) + 1),
        out_specs=[vmem, vmem, vmem],
        scratch_shapes=[pltpu.VMEM(a.shape, a.dtype) for a in arrays]
        + [
            pltpu.VMEM((block * heads, width), jnp.float32),
            pltpu.VMEM((tiles, depth, TILE), jnp.bfloat16),
            pltpu.SemaphoreType.DMA((4,)),
            pltpu.SemaphoreType.DMA((3, rows // block)),
            pltpu.SemaphoreType.DMA((tiles,)),
        ],
        out_shape=[
            jax.ShapeDtypeStruct((rows + ID_ROWS, depth), jnp.bfloat16),
        ]
        + [jax.ShapeDtypeStruct((rows, out_local), jnp.bfloat16) for _ in steps],
        compiler_params=pltpu.CompilerParams(vmem_limit_bytes=57 * MIB),
        cost_estimate=SMALL,
        name="attend",
    )(lengths, me.reshape(1), *arrays, out_weight)


def project_kernel(steps, me_ref, a_hbm, w_ref, *refs):
    *out_refs, a_ref, buffer_ref, a_sem, sem_ref = refs
    out_local = out_refs[0].shape[1]
    tiles = out_local // TILE
    copy = pltpu.make_async_copy(a_hbm, a_ref, a_sem.at[0])
    copy.start()
    for i, step in enumerate(steps):
        for j in range(tiles):
            column = (me_ref[0] ^ step) * out_local + j * TILE
            fetch(w_ref, buffer_ref, sem_ref, i * tiles + j, column).start()
    copy.wait()
    for i, (step, out_ref) in enumerate(zip(steps, out_refs)):
        column = (me_ref[0] ^ step) * out_local
        project_tiles(a_ref, w_ref, buffer_ref, sem_ref, out_ref, tiles, i * tiles, column)


def project(attended, out_weight, me, steps, out_local, dtypes):
    rows, depth = attended.shape[0] - ID_ROWS, attended.shape[1]
    slots = len(dtypes) * (out_local // TILE)
    vmem = pl.BlockSpec(memory_space=pltpu.VMEM)
    hbm = pl.BlockSpec(memory_space=pl.ANY)
    return pl.pallas_call(
        functools.partial(project_kernel, steps),
        in_specs=[pl.BlockSpec(memory_space=pltpu.SMEM), hbm, hbm],
        out_specs=[vmem for _ in dtypes],
        scratch_shapes=[
            pltpu.VMEM(attended.shape, attended.dtype),
            pltpu.VMEM((slots, depth, TILE), jnp.bfloat16),
            pltpu.SemaphoreType.DMA((1,)),
            pltpu.SemaphoreType.DMA((slots,)),
        ],
        out_shape=[jax.ShapeDtypeStruct((rows, out_local), dtype) for dtype in dtypes],
        compiler_params=pltpu.CompilerParams(vmem_limit_bytes=40 * MIB),
        cost_estimate=SMALL,
        name="project",
    )(me.reshape(1), attended, out_weight)


def masked(low, owner, adapters, ranks, adapters_here):
    terms = jnp.concatenate([low] * adapters_here, axis=0)
    row = lax.broadcasted_iota(jnp.int32, terms.shape, 0)
    return jnp.where(row // ranks + owner * adapters_here == adapters, terms, 0.0)


def block_parts(blocks):
    arrays, places = [], []
    for i, parts in enumerate(blocks):
        first = 0
        for part in parts:
            arrays.append(part)
            places.append((i, first, part.shape[0]))
            first += part.shape[0]
    return arrays, places


def fetch_blocks(sources, places, column, target, sems, offset):
    columns = pl.ds(column, target.shape[2])
    return [
        pltpu.make_async_copy(
            source.at[:, columns], target.at[i, pl.ds(first, count)], sems.at[offset + j]
        )
        for j, (source, (i, first, count)) in enumerate(zip(sources, places))
    ]


def low_kernel(ranks, places, keys, here_ref, *refs):
    sides, sources = refs[:2], refs[2 : 2 + len(places)]
    out_ref, adapters_ref, side_ref, block_ref, sems = refs[2 + len(places) :]
    copies = fetch_all(sides, [side_ref.at[i] for i in range(2)], sems)
    parts = fetch_blocks(sources, places, 0, block_ref, sems, 2)
    for copy in parts:
        copy.start()
    blocks, pair = block_ref.shape[:2]
    rows = side_ref.shape[1] - ID_ROWS
    sides_t, adapters = [], []
    for i, copy in enumerate(copies):
        copy.wait()
        sides_t.append(side_ref[i, :rows].astype(jnp.float32).T.astype(jnp.bfloat16))
        ids = side_ref[i, rows:, :rows].astype(jnp.float32)
        adapters.append(ids[:8].astype(jnp.int32))
    a_t = jnp.concatenate(sides_t, axis=1)
    adapters_ref[...] = jnp.concatenate(adapters, axis=1)
    adapters = adapters_ref[:1, :]
    row = lax.broadcasted_iota(jnp.int32, (pair, a_t.shape[1]), 0)
    total = jnp.zeros(row.shape, jnp.float32)
    for i in range(blocks):
        for copy, place in zip(parts, places):
            if place[0] == i:
                copy.wait()
        part = jnp.dot(block_ref[i], a_t, preferred_element_type=jnp.float32)
        first = (here_ref[0] ^ keys[i]) * (pair // ranks)
        total += jnp.where(row // ranks + first == adapters, part, 0.0)
    low = total[:ranks]
    for a in range(1, pair // ranks):
        low += total[a * ranks : (a + 1) * ranks]
    out_ref[...] = low.astype(out_ref.dtype)


def low_rank(sides, blocks, depth, here, keys, rank):
    rows = sides[0].shape[0] - ID_ROWS
    arrays, places = block_parts(blocks)
    pair = sum(part.shape[0] for part in blocks[0])
    vmem = pl.BlockSpec(memory_space=pltpu.VMEM)
    return pl.pallas_call(
        functools.partial(low_kernel, rank, places, keys),
        in_specs=[pl.BlockSpec(memory_space=pltpu.SMEM)]
        + [pl.BlockSpec(memory_space=pl.ANY)] * (2 + len(arrays)),
        out_specs=[vmem, vmem],
        out_shape=[
            jax.ShapeDtypeStruct((rank, 2 * rows), jnp.bfloat16),
            jax.ShapeDtypeStruct((8, 2 * rows), jnp.int32),
        ],
        scratch_shapes=[
            pltpu.VMEM((2, *sides[0].shape), jnp.bfloat16),
            pltpu.VMEM((len(blocks), pair, depth), jnp.bfloat16),
            pltpu.SemaphoreType.DMA((2 + len(arrays),)),
        ],
        compiler_params=pltpu.CompilerParams(vmem_limit_bytes=16 * MIB),
        cost_estimate=SMALL,
        name="low_rank",
    )(here.reshape(1), *sides, *arrays)


def delta_kernel(ranks, places, column, keys, here_ref, adapters_ref, low_ref, *refs):
    sources = refs[: len(places)]
    mine_ref, other_ref, block_ref, sems = refs[len(places) :]
    parts = fetch_blocks(sources, places, column, block_ref, sems, 0)
    for copy in parts:
        copy.start()
    blocks, pair, width = block_ref.shape
    low = low_ref[...].astype(jnp.float32)
    sides = []
    for i in range(blocks):
        mine = masked(low, here_ref[0] ^ keys[i], adapters_ref[:1, :], ranks, pair // ranks)
        sides.append(mine.T.astype(jnp.bfloat16))
    for copy in parts:
        copy.wait()
    delta = jnp.dot(
        jnp.concatenate(sides, axis=1),
        block_ref[...].reshape(blocks * pair, width),
        preferred_element_type=jnp.float32,
    )
    delta = (0.5 * delta).astype(jnp.bfloat16)
    rows = mine_ref.shape[0]
    mine_ref[...] = delta[:rows]
    other_ref[...] = delta[rows:]


def correct(low, adapters, blocks, column, out_local, here, keys, rank):
    slots = adapters.shape[1]
    arrays, places = block_parts(blocks)
    pair = sum(part.shape[0] for part in blocks[0])
    vmem = pl.BlockSpec(memory_space=pltpu.VMEM)
    out = jax.ShapeDtypeStruct((slots // 2, out_local), jnp.bfloat16)
    return pl.pallas_call(
        functools.partial(delta_kernel, rank, places, column, keys),
        in_specs=[pl.BlockSpec(memory_space=pltpu.SMEM), vmem, vmem]
        + [pl.BlockSpec(memory_space=pl.ANY)] * len(arrays),
        out_specs=[vmem, vmem],
        out_shape=[out, out],
        scratch_shapes=[
            pltpu.VMEM((len(blocks), pair, out_local), jnp.bfloat16),
            pltpu.SemaphoreType.DMA((len(arrays),)),
        ],
        compiler_params=pltpu.CompilerParams(vmem_limit_bytes=16 * MIB),
        cost_estimate=SMALL,
        name="correct",
    )(here.reshape(1), adapters, low, *arrays)


def finish_kernel(occupied_ref, own_ref, *refs):
    *part_refs, out_ref = refs
    rows = out_ref.shape[0]
    live = jnp.broadcast_to(occupied_ref[...].astype(jnp.float32), (128, rows)).T
    for j in range(0, out_ref.shape[1], 128):
        columns = slice(j, j + 128)
        total = own_ref[:, columns].astype(jnp.float32)
        for ref in part_refs:
            total += ref[:, columns].astype(jnp.float32)
        out_ref[:, columns] = (live * total).astype(out_ref.dtype)


def finish(own, parts, occupied):
    rows, out_local = own.shape
    vmem = pl.BlockSpec(memory_space=pltpu.VMEM)
    return pl.pallas_call(
        finish_kernel,
        in_specs=[vmem] * (2 + len(parts)),
        out_specs=vmem,
        out_shape=jax.ShapeDtypeStruct((rows, out_local), jnp.bfloat16),
        compiler_params=pltpu.CompilerParams(vmem_limit_bytes=16 * MIB),
        cost_estimate=SMALL,
        name="finish",
    )(occupied.reshape(1, rows), own, *parts)


def exchange(value, axis, step):
    count = lax.axis_size(axis)
    return lax.ppermute(value, axis, [(i, i ^ step) for i in range(count)])


def neighbours():
    return [1 << i for i in range(1, lax.axis_size("dp").bit_length() - 1)]


def near_blocks(own):
    return {0: [own], **{bit: [exchange(own, "dp", bit)] for bit in neighbours()[:2]}}


def farther_blocks(blocks):
    for bit in neighbours()[2:]:
        for key in list(blocks):
            blocks[key | bit] = [exchange(part, "dp", bit) for part in blocks[key]]
    return blocks


def forwarded_blocks(blocks):
    a, b = neighbours()[:2]
    half = blocks[0][0].shape[0] // 2
    diagonal = [
        exchange(blocks[a][0][:half], "dp", b),
        exchange(blocks[b][0][half:], "dp", a),
    ]
    return farther_blocks({**blocks, a | b: diagonal})


def direct_blocks(own):
    a, b = neighbours()[:2]
    return farther_blocks({**near_blocks(own), a | b: [exchange(own, "dp", a | b)]})


def together(*values):
    return lax.optimization_barrier(values)


def body(
    queries,
    key_cache,
    value_cache,
    key_new,
    value_new,
    lengths,
    occupied,
    slot_request,
    request_adapter,
    out_weight,
    shrink_weight,
    expand_weight,
):
    adapters_here, depth, rank = shrink_weight.shape
    out_local = expand_weight.shape[2]
    shares = lax.axis_size("mp")
    me = lax.axis_index("mp")
    here = lax.axis_index("dp")
    pair = adapters_here * rank

    shrink = near_blocks(jnp.swapaxes(shrink_weight, 1, 2).reshape(pair, depth))
    expand = expand_weight.reshape(pair, out_local)

    halved = shares == 4
    early = (3, 1) if halved else (shares - 1, shares - 2)
    late = (2, 0) if halved else tuple(range(shares - 3, -1, -1))
    attended, *pieces = attend(
        (
            queries,
            key_cache,
            value_cache,
            key_new,
            value_new,
            slot_request.reshape(1, -1),
            request_adapter.reshape(1, -1),
        ),
        lengths,
        out_weight,
        me,
        early,
        out_local,
    )
    received = [
        exchange(piece, "mp", 1 if halved else step) for piece, step in zip(pieces, early)
    ]
    shrink, attended = together(shrink, attended)
    shrink = forwarded_blocks(shrink)
    beside = exchange(attended, "dp", 1)
    *pieces, own = project(
        attended,
        out_weight,
        me,
        late,
        out_local,
        [jnp.bfloat16] * len(late),
    )
    pieces, received[0], attended, shrink, expand = together(
        pieces, received[0], attended, shrink, expand
    )
    expand = direct_blocks(expand)
    if halved:
        passed = received.pop(0).astype(jnp.float32)
        pieces = [(pieces[0].astype(jnp.float32) + passed).astype(jnp.bfloat16)]
    last = [exchange(part, "mp", step) for part, step in zip(pieces, late)]

    keys = tuple(shrink)
    low, adapters = low_rank(
        [attended, beside], list(shrink.values()), depth, here, keys, rank
    )
    low, received = together(low, received)
    step = 1
    while step < shares:
        arrived = exchange(low, "mp", step)
        low = (low.astype(jnp.float32) + arrived.astype(jnp.float32)).astype(jnp.bfloat16)
        if step == 1:
            low, last = together(low, last)
        step *= 2
    blocks = [expand[key] for key in keys]
    correction, other = correct(low, adapters, blocks, 0, out_local, here, keys, rank)
    parts = [*received, *last, correction, exchange(other, "dp", 1)]
    return finish(own, parts, occupied)


def solution(mesh):
    placed = (
        P("dp", "mp", None),
        P("dp", "mp", None, None),
        P("dp", "mp", None, None),
        P("dp", "mp", None),
        P("dp", "mp", None),
        P("dp"),
        P("dp"),
        P("dp"),
        P(),
        P("mp", None),
        P("dp", "mp", None),
        P("dp", None, "mp"),
    )
    return jax.shard_map(body, mesh=mesh, in_specs=placed, out_specs=P("dp", "mp"), check_vma=False)
```

```python
import functools
import math

import jax
import jax.numpy as jnp
from jax import lax
from jax.experimental import pallas as pl
from jax.experimental.pallas import tpu as pltpu
from jax.sharding import PartitionSpec as P

MIB = 1024 * 1024
TILE = 256
SMALL = pl.CostEstimate(flops=1, bytes_accessed=1, transcendentals=0)
ID_ROWS = 16


def attend_block(lengths, q_ref, k_ref, v_ref, kn_ref, vn_ref, first, acc_ref):
    slots = len(lengths)
    heads, width = q_ref.shape[1:]
    kv_local, cache = k_ref.shape[1], k_ref.shape[2]
    group = heads // kv_local
    inverse = 1.0 / math.sqrt(width)
    lane = lax.broadcasted_iota(jnp.int32, (group, cache), 1)
    parts = []
    for s in range(slots):
        scores = lax.dot_general(
            q_ref[first + s],
            k_ref[first + s].reshape(kv_local * cache, width),
            (((1,), (1,)), ((), ())),
            preferred_element_type=jnp.float32,
        )
        valid = lane < lengths[s]
        for g in range(kv_local):
            part = scores[g * group : (g + 1) * group, g * cache : (g + 1) * cache]
            parts.append(jnp.where(valid, part * inverse, -jnp.inf))
    cached = jnp.concatenate(parts, axis=0)
    block = pl.ds(first, slots)
    q_all = q_ref[block].astype(jnp.float32).reshape(slots * kv_local, group, width)
    kn = kn_ref[block].astype(jnp.float32).reshape(slots * kv_local, 1, width)
    vn = vn_ref[block].astype(jnp.float32).reshape(slots * kv_local, 1, width)
    fresh = (jnp.sum(q_all * kn, axis=-1, keepdims=True) * inverse).reshape(slots * heads, 1)
    top = jnp.maximum(jnp.max(cached, axis=-1, keepdims=True), fresh)
    cached_exp = jnp.exp(cached - top)
    fresh_exp = jnp.exp(fresh - top)
    scale = 1.0 / (jnp.sum(cached_exp, axis=-1, keepdims=True) + fresh_exp)
    weights = (cached_exp * scale).astype(jnp.bfloat16)
    fresh_w = (fresh_exp * scale).astype(jnp.bfloat16).astype(jnp.float32)
    new_part = (fresh_w.reshape(slots * kv_local, group, 1) * vn).reshape(slots * heads, width)
    for s in range(slots):
        values = jnp.concatenate([v_ref[first + s, g] for g in range(kv_local)], axis=1)
        summed = jnp.dot(
            weights[s * heads : (s + 1) * heads], values, preferred_element_type=jnp.float32
        )
        for g in range(kv_local):
            row = s * heads + g * group
            acc_ref[row : row + group, :] = (
                summed[g * group : (g + 1) * group, g * width : (g + 1) * width]
                + new_part[row : row + group]
            )


def fetch(w_ref, buffer_ref, sem_ref, slot, column):
    return pltpu.make_async_copy(
        w_ref.at[:, pl.ds(pl.multiple_of(column, TILE), TILE)],
        buffer_ref.at[slot],
        sem_ref.at[slot],
    )


def project_tiles(a_ref, w_ref, buffer_ref, sem_ref, out_ref, tiles, first_slot, column):
    def tile(j, carry):
        slot = first_slot + j
        fetch(w_ref, buffer_ref, sem_ref, slot, column + j * TILE).wait()
        out_ref[:, pl.ds(pl.multiple_of(j * TILE, TILE), TILE)] = jnp.dot(
            a_ref[: out_ref.shape[0]], buffer_ref[slot], preferred_element_type=jnp.float32
        ).astype(out_ref.dtype)
        return carry

    lax.fori_loop(0, tiles, tile, 0)


def fetch_all(sources, targets, sems):
    copies = [
        pltpu.make_async_copy(source, target, sems.at[i])
        for i, (source, target) in enumerate(zip(sources, targets))
    ]
    for copy in copies:
        copy.start()
    return copies


def look_up(requests, adapters):
    slots, known = requests.shape[1], adapters.shape[1]
    matches = lax.broadcasted_iota(jnp.int32, (known, slots), 0) == requests
    numbers = jnp.broadcast_to(adapters.astype(jnp.float32), (ID_ROWS, known))
    return jnp.dot(
        numbers.astype(jnp.bfloat16),
        matches.astype(jnp.float32).astype(jnp.bfloat16),
        preferred_element_type=jnp.float32,
    )


def attend_kernel(
    block,
    steps,
    lengths_ref,
    me_ref,
    q_hbm,
    k_hbm,
    v_hbm,
    kn_hbm,
    vn_hbm,
    request_hbm,
    adapter_hbm,
    w_ref,
    out_ref,
    first_ref,
    second_ref,
    q_ref,
    k_ref,
    v_ref,
    kn_ref,
    vn_ref,
    request_ref,
    adapter_ref,
    acc_ref,
    buffer_ref,
    new_sem,
    block_sem,
    sem_ref,
):
    rows, heads, width = q_ref.shape
    blocks = rows // block
    out_local = first_ref.shape[1]
    tiles = out_local // TILE

    def block_copies(i):
        part = pl.ds(pl.multiple_of(i * block, block), block)
        return [
            pltpu.make_async_copy(source.at[part], target.at[part], block_sem.at[j, i])
            for j, (source, target) in enumerate(
                ((q_hbm, q_ref), (k_hbm, k_ref), (v_hbm, v_ref))
            )
        ]

    new_copies = fetch_all(
        (kn_hbm, vn_hbm, request_hbm, adapter_hbm),
        (kn_ref, vn_ref, request_ref, adapter_ref),
        new_sem,
    )

    def begin(i, carry):
        for copy in block_copies(i):
            copy.start()
        return carry

    lax.fori_loop(0, blocks, begin, 0)
    columns = [(me_ref[0] ^ step) * out_local for step in steps]
    for i, column in enumerate(columns):
        for j in range(tiles):
            fetch(w_ref, buffer_ref, sem_ref, i * tiles + j, column + j * TILE).start()
    for copy in new_copies:
        copy.wait()
    out_ref[pl.ds(rows, ID_ROWS), :] = jnp.zeros((ID_ROWS, out_ref.shape[1]), out_ref.dtype)
    out_ref[pl.ds(rows, ID_ROWS), :rows] = look_up(request_ref[...], adapter_ref[...]).astype(
        out_ref.dtype
    )

    def one_block(i, carry):
        for copy in block_copies(i):
            copy.wait()
        first = pl.multiple_of(i * block, block)
        attend_block(
            [lengths_ref[first + s] for s in range(block)],
            q_ref,
            k_ref,
            v_ref,
            kn_ref,
            vn_ref,
            first,
            acc_ref,
        )
        for h in range(heads):
            out_ref[pl.ds(first, block), h * width : (h + 1) * width] = acc_ref[
                pl.ds(h, block, stride=heads), :
            ].astype(out_ref.dtype)
        return carry

    lax.fori_loop(0, blocks, one_block, 0)
    for i, (column, piece_ref) in enumerate(zip(columns, (first_ref, second_ref))):
        project_tiles(out_ref, w_ref, buffer_ref, sem_ref, piece_ref, tiles, i * tiles, column)


def attend(arrays, lengths, out_weight, me, steps, out_local):
    queries, key_cache = arrays[:2]
    rows, heads, width = queries.shape
    cache = key_cache.shape[2]
    block = min(16, rows)
    depth = heads * width
    tiles = len(steps) * (out_local // TILE)
    smem = pl.BlockSpec(memory_space=pltpu.SMEM)
    hbm = pl.BlockSpec(memory_space=pltpu.HBM)
    vmem = pl.BlockSpec(memory_space=pltpu.VMEM)
    return pl.pallas_call(
        functools.partial(attend_kernel, block, steps),
        in_specs=[smem, smem] + [hbm] * (len(arrays) + 1),
        out_specs=[vmem, vmem, vmem],
        scratch_shapes=[pltpu.VMEM(a.shape, a.dtype) for a in arrays]
        + [
            pltpu.VMEM((block * heads, width), jnp.float32),
            pltpu.VMEM((tiles, depth, TILE), jnp.bfloat16),
            pltpu.SemaphoreType.DMA((4,)),
            pltpu.SemaphoreType.DMA((3, rows // block)),
            pltpu.SemaphoreType.DMA((tiles,)),
        ],
        out_shape=[
            jax.ShapeDtypeStruct((rows + ID_ROWS, depth), jnp.bfloat16),
        ]
        + [jax.ShapeDtypeStruct((rows, out_local), jnp.bfloat16) for _ in steps],
        compiler_params=pltpu.CompilerParams(vmem_limit_bytes=57 * MIB),
        cost_estimate=SMALL,
        name="attend",
    )(lengths, me.reshape(1), *arrays, out_weight)


def project_kernel(steps, me_ref, a_hbm, w_ref, *refs):
    *out_refs, a_ref, buffer_ref, a_sem, sem_ref = refs
    out_local = out_refs[0].shape[1]
    tiles = out_local // TILE
    copy = pltpu.make_async_copy(a_hbm, a_ref, a_sem.at[0])
    copy.start()
    for i, step in enumerate(steps):
        for j in range(tiles):
            column = (me_ref[0] ^ step) * out_local + j * TILE
            fetch(w_ref, buffer_ref, sem_ref, i * tiles + j, column).start()
    copy.wait()
    for i, (step, out_ref) in enumerate(zip(steps, out_refs)):
        column = (me_ref[0] ^ step) * out_local
        project_tiles(a_ref, w_ref, buffer_ref, sem_ref, out_ref, tiles, i * tiles, column)


def project(attended, out_weight, me, steps, out_local, dtypes):
    rows, depth = attended.shape[0] - ID_ROWS, attended.shape[1]
    slots = len(dtypes) * (out_local // TILE)
    vmem = pl.BlockSpec(memory_space=pltpu.VMEM)
    hbm = pl.BlockSpec(memory_space=pl.ANY)
    return pl.pallas_call(
        functools.partial(project_kernel, steps),
        in_specs=[pl.BlockSpec(memory_space=pltpu.SMEM), hbm, hbm],
        out_specs=[vmem for _ in dtypes],
        scratch_shapes=[
            pltpu.VMEM(attended.shape, attended.dtype),
            pltpu.VMEM((slots, depth, TILE), jnp.bfloat16),
            pltpu.SemaphoreType.DMA((1,)),
            pltpu.SemaphoreType.DMA((slots,)),
        ],
        out_shape=[jax.ShapeDtypeStruct((rows, out_local), dtype) for dtype in dtypes],
        compiler_params=pltpu.CompilerParams(vmem_limit_bytes=40 * MIB),
        cost_estimate=SMALL,
        name="project",
    )(me.reshape(1), attended, out_weight)


def masked(low, owner, adapters, ranks, adapters_here):
    terms = jnp.concatenate([low] * adapters_here, axis=0)
    row = lax.broadcasted_iota(jnp.int32, terms.shape, 0)
    return jnp.where(row // ranks + owner * adapters_here == adapters, terms, 0.0)


def block_parts(blocks):
    arrays, places = [], []
    for i, parts in enumerate(blocks):
        first = 0
        for part in parts:
            arrays.append(part)
            places.append((i, first, part.shape[0]))
            first += part.shape[0]
    return arrays, places


def fetch_blocks(sources, places, column, target, sems, offset):
    columns = pl.ds(column, target.shape[2])
    return [
        pltpu.make_async_copy(
            source.at[:, columns], target.at[i, pl.ds(first, count)], sems.at[offset + j]
        )
        for j, (source, (i, first, count)) in enumerate(zip(sources, places))
    ]


def low_kernel(ranks, places, keys, here_ref, *refs):
    sides, sources = refs[:2], refs[2 : 2 + len(places)]
    out_ref, adapters_ref, side_ref, block_ref, sems = refs[2 + len(places) :]
    copies = fetch_all(sides, [side_ref.at[i] for i in range(2)], sems)
    parts = fetch_blocks(sources, places, 0, block_ref, sems, 2)
    for copy in parts:
        copy.start()
    blocks, pair = block_ref.shape[:2]
    rows = side_ref.shape[1] - ID_ROWS
    sides_t, adapters = [], []
    for i, copy in enumerate(copies):
        copy.wait()
        sides_t.append(side_ref[i, :rows].astype(jnp.float32).T.astype(jnp.bfloat16))
        ids = side_ref[i, rows:, :rows].astype(jnp.float32)
        adapters.append(ids[:8].astype(jnp.int32))
    a_t = jnp.concatenate(sides_t, axis=1)
    adapters_ref[...] = jnp.concatenate(adapters, axis=1)
    adapters = adapters_ref[:1, :]
    row = lax.broadcasted_iota(jnp.int32, (pair, a_t.shape[1]), 0)
    total = jnp.zeros(row.shape, jnp.float32)
    for i in range(blocks):
        for copy, place in zip(parts, places):
            if place[0] == i:
                copy.wait()
        part = jnp.dot(block_ref[i], a_t, preferred_element_type=jnp.float32)
        first = (here_ref[0] ^ keys[i]) * (pair // ranks)
        total += jnp.where(row // ranks + first == adapters, part, 0.0)
    low = total[:ranks]
    for a in range(1, pair // ranks):
        low += total[a * ranks : (a + 1) * ranks]
    out_ref[...] = low.astype(out_ref.dtype)


def low_rank(sides, blocks, depth, here, keys, rank):
    rows = sides[0].shape[0] - ID_ROWS
    arrays, places = block_parts(blocks)
    pair = sum(part.shape[0] for part in blocks[0])
    vmem = pl.BlockSpec(memory_space=pltpu.VMEM)
    return pl.pallas_call(
        functools.partial(low_kernel, rank, places, keys),
        in_specs=[pl.BlockSpec(memory_space=pltpu.SMEM)]
        + [pl.BlockSpec(memory_space=pl.ANY)] * (2 + len(arrays)),
        out_specs=[vmem, vmem],
        out_shape=[
            jax.ShapeDtypeStruct((rank, 2 * rows), jnp.bfloat16),
            jax.ShapeDtypeStruct((8, 2 * rows), jnp.int32),
        ],
        scratch_shapes=[
            pltpu.VMEM((2, *sides[0].shape), jnp.bfloat16),
            pltpu.VMEM((len(blocks), pair, depth), jnp.bfloat16),
            pltpu.SemaphoreType.DMA((2 + len(arrays),)),
        ],
        compiler_params=pltpu.CompilerParams(vmem_limit_bytes=16 * MIB),
        cost_estimate=SMALL,
        name="low_rank",
    )(here.reshape(1), *sides, *arrays)


def delta_kernel(ranks, places, column, keys, here_ref, adapters_ref, low_ref, *refs):
    sources = refs[: len(places)]
    mine_ref, other_ref, block_ref, sems = refs[len(places) :]
    parts = fetch_blocks(sources, places, column, block_ref, sems, 0)
    for copy in parts:
        copy.start()
    blocks, pair, width = block_ref.shape
    low = low_ref[...].astype(jnp.float32)
    sides = []
    for i in range(blocks):
        mine = masked(low, here_ref[0] ^ keys[i], adapters_ref[:1, :], ranks, pair // ranks)
        sides.append(mine.T.astype(jnp.bfloat16))
    for copy in parts:
        copy.wait()
    delta = jnp.dot(
        jnp.concatenate(sides, axis=1),
        block_ref[...].reshape(blocks * pair, width),
        preferred_element_type=jnp.float32,
    )
    delta = (0.5 * delta).astype(jnp.bfloat16)
    rows = mine_ref.shape[0]
    mine_ref[...] = delta[:rows]
    other_ref[...] = delta[rows:]


def correct(low, adapters, blocks, column, out_local, here, keys, rank):
    slots = adapters.shape[1]
    arrays, places = block_parts(blocks)
    pair = sum(part.shape[0] for part in blocks[0])
    vmem = pl.BlockSpec(memory_space=pltpu.VMEM)
    out = jax.ShapeDtypeStruct((slots // 2, out_local), jnp.bfloat16)
    return pl.pallas_call(
        functools.partial(delta_kernel, rank, places, column, keys),
        in_specs=[pl.BlockSpec(memory_space=pltpu.SMEM), vmem, vmem]
        + [pl.BlockSpec(memory_space=pl.ANY)] * len(arrays),
        out_specs=[vmem, vmem],
        out_shape=[out, out],
        scratch_shapes=[
            pltpu.VMEM((len(blocks), pair, out_local), jnp.bfloat16),
            pltpu.SemaphoreType.DMA((len(arrays),)),
        ],
        compiler_params=pltpu.CompilerParams(vmem_limit_bytes=16 * MIB),
        cost_estimate=SMALL,
        name="correct",
    )(here.reshape(1), adapters, low, *arrays)


def finish_kernel(occupied_ref, own_ref, *refs):
    *part_refs, out_ref = refs
    rows = out_ref.shape[0]
    live = jnp.broadcast_to(occupied_ref[...].astype(jnp.float32), (128, rows)).T
    for j in range(0, out_ref.shape[1], 128):
        columns = slice(j, j + 128)
        total = own_ref[:, columns].astype(jnp.float32)
        for ref in part_refs:
            total += ref[:, columns].astype(jnp.float32)
        out_ref[:, columns] = (live * total).astype(out_ref.dtype)


def finish(own, parts, occupied):
    rows, out_local = own.shape
    vmem = pl.BlockSpec(memory_space=pltpu.VMEM)
    return pl.pallas_call(
        finish_kernel,
        in_specs=[vmem] * (2 + len(parts)),
        out_specs=vmem,
        out_shape=jax.ShapeDtypeStruct((rows, out_local), jnp.bfloat16),
        compiler_params=pltpu.CompilerParams(vmem_limit_bytes=16 * MIB),
        cost_estimate=SMALL,
        name="finish",
    )(occupied.reshape(1, rows), own, *parts)


def add_kernel(a_ref, b_ref, out_ref):
    total = a_ref[...].astype(jnp.float32) + b_ref[...].astype(jnp.float32)
    out_ref[...] = total.astype(out_ref.dtype)


def add(a, b):
    vmem = pl.BlockSpec(memory_space=pltpu.VMEM)
    return pl.pallas_call(
        add_kernel,
        in_specs=[vmem, vmem],
        out_specs=vmem,
        out_shape=jax.ShapeDtypeStruct(a.shape, a.dtype),
        compiler_params=pltpu.CompilerParams(vmem_limit_bytes=16 * MIB),
        cost_estimate=SMALL,
        name="add",
    )(a, b)


def exchange(value, axis, step):
    count = lax.axis_size(axis)
    return lax.ppermute(value, axis, [(i, i ^ step) for i in range(count)])


def neighbours():
    return [1 << i for i in range(1, lax.axis_size("dp").bit_length() - 1)]


def near_blocks(own):
    return {0: [own], **{bit: [exchange(own, "dp", bit)] for bit in neighbours()[:2]}}


def farther_blocks(blocks):
    for bit in neighbours()[2:]:
        for key in list(blocks):
            blocks[key | bit] = [exchange(part, "dp", bit) for part in blocks[key]]
    return blocks


def forwarded_blocks(blocks):
    a, b = neighbours()[:2]
    half = blocks[0][0].shape[0] // 2
    diagonal = [
        exchange(blocks[a][0][:half], "dp", b),
        exchange(blocks[b][0][half:], "dp", a),
    ]
    return farther_blocks({**blocks, a | b: diagonal})


def direct_blocks(own):
    a, b = neighbours()[:2]
    return farther_blocks({**near_blocks(own), a | b: [exchange(own, "dp", a | b)]})


def together(*values):
    return lax.optimization_barrier(values)


def body(
    queries,
    key_cache,
    value_cache,
    key_new,
    value_new,
    lengths,
    occupied,
    slot_request,
    request_adapter,
    out_weight,
    shrink_weight,
    expand_weight,
):
    adapters_here, depth, rank = shrink_weight.shape
    out_local = expand_weight.shape[2]
    shares = lax.axis_size("mp")
    me = lax.axis_index("mp")
    here = lax.axis_index("dp")
    pair = adapters_here * rank

    shrink = near_blocks(jnp.swapaxes(shrink_weight, 1, 2).reshape(pair, depth))
    expand = expand_weight.reshape(pair, out_local)

    halved = shares == 4
    early = (3, 1) if halved else (shares - 1, shares - 2)
    late = (2, 0) if halved else tuple(range(shares - 3, -1, -1))
    attended, *pieces = attend(
        (
            queries,
            key_cache,
            value_cache,
            key_new,
            value_new,
            slot_request.reshape(1, -1),
            request_adapter.reshape(1, -1),
        ),
        lengths,
        out_weight,
        me,
        early,
        out_local,
    )
    received = [
        exchange(piece, "mp", 1 if halved else step) for piece, step in zip(pieces, early)
    ]
    shrink, attended = together(shrink, attended)
    shrink = forwarded_blocks(shrink)
    beside = exchange(attended, "dp", 1)
    *pieces, own = project(
        attended,
        out_weight,
        me,
        late,
        out_local,
        [jnp.bfloat16] * len(late),
    )
    pieces, received[0], attended, shrink, expand = together(
        pieces, received[0], attended, shrink, expand
    )
    expand = direct_blocks(expand)
    if halved:
        pieces = [add(pieces[0], received.pop(0))]
    last = [exchange(part, "mp", step) for part, step in zip(pieces, late)]

    keys = tuple(shrink)
    low, adapters = low_rank(
        [attended, beside], list(shrink.values()), depth, here, keys, rank
    )
    low, received = together(low, received)
    step = 1
    while step < shares:
        arrived = exchange(low, "mp", step)
        low = (low.astype(jnp.float32) + arrived.astype(jnp.float32)).astype(jnp.bfloat16)
        if step == 1:
            low, last = together(low, last)
        step *= 2
    blocks = [expand[key] for key in keys]
    correction, other = correct(low, adapters, blocks, 0, out_local, here, keys, rank)
    parts = [*received, *last, correction, exchange(other, "dp", 1)]
    return finish(own, parts, occupied)


def solution(mesh):
    placed = (
        P("dp", "mp", None),
        P("dp", "mp", None, None),
        P("dp", "mp", None, None),
        P("dp", "mp", None),
        P("dp", "mp", None),
        P("dp"),
        P("dp"),
        P("dp"),
        P(),
        P("mp", None),
        P("dp", "mp", None),
        P("dp", None, "mp"),
    )
    return jax.shard_map(body, mesh=mesh, in_specs=placed, out_specs=P("dp", "mp"), check_vma=False)
```

```python
import functools
import math

import jax
import jax.numpy as jnp
from jax import lax
from jax.experimental import pallas as pl
from jax.experimental.pallas import tpu as pltpu
from jax.sharding import PartitionSpec as P

MIB = 1024 * 1024
TILE = 256
SMALL = pl.CostEstimate(flops=1, bytes_accessed=1, transcendentals=0)
ID_ROWS = 16


def attend_block(lengths, q_ref, k_ref, v_ref, kn_ref, vn_ref, first, acc_ref):
    slots = len(lengths)
    heads, width = q_ref.shape[1:]
    kv_local, cache = k_ref.shape[1], k_ref.shape[2]
    group = heads // kv_local
    inverse = 1.0 / math.sqrt(width)
    lane = lax.broadcasted_iota(jnp.int32, (group, cache), 1)
    parts = []
    for s in range(slots):
        scores = lax.dot_general(
            q_ref[first + s],
            k_ref[first + s].reshape(kv_local * cache, width),
            (((1,), (1,)), ((), ())),
            preferred_element_type=jnp.float32,
        )
        valid = lane < lengths[s]
        for g in range(kv_local):
            part = scores[g * group : (g + 1) * group, g * cache : (g + 1) * cache]
            parts.append(jnp.where(valid, part * inverse, -jnp.inf))
    cached = jnp.concatenate(parts, axis=0)
    block = pl.ds(first, slots)
    q_all = q_ref[block].astype(jnp.float32).reshape(slots * kv_local, group, width)
    kn = kn_ref[block].astype(jnp.float32).reshape(slots * kv_local, 1, width)
    vn = vn_ref[block].astype(jnp.float32).reshape(slots * kv_local, 1, width)
    fresh = (jnp.sum(q_all * kn, axis=-1, keepdims=True) * inverse).reshape(slots * heads, 1)
    top = jnp.maximum(jnp.max(cached, axis=-1, keepdims=True), fresh)
    cached_exp = jnp.exp(cached - top)
    fresh_exp = jnp.exp(fresh - top)
    scale = 1.0 / (jnp.sum(cached_exp, axis=-1, keepdims=True) + fresh_exp)
    weights = (cached_exp * scale).astype(jnp.bfloat16)
    fresh_w = (fresh_exp * scale).astype(jnp.bfloat16).astype(jnp.float32)
    new_part = (fresh_w.reshape(slots * kv_local, group, 1) * vn).reshape(slots * heads, width)
    for s in range(slots):
        values = jnp.concatenate([v_ref[first + s, g] for g in range(kv_local)], axis=1)
        summed = jnp.dot(
            weights[s * heads : (s + 1) * heads], values, preferred_element_type=jnp.float32
        )
        for g in range(kv_local):
            row = s * heads + g * group
            acc_ref[row : row + group, :] = (
                summed[g * group : (g + 1) * group, g * width : (g + 1) * width]
                + new_part[row : row + group]
            )


def fetch(w_ref, buffer_ref, sem_ref, slot, column):
    return pltpu.make_async_copy(
        w_ref.at[:, pl.ds(pl.multiple_of(column, TILE), TILE)],
        buffer_ref.at[slot],
        sem_ref.at[slot],
    )


def project_tiles(a_ref, w_ref, buffer_ref, sem_ref, out_ref, tiles, first_slot, column):
    def tile(j, carry):
        slot = first_slot + j
        fetch(w_ref, buffer_ref, sem_ref, slot, column + j * TILE).wait()
        out_ref[:, pl.ds(pl.multiple_of(j * TILE, TILE), TILE)] = jnp.dot(
            a_ref[: out_ref.shape[0]], buffer_ref[slot], preferred_element_type=jnp.float32
        ).astype(out_ref.dtype)
        return carry

    lax.fori_loop(0, tiles, tile, 0)


def fetch_all(sources, targets, sems):
    copies = [
        pltpu.make_async_copy(source, target, sems.at[i])
        for i, (source, target) in enumerate(zip(sources, targets))
    ]
    for copy in copies:
        copy.start()
    return copies


def look_up(requests, adapters):
    slots, known = requests.shape[1], adapters.shape[1]
    matches = lax.broadcasted_iota(jnp.int32, (known, slots), 0) == requests
    numbers = jnp.broadcast_to(adapters.astype(jnp.float32), (ID_ROWS, known))
    return jnp.dot(
        numbers.astype(jnp.bfloat16),
        matches.astype(jnp.float32).astype(jnp.bfloat16),
        preferred_element_type=jnp.float32,
    )


def attend_kernel(
    block,
    steps,
    lengths_ref,
    me_ref,
    q_hbm,
    k_hbm,
    v_hbm,
    kn_hbm,
    vn_hbm,
    request_hbm,
    adapter_hbm,
    w_ref,
    out_ref,
    first_ref,
    second_ref,
    q_ref,
    k_ref,
    v_ref,
    kn_ref,
    vn_ref,
    request_ref,
    adapter_ref,
    acc_ref,
    buffer_ref,
    new_sem,
    block_sem,
    sem_ref,
):
    rows, heads, width = q_ref.shape
    blocks = rows // block
    out_local = first_ref.shape[1]
    tiles = out_local // TILE

    def block_copies(i):
        part = pl.ds(pl.multiple_of(i * block, block), block)
        return [
            pltpu.make_async_copy(source.at[part], target.at[part], block_sem.at[j, i])
            for j, (source, target) in enumerate(
                ((q_hbm, q_ref), (k_hbm, k_ref), (v_hbm, v_ref))
            )
        ]

    new_copies = fetch_all(
        (kn_hbm, vn_hbm, request_hbm, adapter_hbm),
        (kn_ref, vn_ref, request_ref, adapter_ref),
        new_sem,
    )

    def begin(i, carry):
        for copy in block_copies(i):
            copy.start()
        return carry

    lax.fori_loop(0, blocks, begin, 0)
    columns = [(me_ref[0] ^ step) * out_local for step in steps]
    for i, column in enumerate(columns):
        for j in range(tiles):
            fetch(w_ref, buffer_ref, sem_ref, i * tiles + j, column + j * TILE).start()
    for copy in new_copies:
        copy.wait()
    out_ref[pl.ds(rows, ID_ROWS), :] = jnp.zeros((ID_ROWS, out_ref.shape[1]), out_ref.dtype)
    out_ref[pl.ds(rows, ID_ROWS), :rows] = look_up(request_ref[...], adapter_ref[...]).astype(
        out_ref.dtype
    )

    def one_block(i, carry):
        for copy in block_copies(i):
            copy.wait()
        first = pl.multiple_of(i * block, block)
        attend_block(
            [lengths_ref[first + s] for s in range(block)],
            q_ref,
            k_ref,
            v_ref,
            kn_ref,
            vn_ref,
            first,
            acc_ref,
        )
        for h in range(heads):
            out_ref[pl.ds(first, block), h * width : (h + 1) * width] = acc_ref[
                pl.ds(h, block, stride=heads), :
            ].astype(out_ref.dtype)
        return carry

    lax.fori_loop(0, blocks, one_block, 0)
    for i, (column, piece_ref) in enumerate(zip(columns, (first_ref, second_ref))):
        project_tiles(out_ref, w_ref, buffer_ref, sem_ref, piece_ref, tiles, i * tiles, column)


def attend(arrays, lengths, out_weight, me, steps, out_local):
    queries, key_cache = arrays[:2]
    rows, heads, width = queries.shape
    cache = key_cache.shape[2]
    block = min(16, rows)
    depth = heads * width
    tiles = len(steps) * (out_local // TILE)
    smem = pl.BlockSpec(memory_space=pltpu.SMEM)
    hbm = pl.BlockSpec(memory_space=pltpu.HBM)
    vmem = pl.BlockSpec(memory_space=pltpu.VMEM)
    return pl.pallas_call(
        functools.partial(attend_kernel, block, steps),
        in_specs=[smem, smem] + [hbm] * (len(arrays) + 1),
        out_specs=[vmem, vmem, vmem],
        scratch_shapes=[pltpu.VMEM(a.shape, a.dtype) for a in arrays]
        + [
            pltpu.VMEM((block * heads, width), jnp.float32),
            pltpu.VMEM((tiles, depth, TILE), jnp.bfloat16),
            pltpu.SemaphoreType.DMA((4,)),
            pltpu.SemaphoreType.DMA((3, rows // block)),
            pltpu.SemaphoreType.DMA((tiles,)),
        ],
        out_shape=[
            jax.ShapeDtypeStruct((rows + ID_ROWS, depth), jnp.bfloat16),
        ]
        + [jax.ShapeDtypeStruct((rows, out_local), jnp.bfloat16) for _ in steps],
        compiler_params=pltpu.CompilerParams(vmem_limit_bytes=57 * MIB),
        cost_estimate=SMALL,
        name="attend",
    )(lengths, me.reshape(1), *arrays, out_weight)


def project_kernel(steps, me_ref, a_hbm, w_ref, *refs):
    *out_refs, a_ref, buffer_ref, a_sem, sem_ref = refs
    out_local = out_refs[0].shape[1]
    tiles = out_local // TILE
    copy = pltpu.make_async_copy(a_hbm, a_ref, a_sem.at[0])
    copy.start()
    for i, step in enumerate(steps):
        for j in range(tiles):
            column = (me_ref[0] ^ step) * out_local + j * TILE
            fetch(w_ref, buffer_ref, sem_ref, i * tiles + j, column).start()
    copy.wait()
    for i, (step, out_ref) in enumerate(zip(steps, out_refs)):
        column = (me_ref[0] ^ step) * out_local
        project_tiles(a_ref, w_ref, buffer_ref, sem_ref, out_ref, tiles, i * tiles, column)


def project(attended, out_weight, me, steps, out_local, dtypes):
    rows, depth = attended.shape[0] - ID_ROWS, attended.shape[1]
    slots = len(dtypes) * (out_local // TILE)
    vmem = pl.BlockSpec(memory_space=pltpu.VMEM)
    hbm = pl.BlockSpec(memory_space=pl.ANY)
    return pl.pallas_call(
        functools.partial(project_kernel, steps),
        in_specs=[pl.BlockSpec(memory_space=pltpu.SMEM), hbm, hbm],
        out_specs=[vmem for _ in dtypes],
        scratch_shapes=[
            pltpu.VMEM(attended.shape, attended.dtype),
            pltpu.VMEM((slots, depth, TILE), jnp.bfloat16),
            pltpu.SemaphoreType.DMA((1,)),
            pltpu.SemaphoreType.DMA((slots,)),
        ],
        out_shape=[jax.ShapeDtypeStruct((rows, out_local), dtype) for dtype in dtypes],
        compiler_params=pltpu.CompilerParams(vmem_limit_bytes=40 * MIB),
        cost_estimate=SMALL,
        name="project",
    )(me.reshape(1), attended, out_weight)


def masked(low, owner, adapters, ranks, adapters_here):
    terms = jnp.concatenate([low] * adapters_here, axis=0)
    row = lax.broadcasted_iota(jnp.int32, terms.shape, 0)
    return jnp.where(row // ranks + owner * adapters_here == adapters, terms, 0.0)


def block_parts(blocks):
    arrays, places = [], []
    for i, parts in enumerate(blocks):
        first = 0
        for part in parts:
            arrays.append(part)
            places.append((i, first, part.shape[0]))
            first += part.shape[0]
    return arrays, places


def fetch_blocks(sources, places, column, target, sems, offset):
    columns = pl.ds(column, target.shape[2])
    return [
        pltpu.make_async_copy(
            source.at[:, columns], target.at[i, pl.ds(first, count)], sems.at[offset + j]
        )
        for j, (source, (i, first, count)) in enumerate(zip(sources, places))
    ]


def low_kernel(ranks, places, keys, here_ref, *refs):
    sides, sources = refs[:2], refs[2 : 2 + len(places)]
    out_ref, adapters_ref, side_ref, block_ref, sems = refs[2 + len(places) :]
    copies = fetch_all(sides, [side_ref.at[i] for i in range(2)], sems)
    parts = fetch_blocks(sources, places, 0, block_ref, sems, 2)
    for copy in parts:
        copy.start()
    blocks, pair = block_ref.shape[:2]
    rows = side_ref.shape[1] - ID_ROWS
    sides_t, adapters = [], []
    for i, copy in enumerate(copies):
        copy.wait()
        sides_t.append(side_ref[i, :rows].astype(jnp.float32).T.astype(jnp.bfloat16))
        ids = side_ref[i, rows:, :rows].astype(jnp.float32)
        adapters.append(ids[:8].astype(jnp.int32))
    a_t = jnp.concatenate(sides_t, axis=1)
    adapters_ref[...] = jnp.concatenate(adapters, axis=1)
    adapters = adapters_ref[:1, :]
    row = lax.broadcasted_iota(jnp.int32, (pair, a_t.shape[1]), 0)
    total = jnp.zeros(row.shape, jnp.float32)
    for i in range(blocks):
        for copy, place in zip(parts, places):
            if place[0] == i:
                copy.wait()
        part = jnp.dot(block_ref[i], a_t, preferred_element_type=jnp.float32)
        first = (here_ref[0] ^ keys[i]) * (pair // ranks)
        total += jnp.where(row // ranks + first == adapters, part, 0.0)
    low = total[:ranks]
    for a in range(1, pair // ranks):
        low += total[a * ranks : (a + 1) * ranks]
    out_ref[...] = low.astype(out_ref.dtype)


def low_rank(sides, blocks, depth, here, keys, rank):
    rows = sides[0].shape[0] - ID_ROWS
    arrays, places = block_parts(blocks)
    pair = sum(part.shape[0] for part in blocks[0])
    vmem = pl.BlockSpec(memory_space=pltpu.VMEM)
    return pl.pallas_call(
        functools.partial(low_kernel, rank, places, keys),
        in_specs=[pl.BlockSpec(memory_space=pltpu.SMEM)]
        + [pl.BlockSpec(memory_space=pl.ANY)] * (2 + len(arrays)),
        out_specs=[vmem, vmem],
        out_shape=[
            jax.ShapeDtypeStruct((rank, 2 * rows), jnp.bfloat16),
            jax.ShapeDtypeStruct((8, 2 * rows), jnp.int32),
        ],
        scratch_shapes=[
            pltpu.VMEM((2, *sides[0].shape), jnp.bfloat16),
            pltpu.VMEM((len(blocks), pair, depth), jnp.bfloat16),
            pltpu.SemaphoreType.DMA((2 + len(arrays),)),
        ],
        compiler_params=pltpu.CompilerParams(vmem_limit_bytes=16 * MIB),
        cost_estimate=SMALL,
        name="low_rank",
    )(here.reshape(1), *sides, *arrays)


def delta_kernel(ranks, places, column, keys, here_ref, adapters_ref, low_ref, *refs):
    sources = refs[: len(places)]
    mine_ref, other_ref, block_ref, sems = refs[len(places) :]
    parts = fetch_blocks(sources, places, column, block_ref, sems, 0)
    for copy in parts:
        copy.start()
    blocks, pair, width = block_ref.shape
    low = low_ref[...].astype(jnp.float32)
    sides = []
    for i in range(blocks):
        mine = masked(low, here_ref[0] ^ keys[i], adapters_ref[:1, :], ranks, pair // ranks)
        sides.append(mine.T.astype(jnp.bfloat16))
    for copy in parts:
        copy.wait()
    delta = jnp.dot(
        jnp.concatenate(sides, axis=1),
        block_ref[...].reshape(blocks * pair, width),
        preferred_element_type=jnp.float32,
    )
    delta = (0.5 * delta).astype(jnp.bfloat16)
    rows = mine_ref.shape[0]
    mine_ref[...] = delta[:rows]
    other_ref[...] = delta[rows:]


def correct(low, adapters, blocks, column, out_local, here, keys, rank):
    slots = adapters.shape[1]
    arrays, places = block_parts(blocks)
    pair = sum(part.shape[0] for part in blocks[0])
    vmem = pl.BlockSpec(memory_space=pltpu.VMEM)
    out = jax.ShapeDtypeStruct((slots // 2, out_local), jnp.bfloat16)
    return pl.pallas_call(
        functools.partial(delta_kernel, rank, places, column, keys),
        in_specs=[pl.BlockSpec(memory_space=pltpu.SMEM), vmem, vmem]
        + [pl.BlockSpec(memory_space=pl.ANY)] * len(arrays),
        out_specs=[vmem, vmem],
        out_shape=[out, out],
        scratch_shapes=[
            pltpu.VMEM((len(blocks), pair, out_local), jnp.bfloat16),
            pltpu.SemaphoreType.DMA((len(arrays),)),
        ],
        compiler_params=pltpu.CompilerParams(vmem_limit_bytes=16 * MIB),
        cost_estimate=SMALL,
        name="correct",
    )(here.reshape(1), adapters, low, *arrays)


def finish_kernel(occupied_ref, own_ref, *refs):
    *part_refs, out_ref = refs
    rows = out_ref.shape[0]
    live = jnp.broadcast_to(occupied_ref[...].astype(jnp.float32), (128, rows)).T
    for j in range(0, out_ref.shape[1], 128):
        columns = slice(j, j + 128)
        total = own_ref[:, columns].astype(jnp.float32)
        for ref in part_refs:
            total += ref[:, columns].astype(jnp.float32)
        out_ref[:, columns] = (live * total).astype(out_ref.dtype)


def finish(own, parts, occupied):
    rows, out_local = own.shape
    vmem = pl.BlockSpec(memory_space=pltpu.VMEM)
    return pl.pallas_call(
        finish_kernel,
        in_specs=[vmem] * (2 + len(parts)),
        out_specs=vmem,
        out_shape=jax.ShapeDtypeStruct((rows, out_local), jnp.bfloat16),
        compiler_params=pltpu.CompilerParams(vmem_limit_bytes=16 * MIB),
        cost_estimate=SMALL,
        name="finish",
    )(occupied.reshape(1, rows), own, *parts)


def exchange(value, axis, step):
    count = lax.axis_size(axis)
    return lax.ppermute(value, axis, [(i, i ^ step) for i in range(count)])


def neighbours():
    return [1 << i for i in range(1, lax.axis_size("dp").bit_length() - 1)]


def near_blocks(own):
    return {0: [own], **{bit: [exchange(own, "dp", bit)] for bit in neighbours()[:2]}}


def farther_blocks(blocks):
    for bit in neighbours()[2:]:
        for key in list(blocks):
            blocks[key | bit] = [exchange(part, "dp", bit) for part in blocks[key]]
    return blocks


def forwarded_blocks(blocks):
    a, b = neighbours()[:2]
    half = blocks[0][0].shape[0] // 2
    diagonal = [
        exchange(blocks[a][0][:half], "dp", b),
        exchange(blocks[b][0][half:], "dp", a),
    ]
    return farther_blocks({**blocks, a | b: diagonal})


def direct_blocks(own):
    a, b = neighbours()[:2]
    return farther_blocks({**near_blocks(own), a | b: [exchange(own, "dp", a | b)]})


def together(*values):
    return lax.optimization_barrier(values)


def body(
    queries,
    key_cache,
    value_cache,
    key_new,
    value_new,
    lengths,
    occupied,
    slot_request,
    request_adapter,
    out_weight,
    shrink_weight,
    expand_weight,
):
    adapters_here, depth, rank = shrink_weight.shape
    out_local = expand_weight.shape[2]
    shares = lax.axis_size("mp")
    me = lax.axis_index("mp")
    here = lax.axis_index("dp")
    pair = adapters_here * rank

    shrink = near_blocks(jnp.swapaxes(shrink_weight, 1, 2).reshape(pair, depth))
    expand = expand_weight.reshape(pair, out_local)

    halved = shares == 4
    early = (3, 1) if halved else (shares - 1, shares - 2)
    late = (2, 0) if halved else tuple(range(shares - 3, -1, -1))
    attended, *pieces = attend(
        (
            queries,
            key_cache,
            value_cache,
            key_new,
            value_new,
            slot_request.reshape(1, -1),
            request_adapter.reshape(1, -1),
        ),
        lengths,
        out_weight,
        me,
        early,
        out_local,
    )
    received = [
        exchange(piece, "mp", 1 if halved else step) for piece, step in zip(pieces, early)
    ]
    shrink, attended = together(shrink, attended)
    shrink = forwarded_blocks(shrink)
    beside = exchange(attended, "dp", 1)
    *pieces, own = project(
        attended,
        out_weight,
        me,
        late,
        out_local,
        [jnp.bfloat16] * len(late),
    )
    pieces, received[0], attended, shrink, expand = together(
        pieces, received[0], attended, shrink, expand
    )
    expand = direct_blocks(expand)
    if halved:
        passed = received.pop(0).astype(jnp.float32)
        pieces = [(pieces[0].astype(jnp.float32) + passed).astype(jnp.bfloat16)]
    last = [exchange(part, "mp", step) for part, step in zip(pieces, late)]

    keys = tuple(shrink)
    low, adapters = low_rank(
        [attended, beside], list(shrink.values()), depth, here, keys, rank
    )
    low, received = together(low, received)
    step = shares // 2
    while step:
        arrived = exchange(low, "mp", step)
        low = (low.astype(jnp.float32) + arrived.astype(jnp.float32)).astype(jnp.bfloat16)
        step //= 2
    blocks = [expand[key] for key in keys]
    correction, other = correct(low, adapters, blocks, 0, out_local, here, keys, rank)
    other, last = together(other, last)
    parts = [*received, *last, correction, exchange(other, "dp", 1)]
    return finish(own, parts, occupied)


def solution(mesh):
    placed = (
        P("dp", "mp", None),
        P("dp", "mp", None, None),
        P("dp", "mp", None, None),
        P("dp", "mp", None),
        P("dp", "mp", None),
        P("dp"),
        P("dp"),
        P("dp"),
        P(),
        P("mp", None),
        P("dp", "mp", None),
        P("dp", None, "mp"),
    )
    return jax.shard_map(body, mesh=mesh, in_specs=placed, out_specs=P("dp", "mp"), check_vma=False)
```
